256 devices in a mesh: branch: 2 (over core), row: 8 (over x, z_lo), col: 16 (over z_hi, y).
Axes of the slice: x: 4, y: 4, z: 8 (z_hi: 4, z_lo: 2; z = z_hi * 2 + z_lo), core: 2. Of those that a mesh axis runs over, the one named last changes fastest.
Arguments:
- tokens: bfloat16 [2, 128, 512, 1152], P('branch', 'row', 'col'), may hold values from -26 to 26
- modulation: float32 [3, 1152], replicated, may hold values from -4 to 4
- wqkv: bfloat16 [1152, 3456], replicated, may hold values from -1 to 1
- w_out: bfloat16 [1152, 1152], replicated, may hold values from -0.1875 to 0.1875
- blend: float32 [128, 512], P('row', 'col'), may hold values from 0.1 to 0.6
- reach: int32 [4, 8, 16], P(None, 'row', 'col'), may hold values from 1 to 4, as said below
Outputs:
- guided: bfloat16 [128, 512, 1152], P(('row', 'branch'), 'col')
The draws below stay inside these ranges and needn't reach their ends.
Inputs may be any that keep to these rules, and one draw needn't show every extreme that they name: Each reach is at most 4, and some tile's reach on some side is exactly 4.
All inputs are finite; a program needn't handle non-finite values.
Results may differ from the reference program's by a relative error of at most 0.0067.
Values may be sent and summed in bfloat16 or wider, within the bound.
No kernel may reach another device: no remote copies, remote signals or barrier semaphores. Data moves between devices by JAX's collectives and lax.ppermute only.
A program may use at most 192 MiB of HBM per device.

```python
import math
import jax
import jax.numpy as jnp
from jax import lax

D = 1152
HEADS = 16
HD = 72
TR = 16
TC = 32
HALO = 4
NH = 128
NW = 512
N_ROW = 8
N_COL = 16


def draw_tokens(key, part):
    key = jax.random.fold_in(key, 11)
    shape = (2, NH, NW, D)
    return jnp.clip(jax.random.normal(key, shape, jnp.float32), -6.0, 6.0).astype(jnp.bfloat16)


def draw_wqkv(key, part):
    key = jax.random.fold_in(key, 12)
    return (jnp.clip(jax.random.normal(key, (D, 3 * D), jnp.float32), -6.0, 6.0) / math.sqrt(D)).astype(jnp.bfloat16)


def draw_reach(key, part):
    key = jax.random.fold_in(key, 13)
    row_tiles = NH // TR
    col_tiles = NW // TC
    entries = jax.random.randint(key, (4 * row_tiles * col_tiles,), 1, HALO + 1, jnp.int32)
    chosen_slot = jax.random.randint(jax.random.fold_in(key, 1), (), 0, 4 * row_tiles * col_tiles, jnp.int32)
    entries = entries.at[chosen_slot].set(HALO)
    return entries.reshape(4, row_tiles, col_tiles)


def levels(rng, dims, cuts, low, high):
    gain = 1.0
    for axis_at, shards_of in cuts:
        steps = jax.random.uniform(jax.random.fold_in(jax.random.fold_in(rng, 6), axis_at), (shards_of,), jnp.float32, low / len(cuts), high / len(cuts))
        gain = gain * jnp.repeat(jnp.exp(steps), dims[axis_at] // shards_of).reshape((-1,) + (1,) * (len(dims) - 1 - axis_at))
    return gain


def gaussian(stream_key, dims, deviation, limit, kind=jnp.bfloat16):
    array = jax.random.normal(stream_key, dims, jnp.float32) * deviation
    return jnp.minimum(jnp.maximum(array, -limit), limit).astype(kind)


def setup_inputs(seed: int = 0) -> dict:
    streams_of = jax.random.split(jax.random.key(seed), 7)
    tokens = draw_tokens(jax.random.fold_in(streams_of[6], 71), 0)
    modulation = gaussian(streams_of[1], (3, D), 1.0, 4.0, jnp.float32)
    wqkv = draw_wqkv(jax.random.fold_in(streams_of[6], 71), 0)
    w_out = gaussian(streams_of[3], (D, D), D ** -0.5, 0.1875)
    blend = jnp.clip(0.1 + 0.5 * jax.random.uniform(streams_of[4], (NH, NW), jnp.float32) ** levels(streams_of[4], (NH, NW), ((0, 8), (1, 16)), -0.2, 0.2), 0.1, 0.6)
    reach = draw_reach(jax.random.fold_in(streams_of[6], 71), 0)
    return {"tokens": tokens, "modulation": modulation, "wqkv": wqkv, "w_out": w_out, "blend": blend, "reach": reach}


GUIDANCE = 4.5

def layer_norm(values, modulation):
    widened = values.astype(jnp.float32)
    centered = widened - lax.optimization_barrier(jnp.mean(widened, axis=-1, keepdims=True))
    variance = lax.optimization_barrier(jnp.mean(centered * centered, axis=-1, keepdims=True))
    scaled = centered * lax.rsqrt(variance + 1e-06)
    return (scaled * (1.0 + modulation[1]) + modulation[0]).astype(jnp.bfloat16)

def attend(queries, keys, values, allowed):
    query_count = queries.shape[0]
    key_count = keys.shape[0]
    query_heads = queries.astype(jnp.float32).reshape(query_count, HEADS, HD)
    key_heads = keys.astype(jnp.float32).reshape(key_count, HEADS, HD)
    value_heads = values.astype(jnp.float32).reshape(key_count, HEADS, HD)
    scores = jnp.einsum('qhd,khd->hqk', query_heads, key_heads) * (1.0 / math.sqrt(HD))
    if allowed is not None:
        scores = jnp.where(allowed[None, None, :], scores, -1e+30)
    row_max = lax.optimization_barrier(jnp.max(scores, axis=-1, keepdims=True))
    powers = jnp.exp(scores - row_max)
    weights = (powers / lax.optimization_barrier(jnp.sum(powers, axis=-1, keepdims=True))).astype(jnp.bfloat16)
    attended = jnp.einsum('hqk,khd->qhd', weights.astype(jnp.float32), value_heads)
    return attended.reshape(query_count, D)

def branch_output(branch_tokens, modulation, wqkv, w_out, blend, reach):
    height = TR * N_ROW
    breadth = TC * N_COL
    normed = layer_norm(branch_tokens, modulation).reshape(height * breadth, D)
    joined = jnp.dot(normed, wqkv, preferred_element_type=jnp.float32).astype(jnp.bfloat16)
    query_image = joined[:, :D].reshape(height, breadth, D)
    key_image = joined[:, D:2 * D].reshape(height, breadth, D)
    value_image = joined[:, 2 * D:].reshape(height, breadth, D)
    padding = ((HALO, HALO), (HALO, HALO), (0, 0))
    padded_keys = jnp.pad(key_image, padding)
    padded_values = jnp.pad(value_image, padding)
    zero_index = jnp.zeros((), jnp.int32)

    def one_tile(tile_index):
        row_index = (tile_index // N_COL).astype(jnp.int32)
        col_index = (tile_index % N_COL).astype(jnp.int32)
        row_start = (row_index * TR).astype(jnp.int32)
        col_start = (col_index * TC).astype(jnp.int32)
        query_tile = lax.dynamic_slice(query_image, (row_start, col_start, zero_index), (TR, TC, D))
        window_keys = lax.dynamic_slice(padded_keys, (row_start, col_start, zero_index), (TR + 2 * HALO, TC + 2 * HALO, D))
        window_values = lax.dynamic_slice(padded_values, (row_start, col_start, zero_index), (TR + 2 * HALO, TC + 2 * HALO, D))
        row_offsets = jnp.arange(TR + 2 * HALO, dtype=jnp.int32)
        col_offsets = jnp.arange(TC + 2 * HALO, dtype=jnp.int32)
        global_rows = row_start - HALO + row_offsets
        global_cols = col_start - HALO + col_offsets
        row_fine = (global_rows >= 0) & (global_rows < height)
        row_fine = row_fine & (row_offsets >= HALO - reach[0, row_index, col_index])
        row_fine = row_fine & (row_offsets < HALO + TR + reach[1, row_index, col_index])
        col_fine = (global_cols >= 0) & (global_cols < breadth)
        col_fine = col_fine & (col_offsets >= HALO - reach[2, row_index, col_index])
        col_fine = col_fine & (col_offsets < HALO + TC + reach[3, row_index, col_index])
        allowed = (row_fine[:, None] & col_fine[None, :]).reshape(-1)
        return attend(query_tile.reshape(TR * TC, D), window_keys.reshape(-1, D), window_values.reshape(-1, D), allowed)
    tiles = lax.map(one_tile, jnp.arange(N_ROW * N_COL, dtype=jnp.int32))
    window_out = tiles.reshape(N_ROW, N_COL, TR, TC, D).transpose(0, 2, 1, 3, 4).reshape(height, breadth, D)

    def phases(image):
        return image.reshape(TR, N_ROW, TC, N_COL, D).transpose(1, 3, 0, 2, 4).reshape(N_ROW * N_COL, TR * TC, D)

    def one_phase(triple):
        return attend(triple[0], triple[1], triple[2], None).astype(jnp.bfloat16)
    lattice_out = lax.map(one_phase, (phases(query_image), phases(key_image), phases(value_image)))
    dilated_out = lattice_out.reshape(N_ROW, N_COL, TR, TC, D).transpose(2, 0, 3, 1, 4).reshape(height, breadth, D)
    weight = blend[:, :, None]
    mixed = (weight * window_out + (1.0 - weight) * dilated_out.astype(jnp.float32)).astype(jnp.bfloat16)
    projected = jnp.dot(mixed.reshape(height * breadth, D), w_out, preferred_element_type=jnp.float32)
    result = branch_tokens.astype(jnp.float32).reshape(height * breadth, D) + modulation[2] * projected
    return result.reshape(height, breadth, D)

def reference(tokens, modulation, wqkv, w_out, blend, reach):
    uncond = branch_output(tokens[0], modulation, wqkv, w_out, blend, reach)
    cond = branch_output(tokens[1], modulation, wqkv, w_out, blend, reach)
    return ((1.0 - GUIDANCE) * uncond + GUIDANCE * cond).astype(jnp.bfloat16)
```

```python
import functools
import math

import jax
import jax.numpy as jnp
from jax import lax
from jax.experimental import pallas as pl
from jax.experimental.pallas import tpu as pltpu
from jax.sharding import PartitionSpec as P

HEADS = 16
HALO = 4
GUIDANCE = 4.5
LANES = 128
VMEM_LIMIT = 48 * 1024 * 1024

F32 = jnp.float32
BF16 = jnp.bfloat16


def normalise(tokens, modulation):
    widened = tokens.astype(F32)
    centered = widened - jnp.mean(widened, axis=-1, keepdims=True)
    variance = jnp.mean(centered * centered, axis=-1, keepdims=True)
    scaled = centered * lax.rsqrt(variance + 1e-06)
    return (scaled * (1.0 + modulation[1:2]) + modulation[0:1]).astype(BF16)


def head_window(head, head_size, width):
    first = head * head_size
    low = first // LANES * LANES
    high = min(-(-(first + head_size) // LANES) * LANES, width)
    return first, low, high


def attend_head(head, queries, pairs, out_ref, rows):
    width = queries.shape[-1]
    head_size = width // HEADS
    first, low, high = head_window(head, head_size, width)
    lane = lax.broadcasted_iota(jnp.int32, (1, high - low), 1) + low
    inside = (lane >= first) & (lane < first + head_size)
    outside_lane = 0 if first > low else head_size
    query = queries[rows, low:high]
    query = jnp.where(inside, query, jnp.zeros_like(query))
    scores = []
    for keys, values, bias in pairs:
        score = lax.dot_general(
            query, keys[:, low:high], (((1,), (1,)), ((), ())), preferred_element_type=F32
        )
        scores.append(score if bias is None else score + bias[...])
    top = functools.reduce(
        jnp.maximum, [jnp.max(score, axis=-1, keepdims=True) for score in scores]
    )
    total = None
    for score, (keys, values, bias) in zip(scores, pairs):
        powers = jnp.exp2(score - top).astype(BF16)
        value = values[:, low:high]
        value = jnp.where(inside, value, jnp.ones_like(value))
        part = jnp.dot(powers, value, preferred_element_type=F32)
        total = part if total is None else total + part
    attended = total * (1.0 / total[:, outside_lane : outside_lane + 1])
    attended = attended.astype(out_ref.dtype)
    out_ref[rows, low:high] = jnp.where(inside, attended, out_ref[rows, low:high])


def attend_all(queries, pairs, out_ref, block):
    def body(step, carry):
        rows = pl.ds(pl.multiple_of(step * block, block), block)
        for head in range(HEADS):
            attend_head(head, queries, pairs, out_ref, rows)
        return carry

    lax.fori_loop(0, queries.shape[0] // block, body, 0)


def query_scale(feature_width):
    return math.log2(math.e) / math.sqrt(feature_width // HEADS)


def project_kernel(first_block, tokens, modulation, weights, out, normed):
    step = pl.program_id(0)

    @pl.when(step == 0)
    def _():
        normed[...] = normalise(tokens[...], modulation[...])

    product = jnp.dot(normed[...], weights[...], preferred_element_type=F32)
    if first_block == 0:
        product = product * jnp.where(step == 0, query_scale(tokens.shape[-1]), 1.0)
    out[0] = product.astype(BF16)


def project(tokens, modulation, wqkv, first_block):
    count, width = tokens.shape
    blocks = wqkv.shape[1] // width - first_block
    return pl.pallas_call(
        functools.partial(project_kernel, first_block),
        grid=(blocks,),
        in_specs=[
            pl.BlockSpec((count, width), lambda j: (0, 0)),
            pl.BlockSpec(modulation.shape, lambda j: (0, 0)),
            pl.BlockSpec((width, width), lambda j: (0, j + first_block)),
        ],
        out_specs=pl.BlockSpec((1, count, width), lambda j: (j, 0, 0)),
        out_shape=jax.ShapeDtypeStruct((blocks, count, width), BF16),
        scratch_shapes=[pltpu.VMEM((count, width), BF16)],
        compiler_params=pltpu.CompilerParams(vmem_limit_bytes=VMEM_LIMIT),
        cost_estimate=pl.CostEstimate(
            flops=2 * count * width * width * blocks,
            bytes_accessed=2 * (width * width * blocks + count * width * (blocks + 1)),
            transcendentals=count,
        ),
        name="project",
    )(tokens, modulation, wqkv)


def lattice_kernel(tokens, modulation, weights, out, normed, qkv):
    step = pl.program_id(0)

    @pl.when(step == 0)
    def _():
        normed[...] = normalise(tokens[...], modulation[...])

    product = jnp.dot(normed[...], weights[...], preferred_element_type=F32)
    product = product * jnp.where(step == 0, query_scale(tokens.shape[-1]), 1.0)
    qkv[step] = product.astype(BF16)

    @pl.when(step == 2)
    def _():
        out[...] = jnp.zeros_like(out)
        attend_all(qkv.at[0], [(qkv.at[1], qkv.at[2], None)], out, 256)


def lattice(tokens, modulation, wqkv):
    count, width = tokens.shape
    return pl.pallas_call(
        lattice_kernel,
        grid=(3,),
        in_specs=[
            pl.BlockSpec((count, width), lambda j: (0, 0)),
            pl.BlockSpec(modulation.shape, lambda j: (0, 0)),
            pl.BlockSpec((width, width), lambda j: (0, j)),
        ],
        out_specs=pl.BlockSpec((count, width), lambda j: (0, 0)),
        out_shape=jax.ShapeDtypeStruct((count, width), BF16),
        scratch_shapes=[
            pltpu.VMEM((count, width), BF16),
            pltpu.VMEM((3, count, width), BF16),
        ],
        compiler_params=pltpu.CompilerParams(vmem_limit_bytes=VMEM_LIMIT),
        cost_estimate=pl.CostEstimate(
            flops=2 * count * width * width * 3 + 4 * count * count * width * 3,
            bytes_accessed=2 * (3 * width * width + 2 * count * width),
            transcendentals=count * count * HEADS,
        ),
        name="lattice",
    )(tokens, modulation, wqkv)


def window_kernel(queries, keys, values, halo_keys, halo_values, bias, out):
    out[...] = jnp.zeros_like(out)
    pairs = [(keys, values, None), (halo_keys, halo_values, bias)]
    attend_all(queries, pairs, out, 256)


def window(own, halo, bias):
    _, count, width = own.shape
    halo_count = halo.shape[1]

    def part(array, index):
        return pl.BlockSpec((None,) + array.shape[1:], lambda j: (index, 0, 0))

    return pl.pallas_call(
        window_kernel,
        grid=(1,),
        in_specs=[
            part(own, 0),
            part(own, 1),
            part(own, 2),
            part(halo, 0),
            part(halo, 1),
            pl.BlockSpec(bias.shape, lambda j: (0, 0)),
        ],
        out_specs=pl.BlockSpec((count, width), lambda j: (0, 0)),
        out_shape=jax.ShapeDtypeStruct((count, width), BF16),
        compiler_params=pltpu.CompilerParams(vmem_limit_bytes=VMEM_LIMIT),
        cost_estimate=pl.CostEstimate(
            flops=4 * count * (count + halo_count) * width * 3,
            bytes_accessed=2 * (4 * count * width + 2 * halo_count * width),
            transcendentals=count * (count + halo_count) * HEADS,
        ),
        name="window",
    )(own, own, own, halo, halo, bias)


def finish_kernel(
    coefficients, window_mine, window_theirs, dilated, blend, tokens_mine, tokens_theirs, gate, weights, out
):
    mine = coefficients[0]
    theirs = coefficients[1]
    weight = blend[...]
    both = mine * window_mine[...].astype(F32) + theirs * window_theirs[...].astype(F32)
    mixed = (weight * both + (1.0 - weight) * dilated[...].astype(F32)).astype(BF16)
    projected = jnp.dot(mixed, weights[...], preferred_element_type=F32)
    kept = mine * tokens_mine[...].astype(F32) + theirs * tokens_theirs[...].astype(F32)
    out[...] = (kept + gate[...] * projected).astype(BF16)


def finish(coefficients, window_mine, window_theirs, dilated, blend, tokens_mine, tokens_theirs, gate, w_out):
    count, width = window_mine.shape
    vmem = pl.BlockSpec(memory_space=pltpu.VMEM)
    return pl.pallas_call(
        finish_kernel,
        in_specs=[pl.BlockSpec(memory_space=pltpu.SMEM)] + [vmem] * 8,
        out_specs=vmem,
        out_shape=jax.ShapeDtypeStruct((count, width), BF16),
        compiler_params=pltpu.CompilerParams(vmem_limit_bytes=VMEM_LIMIT),
        cost_estimate=pl.CostEstimate(
            flops=2 * count * width * width,
            bytes_accessed=2 * (width * width + 6 * count * width),
            transcendentals=0,
        ),
        name="finish",
    )(coefficients, window_mine, window_theirs, dilated, blend, tokens_mine, tokens_theirs, gate, w_out)


def halo_bias(reach, rows, cols):
    row_start = lax.axis_index("row") * rows
    col_start = lax.axis_index("col") * cols
    height = rows * lax.axis_size("row")
    breadth = cols * lax.axis_size("col")
    row_offsets = jnp.arange(rows + 2 * HALO, dtype=jnp.int32)
    col_offsets = jnp.arange(cols + 2 * HALO, dtype=jnp.int32)
    global_rows = row_start - HALO + row_offsets
    global_cols = col_start - HALO + col_offsets
    row_fine = (global_rows >= 0) & (global_rows < height)
    row_fine = row_fine & (row_offsets >= HALO - reach[0, 0, 0])
    row_fine = row_fine & (row_offsets < HALO + rows + reach[1, 0, 0])
    col_fine = (global_cols >= 0) & (global_cols < breadth)
    col_fine = col_fine & (col_offsets >= HALO - reach[2, 0, 0])
    col_fine = col_fine & (col_offsets < HALO + cols + reach[3, 0, 0])
    allowed = row_fine[:, None] & col_fine[None, :]
    inner = slice(HALO, HALO + cols)
    parts = [
        allowed[:HALO, inner],
        allowed[HALO + rows :, inner],
        allowed[:, :HALO],
        allowed[:, HALO + cols :],
    ]
    joined = jnp.concatenate([part.reshape(-1) for part in parts])
    return jnp.where(joined, 0.0, -1e30).astype(F32).reshape(1, -1)


def halo_tokens(tile):
    rows, cols, width = tile.shape

    def shift(cells, axis, forward):
        count = lax.axis_size(axis)
        if forward:
            pairs = [(i, i + 1) for i in range(count - 1)]
        else:
            pairs = [(i + 1, i) for i in range(count - 1)]
        return lax.ppermute(cells, axis, pairs)

    above = shift(tile[rows - HALO :], "row", True)
    below = shift(tile[:HALO], "row", False)
    right_edge = jnp.concatenate([cells[:, cols - HALO :] for cells in (above, tile, below)], axis=0)
    left_edge = jnp.concatenate([cells[:, :HALO] for cells in (above, tile, below)], axis=0)
    left = shift(right_edge, "col", True)
    right = shift(left_edge, "col", False)
    return jnp.concatenate([cells.reshape(-1, width) for cells in (above, below, left, right)], axis=0)


def on_device(tokens, modulation, wqkv, w_out, blend, reach):
    tile = tokens[0]
    rows, cols, width = tile.shape
    row_groups = lax.axis_size("row")
    col_groups = lax.axis_size("col")
    sub_rows = rows // row_groups
    sub_cols = cols // col_groups
    half = rows // 2 * cols
    branch = lax.axis_index("branch")
    devices = row_groups * col_groups
    coefficients = jnp.stack(
        [
            jnp.where(branch == 1, GUIDANCE, 1.0 - GUIDANCE),
            jnp.where(branch == 1, 1.0 - GUIDANCE, GUIDANCE),
        ]
    ).astype(F32)

    def halves(cells):
        cells = cells.reshape(2, half, width)
        mine = lax.dynamic_index_in_dim(cells, branch, 0, keepdims=False)
        theirs = lax.dynamic_index_in_dim(cells, 1 - branch, 0, keepdims=False)
        return mine, lax.ppermute(theirs, "branch", [(0, 1), (1, 0)])

    outgoing = tile.reshape(sub_rows, row_groups, sub_cols, col_groups, width)
    outgoing = outgoing.transpose(1, 3, 0, 2, 4).reshape(devices, sub_rows * sub_cols, width)
    arrived = lax.all_to_all(outgoing, ("row", "col"), split_axis=0, concat_axis=0, tiled=True)

    flat = tile.reshape(rows * cols, width)
    own = project(flat, modulation, wqkv, 0)
    tokens_mine, tokens_theirs = halves(flat)
    halo = project(halo_tokens(tile), modulation, wqkv, 1)
    window_out = window(own, halo, halo_bias(reach, rows, cols))
    window_mine, window_theirs = halves(window_out)

    arrived = arrived.reshape(devices, sub_rows, sub_cols, width).transpose(1, 0, 2, 3)
    lattice_out = lattice(arrived.reshape(rows * cols, width), modulation, wqkv)
    lattice_mine, lattice_theirs = halves(lattice_out)
    combined = coefficients[0] * lattice_mine.astype(F32) + coefficients[1] * lattice_theirs.astype(F32)
    combined = combined.astype(BF16).reshape(devices, sub_cols, width)
    returned = lax.all_to_all(combined, ("row", "col"), split_axis=0, concat_axis=0, tiled=True)
    returned = returned.reshape(row_groups, col_groups, sub_cols, width).transpose(0, 2, 1, 3)
    dilated = returned.reshape(half, width)

    weight = lax.dynamic_index_in_dim(blend.reshape(2, half, 1), branch, 0, keepdims=False)
    guided = finish(
        coefficients,
        window_mine,
        window_theirs,
        dilated,
        weight,
        tokens_mine,
        tokens_theirs,
        modulation[2:3],
        w_out,
    )
    return guided.reshape(rows // 2, cols, width)


def solution(mesh):
    in_specs = (
        P("branch", "row", "col", None),
        P(),
        P(),
        P(),
        P("row", "col"),
        P(None, "row", "col"),
    )
    out_specs = P(("row", "branch"), "col", None)
    return jax.shard_map(
        on_device, mesh=mesh, in_specs=in_specs, out_specs=out_specs, check_vma=False
    )
```

```python
import functools
import math

import jax
import jax.numpy as jnp
import numpy as np
from jax import lax
from jax.experimental import pallas as pl
from jax.experimental.pallas import tpu as pltpu
from jax.sharding import PartitionSpec as P

HEADS = 16
HALO = 4
GUIDANCE = 4.5
LANES = 128
VMEM_LIMIT = 60 * 1024 * 1024
ROOMY_LIMIT = 56 * 1024 * 1024
SMALL_LIMIT = 16 * 1024 * 1024

F32 = jnp.float32
BF16 = jnp.bfloat16

VMEM = pl.BlockSpec(memory_space=pltpu.VMEM)
SMEM = pl.BlockSpec(memory_space=pltpu.SMEM)
ANY = pl.BlockSpec(memory_space=pl.ANY)
HBM = pl.BlockSpec(memory_space=pltpu.HBM)
MARK = jax.ShapeDtypeStruct((8, LANES), F32)


def normalise(tokens, modulation):
    widened = tokens.astype(F32)
    centered = widened - jnp.mean(widened, axis=-1, keepdims=True)
    variance = jnp.mean(centered * centered, axis=-1, keepdims=True)
    scaled = centered * lax.rsqrt(variance + 1e-06)
    return (scaled * (1.0 + modulation[1:2]) + modulation[0:1]).astype(BF16)


def head_window(head, head_size, width):
    first = head * head_size
    low = first // LANES * LANES
    high = min(-(-(first + head_size) // LANES) * LANES, width)
    return first, low, high


def attend_head(head, queries, pairs, out):
    width = queries.shape[-1]
    head_size = width // HEADS
    first, low, high = head_window(head, head_size, width)
    lane = lax.broadcasted_iota(jnp.int32, (1, high - low), 1) + low
    inside = (lane >= first) & (lane < first + head_size)
    outside_lane = 0 if first > low else head_size
    query = queries[:, low:high]
    query = jnp.where(inside, query, jnp.zeros_like(query))
    scores = []
    for keys, values, bias in pairs:
        score = lax.dot_general(
            query, keys[:, low:high], (((1,), (1,)), ((), ())), preferred_element_type=F32
        )
        scores.append(score if bias is None else score + bias)
    top = functools.reduce(
        jnp.maximum, [jnp.max(score, axis=-1, keepdims=True) for score in scores]
    )
    total = None
    for score, (keys, values, bias) in zip(scores, pairs):
        powers = jnp.exp2(score - top).astype(BF16)
        value = values[:, low:high]
        value = jnp.where(inside, value, jnp.ones_like(value))
        part = jnp.dot(powers, value, preferred_element_type=F32)
        total = part if total is None else total + part
    attended = total * (1.0 / total[:, outside_lane : outside_lane + 1])
    attended = attended.astype(out.dtype)
    out[:, low:high] = jnp.where(inside, attended, out[:, low:high])


def attend_all(queries, pairs, out):
    out[...] = jnp.zeros_like(out)
    for head in range(HEADS):
        attend_head(head, queries, pairs, out)


def query_scale(feature_width):
    return math.log2(math.e) / math.sqrt(feature_width // HEADS)


def fetch_weights(weights, slots, sems, first_block):
    width = weights.shape[0]
    copies = []
    for slot in range(slots.shape[0]):
        start = (first_block + slot) * width
        copy = pltpu.make_async_copy(
            weights.at[:, start : start + width], slots.at[slot], sems.at[slot]
        )
        copy.start()
        copies.append(copy)
    return copies


def project_blocks(normed, copies, slots, out, first_block, sends=()):
    for slot, copy in enumerate(copies):
        copy.wait()
        product = jnp.dot(normed[...], slots[slot], preferred_element_type=F32)
        if first_block + slot == 0:
            product = product * query_scale(normed.shape[-1])
        out[slot] = product.astype(BF16)
        if sends:
            sends[slot].start()


def weight_scratch(width, blocks):
    return [pltpu.VMEM((blocks, width, width), BF16), pltpu.SemaphoreType.DMA((blocks,))]


def give_halves(branch, cells, mine, theirs):
    half = mine.shape[0]
    mine[...] = cells[pl.ds(pl.multiple_of(branch * half, half), half)]
    theirs[...] = cells[pl.ds(pl.multiple_of((1 - branch) * half, half), half)]


def own_kernel(rows, cols, tokens, modulation, weights, *refs):
    own, top, bottom, left, right, mark = refs[:-8]
    normed, qkv, left_strip, right_strip, slots, sems, own_sems, strip_sems = refs[-8:]
    copies = fetch_weights(weights, slots, sems, 0)
    strip = HALO * cols
    sends = []

    def send(source, target):
        copy = pltpu.make_async_copy(source, target, strip_sems.at[len(sends)])
        copy.start()
        sends.append(copy)

    send(tokens.at[:strip], top)
    send(tokens.at[rows * cols - strip :], bottom)
    upper = lax.broadcasted_iota(jnp.int32, (2 * HALO, 1), 0) < HALO
    wide = 2 * HALO
    for pair in range(rows // 2):
        place = slice(wide * pair, wide * (pair + 1))
        start = 2 * pair * cols
        first = tokens[start : start + wide].astype(F32)
        second = tokens[start + cols : start + cols + wide].astype(F32)
        left_strip[place] = jnp.where(upper, first, pltpu.roll(second, HALO, 0)).astype(BF16)
        start += cols - wide
        first = tokens[start : start + wide].astype(F32)
        second = tokens[start + cols : start + cols + wide].astype(F32)
        right_strip[place] = jnp.where(upper, pltpu.roll(first, HALO, 0), second).astype(BF16)
    send(left_strip, left)
    send(right_strip, right)
    mark[...] = jnp.zeros_like(mark)
    normed[...] = normalise(tokens[...], modulation[...])
    outs = [pltpu.make_async_copy(qkv.at[j], own.at[j], own_sems.at[j]) for j in range(3)]
    project_blocks(normed, copies, slots, qkv, 0, outs)
    for copy in sends + outs:
        copy.wait()


def own_tile(tokens, modulation, wqkv, rows, cols):
    count, width = tokens.shape

    def tokens_of(number):
        return jax.ShapeDtypeStruct((number, width), BF16)

    shapes = [jax.ShapeDtypeStruct((3, count, width), BF16)]
    shapes += [tokens_of(HALO * cols)] * 2
    shapes += [tokens_of(HALO * rows)] * 2
    return pl.pallas_call(
        functools.partial(own_kernel, rows, cols),
        in_specs=[VMEM, VMEM, HBM],
        out_specs=[HBM] * len(shapes) + [VMEM],
        out_shape=shapes + [MARK],
        scratch_shapes=[
            pltpu.VMEM((count, width), BF16),
            pltpu.VMEM((3, count, width), BF16),
            pltpu.VMEM((HALO * rows, width), BF16),
            pltpu.VMEM((HALO * rows, width), BF16),
        ]
        + weight_scratch(width, 3)
        + [pltpu.SemaphoreType.DMA((3,)), pltpu.SemaphoreType.DMA((len(shapes) - 1,))],
        compiler_params=pltpu.CompilerParams(vmem_limit_bytes=VMEM_LIMIT),
        cost_estimate=pl.CostEstimate(
            flops=2 * count * width * width * 3,
            bytes_accessed=2 * (width * width * 3 + count * width * 4),
            transcendentals=count,
        ),
        name="own_tile",
    )(tokens, modulation, wqkv)


def lattice_project_kernel(tokens, modulation, weights, *refs):
    qkv, normed, slots, sems = refs[-4:]
    copies = fetch_weights(weights, slots, sems, 0)
    normed[...] = normalise(tokens[...], modulation[...])
    project_blocks(normed, copies, slots, qkv, 0)


def lattice_project(tokens, modulation, wqkv, after):
    count, width = tokens.shape
    return pl.pallas_call(
        lattice_project_kernel,
        in_specs=[VMEM, VMEM, HBM] + [ANY] * len(after),
        out_specs=VMEM,
        out_shape=jax.ShapeDtypeStruct((3, count, width), BF16),
        scratch_shapes=[pltpu.VMEM((count, width), BF16)] + weight_scratch(width, 3),
        compiler_params=pltpu.CompilerParams(vmem_limit_bytes=ROOMY_LIMIT),
        cost_estimate=pl.CostEstimate(flops=0, bytes_accessed=2 * count * width, transcendentals=0),
        name="lattice_project",
    )(tokens, modulation, wqkv, *after)


def lattice_attend_kernel(branch, qkv, *refs):
    mine, theirs, whole = refs[-3:]
    attend_all(qkv.at[0], [(qkv.at[1], qkv.at[2], None)], whole)
    give_halves(branch[0], whole, mine, theirs)


def lattice_attend(branch, qkv, after):
    _, count, width = qkv.shape
    half = jax.ShapeDtypeStruct((count // 2, width), BF16)
    return pl.pallas_call(
        lattice_attend_kernel,
        in_specs=[SMEM, VMEM] + [HBM] * len(after),
        out_specs=[VMEM, VMEM],
        out_shape=[half, half],
        scratch_shapes=[pltpu.VMEM((count, width), BF16)],
        compiler_params=pltpu.CompilerParams(vmem_limit_bytes=ROOMY_LIMIT),
        cost_estimate=pl.CostEstimate(
            flops=4 * count * count * width * 3,
            bytes_accessed=2 * 4 * count * width,
            transcendentals=count * count * HEADS,
        ),
        name="lattice_attend",
    )(branch, qkv, *after)


def combine_kernel(coefficients, branch, tokens, mine, theirs, *refs):
    out, tokens_send, sem = refs[-3:]
    half = mine.shape[0]
    rows = pl.ds(pl.multiple_of((1 - branch[0]) * half, half), half)
    copy = pltpu.make_async_copy(tokens.at[rows], tokens_send, sem)
    copy.start()
    both = coefficients[0] * mine[...].astype(F32) + coefficients[1] * theirs[...].astype(F32)
    out[...] = both.astype(BF16)
    copy.wait()


def combine(coefficients, branch, tokens, mine, theirs, after):
    half = jax.ShapeDtypeStruct(mine.shape, BF16)
    return pl.pallas_call(
        combine_kernel,
        in_specs=[SMEM, SMEM, HBM, VMEM, VMEM] + [HBM] * len(after),
        out_specs=[VMEM, HBM],
        out_shape=[half, half],
        scratch_shapes=[pltpu.SemaphoreType.DMA],
        compiler_params=pltpu.CompilerParams(vmem_limit_bytes=ROOMY_LIMIT),
        cost_estimate=pl.CostEstimate(flops=3 * mine.size, bytes_accessed=6 * mine.size, transcendentals=0),
        name="combine",
    )(coefficients, branch, tokens, mine, theirs, *after)


def halo_places(rows, cols):
    def block(first_row, height, first_col, breadth):
        row, col = np.mgrid[first_row : first_row + height, first_col : first_col + breadth]
        return np.stack([row.reshape(-1), col.reshape(-1)])

    blocks = [block(-HALO, HALO, 0, cols), block(rows, HALO, 0, cols)]
    blocks += [block(0, rows, -HALO, HALO), block(0, rows, cols, HALO)]
    blocks += [block(-HALO, HALO, -HALO, HALO), block(-HALO, HALO, cols, HALO)]
    blocks += [block(rows, HALO, -HALO, HALO), block(rows, HALO, cols, HALO)]
    return np.concatenate(blocks, axis=1).astype(np.int32)


def window_kernel(rows, cols, parts, branch, limits, places, tokens, own, *refs):
    halo, (modulation, weights) = refs[:parts], refs[parts : parts + 2]
    mine, theirs, gathered, normed, halo_kv, own_qkv, whole, slots, sems, own_sems, halo_sems, sent = refs[-12:]
    half = whole.shape[0] // 2
    first = pl.ds(pl.multiple_of(branch[0] * half, half), half)
    second = pl.ds(pl.multiple_of((1 - branch[0]) * half, half), half)
    sends = [
        pltpu.make_async_copy(tokens.at[first], mine.at[1], sent.at[0]),
        pltpu.make_async_copy(whole.at[first], mine.at[0], sent.at[1]),
        pltpu.make_async_copy(whole.at[second], theirs, sent.at[2]),
    ]
    arrivals = []
    start = 0
    for index, part in enumerate(halo):
        place = gathered.at[start : start + part.shape[0]]
        arrivals.append(pltpu.make_async_copy(part, place, halo_sems.at[index]))
        arrivals[-1].start()
        start += part.shape[0]
    copies = fetch_weights(weights, slots, sems, 1)
    own_copies = [pltpu.make_async_copy(own.at[j], own_qkv.at[j], own_sems.at[j]) for j in range(3)]
    for copy in own_copies + sends[:1]:
        copy.start()
    row, col = places[0:1], places[1:2]
    allowed = (row >= -limits[0]) & (row < rows + limits[1])
    allowed = allowed & (col >= -limits[2]) & (col < cols + limits[3])
    bias = jnp.where(allowed, 0.0, -1e30).astype(F32)
    for copy in arrivals:
        copy.wait()
    normed[...] = normalise(gathered[...], modulation[...])
    project_blocks(normed, copies, slots, halo_kv, 1)
    for copy in own_copies:
        copy.wait()
    pairs = [(own_qkv.at[1], own_qkv.at[2], None), (halo_kv.at[0], halo_kv.at[1], bias)]
    attend_all(own_qkv.at[0], pairs, whole)
    for copy in sends[1:]:
        copy.start()
    for copy in sends:
        copy.wait()


def window(branch, limits, tokens, own, halo, modulation, wqkv, rows, cols, after):
    _, count, width = own.shape
    places = jnp.asarray(halo_places(rows, cols))
    halo_count = places.shape[1]
    half = (count // 2, width)
    return pl.pallas_call(
        functools.partial(window_kernel, rows, cols, len(halo)),
        in_specs=[SMEM, SMEM, VMEM, HBM, HBM] + [HBM] * len(halo) + [VMEM, HBM] + [HBM] * len(after),
        out_specs=[HBM, HBM],
        out_shape=[jax.ShapeDtypeStruct((2,) + half, BF16), jax.ShapeDtypeStruct(half, BF16)],
        scratch_shapes=[
            pltpu.VMEM((halo_count, width), BF16),
            pltpu.VMEM((halo_count, width), BF16),
            pltpu.VMEM((2, halo_count, width), BF16),
            pltpu.VMEM((3, count, width), BF16),
            pltpu.VMEM((count, width), BF16),
        ]
        + weight_scratch(width, 2)
        + [pltpu.SemaphoreType.DMA((3,)), pltpu.SemaphoreType.DMA((len(halo),)), pltpu.SemaphoreType.DMA((3,))],
        compiler_params=pltpu.CompilerParams(vmem_limit_bytes=VMEM_LIMIT),
        cost_estimate=pl.CostEstimate(
            flops=4 * count * (count + halo_count) * width * 3 + 4 * halo_count * width * width,
            bytes_accessed=2 * (4 * count * width + 2 * halo_count * width + 2 * width * width),
            transcendentals=count * (count + halo_count) * HEADS,
        ),
        name="window",
    )(branch, limits, places, tokens, own, *halo, modulation, wqkv, *after)


def finish_kernel(coefficients, mine, window_theirs, tokens_theirs, dilated, blend, gate, weights, out):
    weight = blend[...]

    def branches(index, theirs):
        return coefficients[0] * mine[index].astype(F32) + coefficients[1] * theirs[...].astype(F32)

    mixed = (weight * branches(0, window_theirs) + (1.0 - weight) * dilated[...].astype(F32)).astype(BF16)
    projected = jnp.dot(mixed, weights[...], preferred_element_type=F32)
    out[...] = (branches(1, tokens_theirs) + gate[...] * projected).astype(BF16)


def finish(coefficients, mine, window_theirs, tokens_theirs, dilated, blend, gate, w_out):
    count, width = dilated.shape
    return pl.pallas_call(
        finish_kernel,
        in_specs=[SMEM] + [VMEM] * 7,
        out_specs=VMEM,
        out_shape=jax.ShapeDtypeStruct((count, width), BF16),
        compiler_params=pltpu.CompilerParams(vmem_limit_bytes=SMALL_LIMIT),
        cost_estimate=pl.CostEstimate(
            flops=2 * count * width * width,
            bytes_accessed=2 * (width * width + 6 * count * width),
            transcendentals=0,
        ),
        name="finish",
    )(coefficients, mine, window_theirs, tokens_theirs, dilated, blend, gate, w_out)


def window_limits(reach):
    row, col = lax.axis_index("row"), lax.axis_index("col")
    last_row, last_col = lax.axis_size("row") - 1, lax.axis_size("col") - 1
    inner = jnp.stack([row > 0, row < last_row, col > 0, col < last_col])
    return jnp.where(inner, reach.reshape(4), 0)


def shift(cells, axis, forward):
    count = lax.axis_size(axis)
    if forward:
        pairs = [(i, i + 1) for i in range(count - 1)]
    else:
        pairs = [(i + 1, i) for i in range(count - 1)]
    return lax.ppermute(cells, axis, pairs)


def side_tokens(top, bottom, left, right):
    return (
        shift(bottom, "row", True),
        shift(top, "row", False),
        shift(right, "col", True),
        shift(left, "col", False),
    )


def corner_tokens(left, right):
    square = HALO * HALO
    last = left.shape[0] - square
    lower = jnp.concatenate([left[last:], right[last:]], axis=0)
    upper = jnp.concatenate([left[:square], right[:square]], axis=0)
    return shift(lower, "row", True), shift(upper, "row", False)


def on_device(tokens, modulation, wqkv, w_out, blend, reach):
    tile = tokens[0]
    rows, cols, width = tile.shape
    row_groups = lax.axis_size("row")
    col_groups = lax.axis_size("col")
    sub_rows = rows // row_groups
    sub_cols = cols // col_groups
    half = rows // 2 * cols
    branch = lax.axis_index("branch")
    devices = row_groups * col_groups
    coefficients = jnp.stack(
        [
            jnp.where(branch == 1, GUIDANCE, 1.0 - GUIDANCE),
            jnp.where(branch == 1, 1.0 - GUIDANCE, GUIDANCE),
        ]
    ).astype(F32)

    branch_scalar = branch.reshape(1).astype(jnp.int32)

    def other_core(cells):
        return lax.ppermute(cells, "branch", [(0, 1), (1, 0)])

    outgoing = tile.reshape(sub_rows, row_groups, sub_cols, col_groups, width)
    outgoing = outgoing.transpose(1, 3, 0, 2, 4).reshape(devices, sub_rows * sub_cols, width)
    arrived = lax.all_to_all(outgoing, ("row", "col"), split_axis=0, concat_axis=0, tiled=True)

    flat = tile.reshape(rows * cols, width)
    own, top, bottom, left, right, mark = own_tile(flat, modulation, wqkv, rows, cols)
    sides = side_tokens(top, bottom, left, right)
    corners = corner_tokens(*sides[2:])

    arrived = arrived.reshape(devices, sub_rows, sub_cols, width).transpose(1, 0, 2, 3)
    arrived = arrived.reshape(rows * cols, width)
    lattice_qkv = lattice_project(arrived, modulation, wqkv, [mark])
    lattice_mine, lattice_send = lattice_attend(branch_scalar, lattice_qkv, sides)
    combined, tokens_send = combine(
        coefficients, branch_scalar, flat, lattice_mine, other_core(lattice_send), corners
    )
    tokens_theirs = other_core(tokens_send)
    combined = combined.reshape(devices, sub_cols, width)
    returned = lax.all_to_all(combined, ("row", "col"), split_axis=0, concat_axis=0, tiled=True)

    limits = window_limits(reach)
    mine, send = window(
        branch_scalar, limits, flat, own, sides + corners, modulation, wqkv, rows, cols, [combined]
    )
    window_theirs = other_core(send)
    returned = returned.reshape(row_groups, col_groups, sub_cols, width).transpose(0, 2, 1, 3)
    dilated = returned.reshape(half, width)

    weight = lax.dynamic_index_in_dim(blend.reshape(2, half, 1), branch, 0, keepdims=False)
    guided = finish(
        coefficients, mine, window_theirs, tokens_theirs, dilated, weight, modulation[2:3], w_out
    )
    return guided.reshape(rows // 2, cols, width)


def solution(mesh):
    in_specs = (
        P("branch", "row", "col", None),
        P(),
        P(),
        P(),
        P("row", "col"),
        P(None, "row", "col"),
    )
    out_specs = P(("row", "branch"), "col", None)
    return jax.shard_map(
        on_device, mesh=mesh, in_specs=in_specs, out_specs=out_specs, check_vma=False
    )
```

```python
import functools
import math

import jax
import jax.numpy as jnp
import numpy as np
from jax import lax
from jax.experimental import pallas as pl
from jax.experimental.pallas import tpu as pltpu
from jax.sharding import PartitionSpec as P

HEADS = 16
HALO = 4
GUIDANCE = 4.5
LANES = 128
VMEM_LIMIT = 56 * 1024 * 1024
SMALL_LIMIT = 16 * 1024 * 1024
CHUNK = 768
IN_FLIGHT = 3

F32 = jnp.float32
BF16 = jnp.bfloat16

VMEM = pl.BlockSpec(memory_space=pltpu.VMEM)
SMEM = pl.BlockSpec(memory_space=pltpu.SMEM)
ANY = pl.BlockSpec(memory_space=pl.ANY)
HBM = pl.BlockSpec(memory_space=pltpu.HBM)
MARK = jax.ShapeDtypeStruct((8, LANES), F32)


def normalise(tokens, modulation):
    widened = tokens.astype(F32)
    centered = widened - jnp.mean(widened, axis=-1, keepdims=True)
    variance = jnp.mean(centered * centered, axis=-1, keepdims=True)
    scaled = centered * lax.rsqrt(variance + 1e-06)
    return (scaled * (1.0 + modulation[1:2]) + modulation[0:1]).astype(BF16)


def head_window(head, head_size, width):
    first = head * head_size
    low = first // LANES * LANES
    high = min(-(-(first + head_size) // LANES) * LANES, width)
    return first, low, high


def attend_head(head, queries, pairs, out):
    width = queries.shape[-1]
    head_size = width // HEADS
    first, low, high = head_window(head, head_size, width)
    lane = lax.broadcasted_iota(jnp.int32, (1, high - low), 1) + low
    inside = (lane >= first) & (lane < first + head_size)
    outside_lane = 0 if first > low else head_size
    query = queries[:, low:high]
    query = jnp.where(inside, query, jnp.zeros_like(query))
    scores = []
    for keys, values, bias in pairs:
        score = lax.dot_general(
            query, keys[:, low:high], (((1,), (1,)), ((), ())), preferred_element_type=F32
        )
        scores.append(score if bias is None else score + bias)
    top = functools.reduce(
        jnp.maximum, [jnp.max(score, axis=-1, keepdims=True) for score in scores]
    )
    total = None
    for score, (keys, values, bias) in zip(scores, pairs):
        powers = jnp.exp2(score - top).astype(BF16)
        value = values[:, low:high]
        value = jnp.where(inside, value, jnp.ones_like(value))
        part = jnp.dot(powers, value, preferred_element_type=F32)
        total = part if total is None else total + part
    attended = total * (1.0 / total[:, outside_lane : outside_lane + 1])
    attended = attended.astype(out.dtype)
    out[:, low:high] = jnp.where(inside, attended, out[:, low:high])


def attend_all(queries, pairs, out):
    out[...] = jnp.zeros_like(out)
    for head in range(HEADS):
        attend_head(head, queries, pairs, out)


def query_scale(feature_width):
    return math.log2(math.e) / math.sqrt(feature_width // HEADS)


def column_chunks(width):
    return [(start, min(CHUNK, width - start)) for start in range(0, width, CHUNK)]


def stream_project(normed, weights, first_column, buffer, sems, out, sends=()):
    width = normed.shape[-1]
    chunks = column_chunks(out.shape[-1])
    copies = [
        pltpu.make_async_copy(
            weights.at[:, first_column + start : first_column + start + size],
            buffer.at[:, start : start + size],
            sems.at[index],
        )
        for index, (start, size) in enumerate(chunks)
    ]
    for copy in copies[:IN_FLIGHT]:
        copy.start()

    def multiply():
        for index, (start, size) in enumerate(chunks):
            copies[index].wait()
            if index + IN_FLIGHT < len(chunks):
                copies[index + IN_FLIGHT].start()
            product = jnp.dot(normed[...], buffer[:, start : start + size], preferred_element_type=F32)
            if first_column + start < width:
                column = lax.broadcasted_iota(jnp.int32, (1, size), 1) + first_column + start
                product = product * jnp.where(column < width, query_scale(width), 1.0)
            out[:, start : start + size] = product.astype(BF16)
            if sends:
                sends[index].start()

    return multiply


def weight_scratch(width, columns):
    return [pltpu.VMEM((width, columns), BF16), pltpu.SemaphoreType.DMA((len(column_chunks(columns)),))]


def split_heads(qkv, width):
    return [qkv.at[:, start : start + width] for start in range(0, qkv.shape[-1], width)]


def strips_kernel(place_of, tile, pair, other, first, last, sems):
    rows, cols, _ = tile.shape
    wide = 2 * HALO
    copies = [
        pltpu.make_async_copy(tile.at[:, :wide], first, sems.at[0]),
        pltpu.make_async_copy(tile.at[:, cols - wide :], last, sems.at[1]),
    ]
    for copy in copies:
        copy.start()
    upper = lax.broadcasted_iota(jnp.int32, (wide, 1), 0) < HALO
    even = place_of[1] == 0
    for copy in copies:
        copy.wait()
    for step in range(rows // 2):
        place = slice(wide * step, wide * (step + 1))
        one, two = first[2 * step].astype(F32), first[2 * step + 1].astype(F32)
        left = jnp.where(upper, one, pltpu.roll(two, HALO, 0)).astype(BF16)
        one, two = last[2 * step].astype(F32), last[2 * step + 1].astype(F32)
        right = jnp.where(upper, pltpu.roll(one, HALO, 0), two).astype(BF16)
        pair[place] = jnp.where(even, right, left)
        other[place] = jnp.where(even, left, right)


def strips(place_of, tile):
    rows, cols, width = tile.shape
    shape = jax.ShapeDtypeStruct((rows * HALO, width), BF16)
    return pl.pallas_call(
        strips_kernel,
        in_specs=[SMEM, HBM],
        out_specs=[VMEM, VMEM],
        out_shape=[shape, shape],
        scratch_shapes=[pltpu.VMEM((rows, 2 * HALO, width), BF16)] * 2 + [pltpu.SemaphoreType.DMA((2,))],
        compiler_params=pltpu.CompilerParams(vmem_limit_bytes=VMEM_LIMIT),
        cost_estimate=pl.CostEstimate(flops=0, bytes_accessed=8 * rows * HALO * width, transcendentals=0),
        name="strips",
    )(place_of, tile)


def hold_kernel(cells, after, out):
    pass


def hold(cells, after):
    return pl.pallas_call(
        hold_kernel,
        in_specs=[ANY, ANY],
        out_specs=ANY,
        out_shape=jax.ShapeDtypeStruct(cells.shape, cells.dtype),
        input_output_aliases={0: 0},
        name="hold",
    )(cells, after)


def own_kernel(half, branch, tokens, modulation, weights, *refs):
    own, tokens_send, mark, here, normed, qkv, buffer, sems, own_sems, copy_sems = refs
    arrival = pltpu.make_async_copy(tokens, here, copy_sems.at[0])
    arrival.start()
    sends = [
        pltpu.make_async_copy(
            qkv.at[:, start : start + size], own.at[:, start : start + size], own_sems.at[index]
        )
        for index, (start, size) in enumerate(column_chunks(qkv.shape[-1]))
    ]
    multiply = stream_project(normed, weights, 0, buffer, sems, qkv, sends)
    mark[...] = jnp.zeros_like(mark)
    arrival.wait()
    other = pl.ds(pl.multiple_of((1 - branch[0]) * half, half), half)
    sends.append(pltpu.make_async_copy(here.at[other], tokens_send, copy_sems.at[1]))
    sends[-1].start()
    normed[...] = normalise(here[...], modulation[...])
    multiply()
    for copy in sends:
        copy.wait()


def own_tile(branch, tokens, modulation, wqkv):
    count, width = tokens.shape
    columns = wqkv.shape[1]
    half = count // 2
    return pl.pallas_call(
        functools.partial(own_kernel, half),
        in_specs=[SMEM, HBM, VMEM, HBM],
        out_specs=[HBM, HBM, VMEM],
        out_shape=[
            jax.ShapeDtypeStruct((count, columns), BF16),
            jax.ShapeDtypeStruct((half, width), BF16),
            MARK,
        ],
        scratch_shapes=[
            pltpu.VMEM((count, width), BF16),
            pltpu.VMEM((count, width), BF16),
            pltpu.VMEM((count, columns), BF16),
        ]
        + weight_scratch(width, columns)
        + [pltpu.SemaphoreType.DMA((len(column_chunks(columns)),)), pltpu.SemaphoreType.DMA((2,))],
        compiler_params=pltpu.CompilerParams(vmem_limit_bytes=VMEM_LIMIT),
        cost_estimate=pl.CostEstimate(
            flops=2 * count * width * columns,
            bytes_accessed=2 * (width * columns + count * (columns + 2 * width)),
            transcendentals=count,
        ),
        name="own_tile",
    )(branch, tokens, modulation, wqkv)


def lattice_kernel(tokens, modulation, weights, *refs):
    whole, normed, qkv, buffer, sems = refs[-5:]
    multiply = stream_project(normed, weights, 0, buffer, sems, qkv)
    normed[...] = normalise(tokens[...], modulation[...])
    multiply()
    queries, keys, values = split_heads(qkv, tokens.shape[1])
    attend_all(queries, [(keys, values, None)], whole)


def lattice(tokens, modulation, wqkv, after):
    count, width = tokens.shape
    columns = wqkv.shape[1]
    return pl.pallas_call(
        lattice_kernel,
        in_specs=[VMEM, VMEM, HBM] + [ANY] * len(after),
        out_specs=VMEM,
        out_shape=jax.ShapeDtypeStruct((count, width), BF16),
        scratch_shapes=[pltpu.VMEM((count, width), BF16), pltpu.VMEM((count, columns), BF16)]
        + weight_scratch(width, columns),
        compiler_params=pltpu.CompilerParams(vmem_limit_bytes=VMEM_LIMIT),
        cost_estimate=pl.CostEstimate(
            flops=2 * count * width * columns + 4 * count * count * width * 3,
            bytes_accessed=2 * (width * columns + 2 * count * width),
            transcendentals=count * count * HEADS,
        ),
        name="lattice",
    )(tokens, modulation, wqkv, *after)


def other_half_kernel(branch, whole, *refs):
    theirs = refs[-1]
    half = theirs.shape[0]
    theirs[...] = whole[pl.ds(pl.multiple_of((1 - branch[0]) * half, half), half)]


def other_half(branch, whole, after):
    half = (whole.shape[0] // 2, whole.shape[1])
    return pl.pallas_call(
        other_half_kernel,
        in_specs=[SMEM, VMEM] + [HBM] * len(after),
        out_specs=VMEM,
        out_shape=jax.ShapeDtypeStruct(half, BF16),
        compiler_params=pltpu.CompilerParams(vmem_limit_bytes=VMEM_LIMIT),
        cost_estimate=pl.CostEstimate(flops=0, bytes_accessed=2 * whole.size, transcendentals=0),
        name="other_half",
    )(branch, whole, *after)


def combine_kernel(coefficients, branch, whole, theirs, out):
    half = theirs.shape[0]
    mine = whole[pl.ds(pl.multiple_of(branch[0] * half, half), half)]
    both = coefficients[0] * mine.astype(F32) + coefficients[1] * theirs[...].astype(F32)
    out[...] = both.astype(BF16)


def combine(coefficients, branch, whole, theirs):
    return pl.pallas_call(
        combine_kernel,
        in_specs=[SMEM, SMEM, VMEM, VMEM],
        out_specs=VMEM,
        out_shape=jax.ShapeDtypeStruct(theirs.shape, BF16),
        compiler_params=pltpu.CompilerParams(vmem_limit_bytes=VMEM_LIMIT),
        cost_estimate=pl.CostEstimate(flops=3 * theirs.size, bytes_accessed=6 * theirs.size, transcendentals=0),
        name="combine",
    )(coefficients, branch, whole, theirs)


def halo_places(rows, cols):
    def block(first_row, height, first_col, breadth):
        row, col = np.mgrid[first_row : first_row + height, first_col : first_col + breadth]
        return np.stack([row.reshape(-1), col.reshape(-1)])

    lines = []
    for pair, other in ((cols, -HALO), (-HALO, cols)):
        blocks = [block(-HALO, HALO, 0, cols), block(-HALO, HALO, pair, HALO)]
        blocks += [block(rows, HALO, 0, cols), block(rows, HALO, pair, HALO)]
        blocks += [block(0, rows, pair, HALO), block(0, rows, other, HALO)]
        blocks += [block(-HALO, HALO, other, HALO), block(rows, HALO, other, HALO)]
        lines.append(np.concatenate(blocks, axis=1))
    return np.concatenate(lines, axis=0).astype(np.int32)


def window_kernel(rows, cols, parts, branch, limits, places, tokens, own, *refs):
    halo, (modulation, weights) = refs[:parts], refs[parts : parts + 2]
    mine, theirs, here, gathered, normed, halo_kv, qkv, whole, buffer, sems, copy_sems = refs[-11:]
    half, width = theirs.shape
    first = pl.ds(pl.multiple_of(branch[0] * half, half), half)
    second = pl.ds(pl.multiple_of((1 - branch[0]) * half, half), half)
    arrivals = []
    start = 0
    for index, part in enumerate(halo):
        place = gathered.at[start : start + part.shape[0]]
        arrivals.append(pltpu.make_async_copy(part, place, copy_sems.at[index]))
        arrivals[-1].start()
        start += part.shape[0]
    multiply = stream_project(normed, weights, width, buffer, sems, halo_kv)
    own_copy = pltpu.make_async_copy(own, qkv, copy_sems.at[parts])
    tokens_copy = pltpu.make_async_copy(tokens.at[first], here, copy_sems.at[parts + 1])
    sends = [
        pltpu.make_async_copy(here, mine.at[1], copy_sems.at[parts + 2]),
        pltpu.make_async_copy(whole.at[first], mine.at[0], copy_sems.at[parts + 3]),
        pltpu.make_async_copy(whole.at[second], theirs, copy_sems.at[parts + 4]),
    ]
    own_copy.start()
    tokens_copy.start()
    even = branch[1] == 0
    row = jnp.where(even, places[0:1], places[2:3])
    col = jnp.where(even, places[1:2], places[3:4])
    allowed = (row >= -limits[0]) & (row < rows + limits[1])
    allowed = allowed & (col >= -limits[2]) & (col < cols + limits[3])
    bias = jnp.where(allowed, 0.0, -1e30).astype(F32)
    for copy in arrivals:
        copy.wait()
    normed[...] = normalise(gathered[...], modulation[...])
    multiply()
    own_copy.wait()
    tokens_copy.wait()
    sends[0].start()
    queries, keys, values = split_heads(qkv, width)
    halo_keys, halo_values = split_heads(halo_kv, width)
    attend_all(queries, [(keys, values, None), (halo_keys, halo_values, bias)], whole)
    for copy in sends[1:]:
        copy.start()
    for copy in sends:
        copy.wait()


def window(branch, limits, tokens, own, halo, modulation, wqkv, rows, cols, after):
    count, width = tokens.shape
    places = jnp.asarray(halo_places(rows, cols))
    halo_count = places.shape[1]
    half = (count // 2, width)
    return pl.pallas_call(
        functools.partial(window_kernel, rows, cols, len(halo)),
        in_specs=[SMEM, SMEM, VMEM, HBM, HBM] + [HBM] * len(halo) + [VMEM, HBM] + [HBM] * len(after),
        out_specs=[HBM, HBM],
        out_shape=[jax.ShapeDtypeStruct((2,) + half, BF16), jax.ShapeDtypeStruct(half, BF16)],
        scratch_shapes=[
            pltpu.VMEM(half, BF16),
            pltpu.VMEM((halo_count, width), BF16),
            pltpu.VMEM((halo_count, width), BF16),
            pltpu.VMEM((halo_count, 2 * width), BF16),
            pltpu.VMEM((count, 3 * width), BF16),
            pltpu.VMEM((count, width), BF16),
        ]
        + weight_scratch(width, 2 * width)
        + [pltpu.SemaphoreType.DMA((len(halo) + 5,))],
        compiler_params=pltpu.CompilerParams(vmem_limit_bytes=VMEM_LIMIT),
        cost_estimate=pl.CostEstimate(
            flops=4 * count * (count + halo_count) * width * 3 + 4 * halo_count * width * width,
            bytes_accessed=2 * (4 * count * width + 2 * halo_count * width + 2 * width * width),
            transcendentals=count * (count + halo_count) * HEADS,
        ),
        name="window",
    )(branch, limits, places, tokens, own, *halo, modulation, wqkv, *after)


def finish_kernel(coefficients, mine, window_theirs, tokens_theirs, dilated, blend, gate, weights, out):
    weight = blend[...]

    def branches(index, theirs):
        return coefficients[0] * mine[index].astype(F32) + coefficients[1] * theirs[...].astype(F32)

    mixed = (weight * branches(0, window_theirs) + (1.0 - weight) * dilated[...].astype(F32)).astype(BF16)
    projected = jnp.dot(mixed, weights[...], preferred_element_type=F32)
    out[...] = (branches(1, tokens_theirs) + gate[...] * projected).astype(BF16)


def finish(coefficients, mine, window_theirs, tokens_theirs, dilated, blend, gate, w_out):
    count, width = dilated.shape
    return pl.pallas_call(
        finish_kernel,
        in_specs=[SMEM] + [VMEM] * 7,
        out_specs=VMEM,
        out_shape=jax.ShapeDtypeStruct((count, width), BF16),
        compiler_params=pltpu.CompilerParams(vmem_limit_bytes=SMALL_LIMIT),
        cost_estimate=pl.CostEstimate(
            flops=2 * count * width * width,
            bytes_accessed=2 * (width * width + 6 * count * width),
            transcendentals=0,
        ),
        name="finish",
    )(coefficients, mine, window_theirs, tokens_theirs, dilated, blend, gate, w_out)


def window_limits(reach):
    row, col = lax.axis_index("row"), lax.axis_index("col")
    last_row, last_col = lax.axis_size("row") - 1, lax.axis_size("col") - 1
    inner = jnp.stack([row > 0, row < last_row, col > 0, col < last_col])
    return jnp.where(inner, reach.reshape(4), 0)


def shift(cells, axis, forward):
    count = lax.axis_size(axis)
    if forward:
        pairs = [(i, i + 1) for i in range(count - 1)]
    else:
        pairs = [(i + 1, i) for i in range(count - 1)]
    return lax.ppermute(cells, axis, pairs)


def swap_pairs(cells):
    return lax.ppermute(cells, "col", [(i, i ^ 1) for i in range(lax.axis_size("col"))])


def halo_tokens(tile, pair_side, other_strip):
    rows, cols, width = tile.shape
    row_groups, col_groups = lax.axis_size("row"), lax.axis_size("col")
    square = HALO * HALO

    def beyond(col):
        return col + 1 if col % 2 else col - 1

    def diagonal(cells, down):
        pairs = [
            (row * col_groups + col, (row + down) * col_groups + beyond(col))
            for row in range(row_groups)
            for col in range(col_groups)
            if 0 <= row + down < row_groups and 0 <= beyond(col) < col_groups
        ]
        return lax.ppermute(cells, ("row", "col"), pairs)

    lower = jnp.concatenate([tile[rows - HALO :].reshape(HALO * cols, width), pair_side[-square:]], axis=0)
    upper = jnp.concatenate([tile[:HALO].reshape(HALO * cols, width), pair_side[:square]], axis=0)
    across = [(i, beyond(i)) for i in range(col_groups) if 0 <= beyond(i) < col_groups]
    above = shift(lower, "row", True)
    below = shift(upper, "row", False)
    other_side = lax.ppermute(other_strip, "col", across)
    return above, below, pair_side, other_side, diagonal(other_strip[-square:], 1), diagonal(other_strip[:square], -1)


def on_device(tokens, modulation, wqkv, w_out, blend, reach):
    tile = tokens[0]
    rows, cols, width = tile.shape
    row_groups = lax.axis_size("row")
    col_groups = lax.axis_size("col")
    sub_rows = rows // row_groups
    sub_cols = cols // col_groups
    half = rows // 2 * cols
    branch = lax.axis_index("branch")
    devices = row_groups * col_groups
    coefficients = jnp.stack(
        [
            jnp.where(branch == 1, GUIDANCE, 1.0 - GUIDANCE),
            jnp.where(branch == 1, 1.0 - GUIDANCE, GUIDANCE),
        ]
    ).astype(F32)

    place_of = jnp.stack([branch, lax.axis_index("col") % 2]).astype(jnp.int32)

    def other_core(cells):
        return lax.ppermute(cells, "branch", [(0, 1), (1, 0)])

    outgoing = tile.reshape(sub_rows, row_groups, sub_cols, col_groups, width)
    outgoing = outgoing.transpose(1, 3, 0, 2, 4).reshape(devices, sub_rows * sub_cols, width)
    pair_strip, other_strip = strips(place_of, tile)
    pair_side = swap_pairs(pair_strip)
    outgoing = hold(outgoing, pair_side)
    arrived = lax.all_to_all(outgoing, ("row", "col"), split_axis=0, concat_axis=0, tiled=True)

    flat = tile.reshape(rows * cols, width)
    halo = halo_tokens(tile, pair_side, other_strip)
    own, tokens_send, mark = own_tile(place_of, flat, modulation, wqkv)
    tokens_theirs = other_core(tokens_send)

    arrived = arrived.reshape(devices, sub_rows, sub_cols, width).transpose(1, 0, 2, 3)
    arrived = arrived.reshape(rows * cols, width)
    lattice_out = lattice(arrived, modulation, wqkv, [mark])
    lattice_theirs = other_core(other_half(place_of, lattice_out, halo[:2] + halo[3:]))
    combined = combine(coefficients, place_of, lattice_out, lattice_theirs)
    combined = combined.reshape(devices, sub_cols, width)
    returned = lax.all_to_all(combined, ("row", "col"), split_axis=0, concat_axis=0, tiled=True)

    limits = window_limits(reach)
    mine, send = window(
        place_of, limits, flat, own, halo, modulation, wqkv, rows, cols, [combined]
    )
    window_theirs = other_core(send)
    returned = returned.reshape(row_groups, col_groups, sub_cols, width).transpose(0, 2, 1, 3)
    dilated = returned.reshape(half, width)

    weight = lax.dynamic_index_in_dim(blend.reshape(2, half, 1), branch, 0, keepdims=False)
    guided = finish(
        coefficients, mine, window_theirs, tokens_theirs, dilated, weight, modulation[2:3], w_out
    )
    return guided.reshape(rows // 2, cols, width)


def solution(mesh):
    in_specs = (
        P("branch", "row", "col", None),
        P(),
        P(),
        P(),
        P("row", "col"),
        P(None, "row", "col"),
    )
    out_specs = P(("row", "branch"), "col", None)
    return jax.shard_map(
        on_device, mesh=mesh, in_specs=in_specs, out_specs=out_specs, check_vma=False
    )
```

```python
import functools
import math

import jax
import jax.numpy as jnp
import numpy as np
from jax import lax
from jax.experimental import pallas as pl
from jax.experimental.pallas import tpu as pltpu
from jax.sharding import PartitionSpec as P

HEADS = 16
HALO = 4
GUIDANCE = 4.5
LANES = 128
VMEM_LIMIT = 24 * 1024 * 1024
SMALL_LIMIT = 4 * 1024 * 1024
FINISH_LIMIT = 16 * 1024 * 1024
CHUNK = 768
IN_FLIGHT = 3

F32 = jnp.float32
BF16 = jnp.bfloat16

VMEM = pl.BlockSpec(memory_space=pltpu.VMEM)
SMEM = pl.BlockSpec(memory_space=pltpu.SMEM)
ANY = pl.BlockSpec(memory_space=pl.ANY)
HBM = pl.BlockSpec(memory_space=pltpu.HBM)
MARK = jax.ShapeDtypeStruct((8, LANES), F32)


def in_hbm(array):
    return pltpu.with_memory_space_constraint(array, pltpu.HBM)


def normalise(tokens, modulation):
    widened = tokens.astype(F32)
    centered = widened - jnp.mean(widened, axis=-1, keepdims=True)
    variance = jnp.mean(centered * centered, axis=-1, keepdims=True)
    scaled = centered * lax.rsqrt(variance + 1e-06)
    return (scaled * (1.0 + modulation[1:2]) + modulation[0:1]).astype(BF16)


def head_window(head, head_size, width):
    first = head * head_size
    low = first // LANES * LANES
    high = min(-(-(first + head_size) // LANES) * LANES, width)
    return first, low, high


def attend_head(head, queries, pairs, out):
    width = queries.shape[-1]
    head_size = width // HEADS
    first, low, high = head_window(head, head_size, width)
    lane = lax.broadcasted_iota(jnp.int32, (1, high - low), 1) + low
    inside = (lane >= first) & (lane < first + head_size)
    outside_lane = 0 if first > low else head_size
    query = queries[:, low:high]
    query = jnp.where(inside, query, jnp.zeros_like(query))
    scores = []
    for keys, values, bias in pairs:
        score = lax.dot_general(
            query, keys[:, low:high], (((1,), (1,)), ((), ())), preferred_element_type=F32
        )
        scores.append(score if bias is None else score + bias)
    top = functools.reduce(
        jnp.maximum, [jnp.max(score, axis=-1, keepdims=True) for score in scores]
    )
    total = None
    for score, (keys, values, bias) in zip(scores, pairs):
        powers = jnp.exp2(score - top).astype(BF16)
        value = values[:, low:high]
        value = jnp.where(inside, value, jnp.ones_like(value))
        part = jnp.dot(powers, value, preferred_element_type=F32)
        total = part if total is None else total + part
    attended = total * (1.0 / total[:, outside_lane : outside_lane + 1])
    attended = attended.astype(out.dtype)
    out[:, low:high] = jnp.where(inside, attended, out[:, low:high])


def attend_all(queries, pairs, out):
    out[...] = jnp.zeros_like(out)
    for head in range(HEADS):
        attend_head(head, queries, pairs, out)


def query_scale(feature_width):
    return math.log2(math.e) / math.sqrt(feature_width // HEADS)


def column_chunks(width):
    return [(start, min(CHUNK, width - start)) for start in range(0, width, CHUNK)]


def stream_project(normed, weights, first_column, buffer, sems, out, sends=()):
    width = normed.shape[-1]
    chunks = column_chunks(out.shape[-1])
    copies = [
        pltpu.make_async_copy(
            weights.at[:, first_column + start : first_column + start + size],
            buffer.at[:, start : start + size],
            sems.at[index],
        )
        for index, (start, size) in enumerate(chunks)
    ]
    for copy in copies[:IN_FLIGHT]:
        copy.start()

    def multiply():
        for index, (start, size) in enumerate(chunks):
            copies[index].wait()
            if index + IN_FLIGHT < len(chunks):
                copies[index + IN_FLIGHT].start()
            product = jnp.dot(normed[...], buffer[:, start : start + size], preferred_element_type=F32)
            if first_column + start < width:
                column = lax.broadcasted_iota(jnp.int32, (1, size), 1) + first_column + start
                product = product * jnp.where(column < width, query_scale(width), 1.0)
            out[:, start : start + size] = product.astype(BF16)
            if sends:
                sends[index].start()

    return multiply


def weight_scratch(width, columns):
    return [pltpu.VMEM((width, columns), BF16), pltpu.SemaphoreType.DMA((len(column_chunks(columns)),))]


def split_heads(qkv, width):
    return [qkv.at[:, start : start + width] for start in range(0, qkv.shape[-1], width)]


def strips_kernel(tile, left, right, first, last, sems):
    rows, cols, _ = tile.shape
    wide = 2 * HALO
    copies = [
        pltpu.make_async_copy(tile.at[:, :wide], first, sems.at[0]),
        pltpu.make_async_copy(tile.at[:, cols - wide :], last, sems.at[1]),
    ]
    for copy in copies:
        copy.start()
    upper = lax.broadcasted_iota(jnp.int32, (wide, 1), 0) < HALO
    for copy in copies:
        copy.wait()
    for pair in range(rows // 2):
        place = slice(wide * pair, wide * (pair + 1))
        one, two = first[2 * pair].astype(F32), first[2 * pair + 1].astype(F32)
        left[place] = jnp.where(upper, one, pltpu.roll(two, HALO, 0)).astype(BF16)
        one, two = last[2 * pair].astype(F32), last[2 * pair + 1].astype(F32)
        right[place] = jnp.where(upper, pltpu.roll(one, HALO, 0), two).astype(BF16)


def strips(tile):
    rows, cols, width = tile.shape
    shape = jax.ShapeDtypeStruct((rows * HALO, width), BF16)
    return pl.pallas_call(
        strips_kernel,
        in_specs=[HBM],
        out_specs=[VMEM, VMEM],
        out_shape=[shape, shape],
        scratch_shapes=[pltpu.VMEM((rows, 2 * HALO, width), BF16)] * 2 + [pltpu.SemaphoreType.DMA((2,))],
        compiler_params=pltpu.CompilerParams(vmem_limit_bytes=SMALL_LIMIT),
        cost_estimate=pl.CostEstimate(flops=0, bytes_accessed=8 * rows * HALO * width, transcendentals=0),
        name="strips",
    )(tile)


def hold_kernel(cells, *refs):
    pass


def hold(cells, after):
    return pl.pallas_call(
        hold_kernel,
        in_specs=[ANY] * (1 + len(after)),
        out_specs=ANY,
        out_shape=jax.ShapeDtypeStruct(cells.shape, cells.dtype),
        input_output_aliases={0: 0},
        compiler_params=pltpu.CompilerParams(vmem_limit_bytes=SMALL_LIMIT),
        name="hold",
    )(cells, *after)


def own_kernel(half, branch, tokens, modulation, weights, *refs):
    own, tokens_send, mark, here, normed, qkv, buffer, sems, own_sems, copy_sems = refs
    arrival = pltpu.make_async_copy(tokens, here, copy_sems.at[0])
    arrival.start()
    sends = [
        pltpu.make_async_copy(
            qkv.at[:, start : start + size], own.at[:, start : start + size], own_sems.at[index]
        )
        for index, (start, size) in enumerate(column_chunks(qkv.shape[-1]))
    ]
    multiply = stream_project(normed, weights, 0, buffer, sems, qkv, sends)
    mark[...] = jnp.zeros_like(mark)
    arrival.wait()
    other = pl.ds(pl.multiple_of((1 - branch[0]) * half, half), half)
    sends.append(pltpu.make_async_copy(here.at[other], tokens_send, copy_sems.at[1]))
    sends[-1].start()
    normed[...] = normalise(here[...], modulation[...])
    multiply()
    for copy in sends:
        copy.wait()


def own_tile(branch, tokens, modulation, wqkv):
    count, width = tokens.shape
    columns = wqkv.shape[1]
    half = count // 2
    return pl.pallas_call(
        functools.partial(own_kernel, half),
        in_specs=[SMEM, HBM, VMEM, HBM],
        out_specs=[HBM, HBM, VMEM],
        out_shape=[
            pltpu.HBM((count, columns), BF16),
            pltpu.HBM((half, width), BF16),
            MARK,
        ],
        scratch_shapes=[
            pltpu.VMEM((count, width), BF16),
            pltpu.VMEM((count, width), BF16),
            pltpu.VMEM((count, columns), BF16),
        ]
        + weight_scratch(width, columns)
        + [pltpu.SemaphoreType.DMA((len(column_chunks(columns)),)), pltpu.SemaphoreType.DMA((2,))],
        compiler_params=pltpu.CompilerParams(vmem_limit_bytes=VMEM_LIMIT),
        cost_estimate=pl.CostEstimate(
            flops=2 * count * width * columns,
            bytes_accessed=2 * (width * columns + count * (columns + 2 * width)),
            transcendentals=count,
        ),
        name="own_tile",
    )(branch, tokens, modulation, wqkv)


def lattice_kernel(tokens, modulation, weights, *refs):
    whole, normed, qkv, buffer, sems = refs[-5:]
    multiply = stream_project(normed, weights, 0, buffer, sems, qkv)
    normed[...] = normalise(tokens[...], modulation[...])
    multiply()
    queries, keys, values = split_heads(qkv, tokens.shape[1])
    attend_all(queries, [(keys, values, None)], whole)


def lattice(tokens, modulation, wqkv, after):
    count, width = tokens.shape
    columns = wqkv.shape[1]
    return pl.pallas_call(
        lattice_kernel,
        in_specs=[VMEM, VMEM, HBM] + [ANY] * len(after),
        out_specs=VMEM,
        out_shape=jax.ShapeDtypeStruct((count, width), BF16),
        scratch_shapes=[pltpu.VMEM((count, width), BF16), pltpu.VMEM((count, columns), BF16)]
        + weight_scratch(width, columns),
        compiler_params=pltpu.CompilerParams(vmem_limit_bytes=VMEM_LIMIT),
        cost_estimate=pl.CostEstimate(
            flops=2 * count * width * columns + 4 * count * count * width * 3,
            bytes_accessed=2 * (width * columns + 2 * count * width),
            transcendentals=count * count * HEADS,
        ),
        name="lattice",
    )(tokens, modulation, wqkv, *after)


def other_half_kernel(branch, whole, *refs):
    theirs = refs[-1]
    half = theirs.shape[0]
    theirs[...] = whole[pl.ds(pl.multiple_of((1 - branch[0]) * half, half), half)]


def other_half(branch, whole, after):
    half = (whole.shape[0] // 2, whole.shape[1])
    return pl.pallas_call(
        other_half_kernel,
        in_specs=[SMEM, VMEM] + [HBM] * len(after),
        out_specs=VMEM,
        out_shape=jax.ShapeDtypeStruct(half, BF16),
        compiler_params=pltpu.CompilerParams(vmem_limit_bytes=SMALL_LIMIT),
        cost_estimate=pl.CostEstimate(flops=0, bytes_accessed=2 * whole.size, transcendentals=0),
        name="other_half",
    )(branch, whole, *after)


def guidance(branch):
    conditional = branch[0] == 1
    return jnp.where(conditional, GUIDANCE, 1.0 - GUIDANCE), jnp.where(conditional, 1.0 - GUIDANCE, GUIDANCE)


def combine_kernel(branch, whole, theirs, out):
    own_factor, other_factor = guidance(branch)
    half = theirs.shape[0]
    mine = whole[pl.ds(pl.multiple_of(branch[0] * half, half), half)]
    both = own_factor * mine.astype(F32) + other_factor * theirs[...].astype(F32)
    out[...] = both.astype(BF16)


def combine(branch, whole, theirs):
    return pl.pallas_call(
        combine_kernel,
        in_specs=[SMEM, VMEM, VMEM],
        out_specs=VMEM,
        out_shape=jax.ShapeDtypeStruct(theirs.shape, BF16),
        compiler_params=pltpu.CompilerParams(vmem_limit_bytes=SMALL_LIMIT),
        cost_estimate=pl.CostEstimate(flops=3 * theirs.size, bytes_accessed=6 * theirs.size, transcendentals=0),
        name="combine",
    )(branch, whole, theirs)


def halo_places(rows, cols):
    def block(first_row, height, first_col, breadth):
        row, col = np.mgrid[first_row : first_row + height, first_col : first_col + breadth]
        return np.stack([row.reshape(-1), col.reshape(-1)])

    blocks = []
    for first_row in (-HALO, rows):
        blocks += [block(first_row, HALO, 0, cols), block(first_row, HALO, -HALO, HALO)]
        blocks += [block(first_row, HALO, cols, HALO)]
    blocks += [block(0, rows, -HALO, HALO), block(0, rows, cols, HALO)]
    return np.concatenate(blocks, axis=1).astype(np.int32)


def window_kernel(rows, cols, parts, branch, reach, places, tokens, own, *refs):
    halo, (modulation, weights) = refs[:parts], refs[parts : parts + 2]
    mine, theirs, here, gathered, normed, halo_kv, qkv, whole, buffer, sems, copy_sems = refs[-11:]
    half, width = theirs.shape
    first = pl.ds(pl.multiple_of(branch[0] * half, half), half)
    second = pl.ds(pl.multiple_of((1 - branch[0]) * half, half), half)
    arrivals = []
    start = 0
    for index, part in enumerate(halo):
        place = gathered.at[start : start + part.shape[0]]
        arrivals.append(pltpu.make_async_copy(part, place, copy_sems.at[index]))
        arrivals[-1].start()
        start += part.shape[0]
    multiply = stream_project(normed, weights, width, buffer, sems, halo_kv)
    own_copy = pltpu.make_async_copy(own, qkv, copy_sems.at[parts])
    tokens_copy = pltpu.make_async_copy(tokens.at[first], here, copy_sems.at[parts + 1])
    sends = [
        pltpu.make_async_copy(here, mine.at[1], copy_sems.at[parts + 2]),
        pltpu.make_async_copy(whole.at[first], mine.at[0], copy_sems.at[parts + 3]),
        pltpu.make_async_copy(whole.at[second], theirs, copy_sems.at[parts + 4]),
    ]
    own_copy.start()
    tokens_copy.start()
    row, col = places[0:1], places[1:2]
    limits = [jnp.where(branch[1 + side] != 0, reach[side], 0) for side in range(4)]
    allowed = (row >= -limits[0]) & (row < rows + limits[1])
    allowed = allowed & (col >= -limits[2]) & (col < cols + limits[3])
    bias = jnp.where(allowed, 0.0, -1e30).astype(F32)
    for copy in arrivals:
        copy.wait()
    normed[...] = normalise(gathered[...], modulation[...])
    multiply()
    own_copy.wait()
    tokens_copy.wait()
    sends[0].start()
    queries, keys, values = split_heads(qkv, width)
    halo_keys, halo_values = split_heads(halo_kv, width)
    attend_all(queries, [(keys, values, None), (halo_keys, halo_values, bias)], whole)
    for copy in sends[1:]:
        copy.start()
    for copy in sends:
        copy.wait()


def window(branch, reach, tokens, own, halo, modulation, wqkv, rows, cols, after):
    count, width = tokens.shape
    places = jnp.asarray(halo_places(rows, cols))
    halo_count = places.shape[1]
    half = (count // 2, width)
    return pl.pallas_call(
        functools.partial(window_kernel, rows, cols, len(halo)),
        in_specs=[SMEM, SMEM, VMEM, HBM, HBM] + [HBM] * len(halo) + [VMEM, HBM] + [HBM] * len(after),
        out_specs=[HBM, HBM],
        out_shape=[pltpu.HBM((2,) + half, BF16), pltpu.HBM(half, BF16)],
        scratch_shapes=[
            pltpu.VMEM(half, BF16),
            pltpu.VMEM((halo_count, width), BF16),
            pltpu.VMEM((halo_count, width), BF16),
            pltpu.VMEM((halo_count, 2 * width), BF16),
            pltpu.VMEM((count, 3 * width), BF16),
            pltpu.VMEM((count, width), BF16),
        ]
        + weight_scratch(width, 2 * width)
        + [pltpu.SemaphoreType.DMA((len(halo) + 5,))],
        compiler_params=pltpu.CompilerParams(vmem_limit_bytes=VMEM_LIMIT),
        cost_estimate=pl.CostEstimate(
            flops=4 * count * (count + halo_count) * width * 3 + 4 * halo_count * width * width,
            bytes_accessed=2 * (4 * count * width + 2 * halo_count * width + 2 * width * width),
            transcendentals=count * (count + halo_count) * HEADS,
        ),
        name="window",
    )(branch, reach, places, tokens, in_hbm(own), *[in_hbm(part) for part in halo], modulation, wqkv, *after)


def finish_kernel(branch, mine, window_theirs, tokens_theirs, dilated, blend, gate, weights, out, buffer, sems):
    own_factor, other_factor = guidance(branch)
    size = buffer.shape[1] // 3
    columns = [slice(start, start + size) for start in range(0, buffer.shape[1], size)]
    copies = [
        pltpu.make_async_copy(weights.at[:, place], buffer.at[:, place], sems.at[index])
        for index, place in enumerate(columns)
    ]
    for copy in copies:
        copy.start()
    weight = blend[...]
    both = own_factor * mine[0].astype(F32) + other_factor * window_theirs[...].astype(F32)
    mixed = (weight * both + (1.0 - weight) * dilated[...].astype(F32)).astype(BF16)
    for copy, place in zip(copies, columns):
        copy.wait()
        projected = jnp.dot(mixed, buffer[:, place], preferred_element_type=F32)
        kept = own_factor * mine[1, :, place].astype(F32) + other_factor * tokens_theirs[:, place].astype(F32)
        out[:, place] = (kept + gate[:, place] * projected).astype(BF16)


def finish(branch, mine, window_theirs, tokens_theirs, dilated, blend, gate, w_out):
    count, width = dilated.shape
    return pl.pallas_call(
        finish_kernel,
        in_specs=[SMEM] + [VMEM] * 6 + [HBM],
        out_specs=VMEM,
        out_shape=jax.ShapeDtypeStruct((count, width), BF16),
        scratch_shapes=[pltpu.VMEM((width, width), BF16), pltpu.SemaphoreType.DMA((3,))],
        compiler_params=pltpu.CompilerParams(vmem_limit_bytes=FINISH_LIMIT),
        cost_estimate=pl.CostEstimate(
            flops=2 * count * width * width,
            bytes_accessed=2 * (width * width + 6 * count * width),
            transcendentals=0,
        ),
        name="finish",
    )(branch, mine, window_theirs, tokens_theirs, dilated, blend, gate, w_out)


def shift(cells, axis, forward):
    count = lax.axis_size(axis)
    if forward:
        pairs = [(i, i + 1) for i in range(count - 1)]
    else:
        pairs = [(i + 1, i) for i in range(count - 1)]
    return lax.ppermute(cells, axis, pairs)


def halo_rows(tile, left, right):
    rows, cols, width = tile.shape
    square = HALO * HALO
    lower = [tile[rows - HALO :].reshape(HALO * cols, width), left[-square:], right[-square:]]
    upper = [tile[:HALO].reshape(HALO * cols, width), left[:square], right[:square]]
    above = shift(jnp.concatenate(lower, axis=0), "row", True)
    below = shift(jnp.concatenate(upper, axis=0), "row", False)
    return above, below


def on_device(tokens, modulation, wqkv, w_out, blend, reach):
    tile = tokens[0]
    rows, cols, width = tile.shape
    row_groups = lax.axis_size("row")
    col_groups = lax.axis_size("col")
    sub_rows = rows // row_groups
    sub_cols = cols // col_groups
    half = rows // 2 * cols
    branch = lax.axis_index("branch")
    wqkv, w_out = in_hbm(wqkv), in_hbm(w_out)
    devices = row_groups * col_groups
    row, col = lax.axis_index("row"), lax.axis_index("col")
    inner = [row > 0, row < row_groups - 1, col > 0, col < col_groups - 1]
    place_of = jnp.stack([branch] + [side.astype(branch.dtype) for side in inner]).astype(jnp.int32)

    def other_core(cells):
        return lax.ppermute(cells, "branch", [(0, 1), (1, 0)])

    outgoing = tile.reshape(sub_rows, row_groups, sub_cols, col_groups, width)
    outgoing = outgoing.transpose(1, 3, 0, 2, 4).reshape(devices, sub_rows * sub_cols, width)
    left_strip, right_strip = strips(in_hbm(tile))
    left = shift(right_strip, "col", True)
    right = shift(left_strip, "col", False)
    outgoing = hold(outgoing, [left, right])
    arrived = lax.all_to_all(outgoing, ("row", "col"), split_axis=0, concat_axis=0, tiled=True)

    flat = tile.reshape(rows * cols, width)
    above, below = halo_rows(tile, left, right)
    own, tokens_send, mark = own_tile(place_of, flat, modulation, wqkv)
    tokens_theirs = other_core(tokens_send)

    arrived = arrived.reshape(devices, sub_rows, sub_cols, width).transpose(1, 0, 2, 3)
    arrived = arrived.reshape(rows * cols, width)
    lattice_out = lattice(arrived, modulation, wqkv, [mark])
    lattice_theirs = other_core(other_half(place_of, lattice_out, [above, below]))
    combined = combine(place_of, lattice_out, lattice_theirs)
    combined = combined.reshape(devices, sub_cols, width)
    returned = lax.all_to_all(combined, ("row", "col"), split_axis=0, concat_axis=0, tiled=True)

    mine, send = window(
        place_of, reach.reshape(4), flat, own, [above, below, left, right], modulation, wqkv, rows, cols, [combined]
    )
    window_theirs = other_core(send)
    returned = returned.reshape(row_groups, col_groups, sub_cols, width).transpose(0, 2, 1, 3)
    dilated = returned.reshape(half, width)

    weight = lax.dynamic_index_in_dim(blend.reshape(2, half, 1), branch, 0, keepdims=False)
    guided = finish(
        place_of, mine, window_theirs, tokens_theirs, dilated, weight, modulation[2:3], w_out
    )
    return guided.reshape(rows // 2, cols, width)


def solution(mesh):
    in_specs = (
        P("branch", "row", "col", None),
        P(),
        P(),
        P(),
        P("row", "col"),
        P(None, "row", "col"),
    )
    out_specs = P(("row", "branch"), "col", None)
    return jax.shard_map(
        on_device, mesh=mesh, in_specs=in_specs, out_specs=out_specs, check_vma=False
    )
```

```python
import functools
import math

import jax
import jax.numpy as jnp
import numpy as np
from jax import lax
from jax.experimental import pallas as pl
from jax.experimental.pallas import tpu as pltpu
from jax.sharding import PartitionSpec as P

HEADS = 16
HALO = 4
GUIDANCE = 4.5
LANES = 128
VMEM_LIMIT = 28 * 1024 * 1024
SMALL_LIMIT = 4 * 1024 * 1024
FINISH_LIMIT = 16 * 1024 * 1024
CHUNK = 256
IN_FLIGHT = 3

F32 = jnp.float32
BF16 = jnp.bfloat16

VMEM = pl.BlockSpec(memory_space=pltpu.VMEM)
SMEM = pl.BlockSpec(memory_space=pltpu.SMEM)
ANY = pl.BlockSpec(memory_space=pl.ANY)
HBM = pl.BlockSpec(memory_space=pltpu.HBM)
MARK = jax.ShapeDtypeStruct((8, LANES), F32)


def in_hbm(array):
    return pltpu.with_memory_space_constraint(array, pltpu.HBM)


def normalise(tokens, modulation):
    widened = tokens.astype(F32)
    centered = widened - jnp.mean(widened, axis=-1, keepdims=True)
    variance = jnp.mean(centered * centered, axis=-1, keepdims=True)
    scaled = centered * lax.rsqrt(variance + 1e-06)
    return (scaled * (1.0 + modulation[1:2]) + modulation[0:1]).astype(BF16)


def head_window(head, head_size, width):
    first = head * head_size
    low = first // LANES * LANES
    high = min(-(-(first + head_size) // LANES) * LANES, width)
    return first, low, high


def head_lanes(head, width):
    head_size = width // HEADS
    first, low, high = head_window(head, head_size, width)
    lane = lax.broadcasted_iota(jnp.int32, (1, high - low), 1) + low
    inside = (lane >= first) & (lane < first + head_size)
    return slice(low, high), inside, 0 if first > low else head_size


def head_scores(place, inside, queries, keys):
    query = queries[:, place]
    query = jnp.where(inside, query, jnp.zeros_like(query))
    return lax.dot_general(query, keys[:, place], (((1,), (1,)), ((), ())), preferred_element_type=F32)


def weigh_values(place, inside, scores, top, values):
    powers = jnp.exp2(scores - top).astype(BF16)
    value = values[:, place]
    value = jnp.where(inside, value, jnp.ones_like(value))
    return jnp.dot(powers, value, preferred_element_type=F32)


def attend(queries, keys, values, out):
    width = queries.shape[-1]
    for head in range(HEADS):
        place, inside, spare = head_lanes(head, width)
        scores = head_scores(place, inside, queries, keys)
        top = jnp.max(scores, axis=-1, keepdims=True)
        total = weigh_values(place, inside, scores, top, values)
        attended = (total * (1.0 / total[:, spare : spare + 1])).astype(out.dtype)
        out[:, place] = jnp.where(inside, attended, out[:, place])


def attend_part(queries, keys, values, sums, stats):
    width = queries.shape[-1]
    column = lax.broadcasted_iota(jnp.int32, (1, stats.shape[-1]), 1)
    for head in range(HEADS):
        place, inside, spare = head_lanes(head, width)
        scores = head_scores(place, inside, queries, keys)
        top = jnp.max(scores, axis=-1, keepdims=True)
        total = weigh_values(place, inside, scores, top, values)
        sums[:, place] = jnp.where(inside, total, sums[:, place])
        entry = jnp.where(column == HEADS + head, total[:, spare : spare + 1], stats[...])
        stats[...] = jnp.where(column == head, top, entry)


def attend_rest(queries, keys, values, bias, sums, stats, out):
    width = queries.shape[-1]
    for head in range(HEADS):
        place, inside, spare = head_lanes(head, width)
        scores = head_scores(place, inside, queries, keys) + bias
        before = stats[:, head : head + 1]
        top = jnp.maximum(before, jnp.max(scores, axis=-1, keepdims=True))
        total = weigh_values(place, inside, scores, top, values)
        kept = jnp.exp2(before - top)
        weight = stats[:, HEADS + head : HEADS + head + 1] * kept + total[:, spare : spare + 1]
        attended = ((sums[:, place] * kept + total) * (1.0 / weight)).astype(out.dtype)
        out[:, place] = jnp.where(inside, attended, out[:, place])


def query_scale(feature_width):
    return math.log2(math.e) / math.sqrt(feature_width // HEADS)


def column_chunks(width):
    return [(start, min(CHUNK, width - start)) for start in range(0, width, CHUNK)]


def stream_project(normed, weights, first_column, buffer, sems, out, sends=()):
    width = normed.shape[-1]
    chunks = column_chunks(out.shape[-1])
    copies = [
        pltpu.make_async_copy(
            weights.at[:, first_column + start : first_column + start + size],
            buffer.at[:, start : start + size],
            sems.at[index],
        )
        for index, (start, size) in enumerate(chunks)
    ]
    for copy in copies[:IN_FLIGHT]:
        copy.start()

    def multiply():
        for index, (start, size) in enumerate(chunks):
            copies[index].wait()
            if index + IN_FLIGHT < len(chunks):
                copies[index + IN_FLIGHT].start()
            product = jnp.dot(normed[...], buffer[:, start : start + size], preferred_element_type=F32)
            if first_column + start < width:
                column = lax.broadcasted_iota(jnp.int32, (1, size), 1) + first_column + start
                product = product * jnp.where(column < width, query_scale(width), 1.0)
            out[:, start : start + size] = product.astype(BF16)
            if sends:
                sends[index].start()

    return multiply


def weight_scratch(width, columns):
    return [pltpu.VMEM((width, columns), BF16), pltpu.SemaphoreType.DMA((len(column_chunks(columns)),))]


def split_heads(qkv, width):
    return [qkv.at[:, start : start + width] for start in range(0, qkv.shape[-1], width)]


def arrange_kernel(tile, quarters, left, right, sems):
    _, height, breadth, _ = quarters.shape
    copies = []
    for down in range(2):
        for across in range(2):
            index = 2 * down + across
            source = tile.at[
                height * down : height * (down + 1), breadth * across : breadth * (across + 1)
            ]
            copies.append(pltpu.make_async_copy(source, quarters.at[index], sems.at[index]))
            copies[-1].start()
    wide = 2 * HALO
    upper = lax.broadcasted_iota(jnp.int32, (wide, 1), 0) < HALO
    for copy in copies:
        copy.wait()
    for pair in range(height):
        down, row = divmod(2 * pair, height)
        place = slice(wide * pair, wide * (pair + 1))
        one, two = [quarters[2 * down, row + k, :wide].astype(F32) for k in range(2)]
        left[place] = jnp.where(upper, one, pltpu.roll(two, HALO, 0)).astype(BF16)
        one, two = [quarters[2 * down + 1, row + k, breadth - wide :].astype(F32) for k in range(2)]
        right[place] = jnp.where(upper, pltpu.roll(one, HALO, 0), two).astype(BF16)


def arrange(tile):
    rows, cols, width = tile.shape
    strip = jax.ShapeDtypeStruct((rows * HALO, width), BF16)
    return pl.pallas_call(
        arrange_kernel,
        in_specs=[HBM],
        out_specs=[VMEM, VMEM, VMEM],
        out_shape=[jax.ShapeDtypeStruct((4, rows // 2, cols // 2, width), BF16), strip, strip],
        scratch_shapes=[pltpu.SemaphoreType.DMA((4,))],
        compiler_params=pltpu.CompilerParams(vmem_limit_bytes=SMALL_LIMIT),
        cost_estimate=pl.CostEstimate(flops=0, bytes_accessed=4 * rows * cols * width, transcendentals=0),
        name="arrange",
    )(tile)


def hold_kernel(cells, *refs):
    pass


def hold(cells, after):
    return pl.pallas_call(
        hold_kernel,
        in_specs=[ANY] * (1 + len(after)),
        out_specs=ANY,
        out_shape=jax.ShapeDtypeStruct(cells.shape, cells.dtype),
        input_output_aliases={0: 0},
        compiler_params=pltpu.CompilerParams(vmem_limit_bytes=SMALL_LIMIT),
        name="hold",
    )(cells, *after)


def own_kernel(half, branch, tokens, modulation, weights, *refs):
    queries_out, sums_out, stats_out, tokens_send, mark, here, normed, qkv, sums, stats, buffer, sems, copy_sems = refs
    arrival = pltpu.make_async_copy(tokens, here, copy_sems.at[0])
    arrival.start()
    multiply = stream_project(normed, weights, 0, buffer, sems, qkv)
    mark[...] = jnp.zeros_like(mark)
    stats[...] = jnp.zeros_like(stats)
    arrival.wait()
    queries, keys, values = split_heads(qkv, here.shape[1])
    other = pl.ds(pl.multiple_of((1 - branch[0]) * half, half), half)
    sends = [
        pltpu.make_async_copy(here.at[other], tokens_send, copy_sems.at[1]),
        pltpu.make_async_copy(queries, queries_out, copy_sems.at[2]),
        pltpu.make_async_copy(sums, sums_out, copy_sems.at[3]),
        pltpu.make_async_copy(stats, stats_out, copy_sems.at[4]),
    ]
    sends[0].start()
    normed[...] = normalise(here[...], modulation[...])
    multiply()
    sends[1].start()
    attend_part(queries, keys, values, sums, stats)
    sends[2].start()
    sends[3].start()
    for copy in sends:
        copy.wait()


def own_tile(branch, tokens, modulation, wqkv):
    count, width = tokens.shape
    columns = wqkv.shape[1]
    half = count // 2
    return pl.pallas_call(
        functools.partial(own_kernel, half),
        in_specs=[SMEM, HBM, VMEM, HBM],
        out_specs=[HBM, HBM, HBM, HBM, VMEM],
        out_shape=[
            pltpu.HBM((count, width), BF16),
            pltpu.HBM((count, width), F32),
            pltpu.HBM((count, LANES), F32),
            pltpu.HBM((half, width), BF16),
            MARK,
        ],
        scratch_shapes=[
            pltpu.VMEM((count, width), BF16),
            pltpu.VMEM((count, width), BF16),
            pltpu.VMEM((count, columns), BF16),
            pltpu.VMEM((count, width), F32),
            pltpu.VMEM((count, LANES), F32),
        ]
        + weight_scratch(width, columns)
        + [pltpu.SemaphoreType.DMA((5,))],
        compiler_params=pltpu.CompilerParams(vmem_limit_bytes=VMEM_LIMIT),
        cost_estimate=pl.CostEstimate(
            flops=2 * count * width * columns + 4 * count * count * width * 3,
            bytes_accessed=2 * (width * columns + 5 * count * width),
            transcendentals=count * count * HEADS,
        ),
        name="own_tile",
    )(branch, tokens, modulation, wqkv)


def lattice_kernel(tokens, modulation, weights, *refs):
    whole, normed, qkv, buffer, sems = refs[-5:]
    multiply = stream_project(normed, weights, 0, buffer, sems, qkv)
    normed[...] = normalise(tokens[...], modulation[...])
    multiply()
    queries, keys, values = split_heads(qkv, tokens.shape[1])
    attend(queries, keys, values, whole)


def lattice(tokens, modulation, wqkv, after):
    count, width = tokens.shape
    columns = wqkv.shape[1]
    return pl.pallas_call(
        lattice_kernel,
        in_specs=[VMEM, VMEM, HBM] + [ANY] * len(after),
        out_specs=VMEM,
        out_shape=jax.ShapeDtypeStruct((count, width), BF16),
        scratch_shapes=[pltpu.VMEM((count, width), BF16), pltpu.VMEM((count, columns), BF16)]
        + weight_scratch(width, columns),
        compiler_params=pltpu.CompilerParams(vmem_limit_bytes=VMEM_LIMIT),
        cost_estimate=pl.CostEstimate(
            flops=2 * count * width * columns + 4 * count * count * width * 3,
            bytes_accessed=2 * (width * columns + 2 * count * width),
            transcendentals=count * count * HEADS,
        ),
        name="lattice",
    )(tokens, modulation, wqkv, *after)


def other_half_kernel(branch, whole, *refs):
    theirs = refs[-1]
    half = theirs.shape[0]
    theirs[...] = whole[pl.ds(pl.multiple_of((1 - branch[0]) * half, half), half)]


def other_half(branch, whole, after):
    half = (whole.shape[0] // 2, whole.shape[1])
    return pl.pallas_call(
        other_half_kernel,
        in_specs=[SMEM, VMEM] + [HBM] * len(after),
        out_specs=VMEM,
        out_shape=jax.ShapeDtypeStruct(half, BF16),
        compiler_params=pltpu.CompilerParams(vmem_limit_bytes=SMALL_LIMIT),
        cost_estimate=pl.CostEstimate(flops=0, bytes_accessed=2 * whole.size, transcendentals=0),
        name="other_half",
    )(branch, whole, *after)


def guidance(branch):
    conditional = branch[0] == 1
    return jnp.where(conditional, GUIDANCE, 1.0 - GUIDANCE), jnp.where(conditional, 1.0 - GUIDANCE, GUIDANCE)


def combine_kernel(branch, whole, theirs, out):
    own_factor, other_factor = guidance(branch)
    half = theirs.shape[0]
    mine = whole[pl.ds(pl.multiple_of(branch[0] * half, half), half)]
    both = own_factor * mine.astype(F32) + other_factor * theirs[...].astype(F32)
    out[...] = both.astype(BF16)


def combine(branch, whole, theirs):
    return pl.pallas_call(
        combine_kernel,
        in_specs=[SMEM, VMEM, VMEM],
        out_specs=VMEM,
        out_shape=jax.ShapeDtypeStruct(theirs.shape, BF16),
        compiler_params=pltpu.CompilerParams(vmem_limit_bytes=SMALL_LIMIT),
        cost_estimate=pl.CostEstimate(flops=3 * theirs.size, bytes_accessed=6 * theirs.size, transcendentals=0),
        name="combine",
    )(branch, whole, theirs)


def halo_places(rows, cols):
    def block(first_row, height, first_col, breadth):
        row, col = np.mgrid[first_row : first_row + height, first_col : first_col + breadth]
        return np.stack([row.reshape(-1), col.reshape(-1)])

    blocks = []
    for first_row in (-HALO, rows):
        blocks += [block(first_row, HALO, 0, cols), block(first_row, HALO, -HALO, HALO)]
        blocks += [block(first_row, HALO, cols, HALO)]
    blocks += [block(0, rows, -HALO, HALO), block(0, rows, cols, HALO)]
    return np.concatenate(blocks, axis=1).astype(np.int32)


def window_kernel(rows, cols, parts, branch, reach, places, tokens, own_queries, own_sums, own_stats, *refs):
    halo, (modulation, weights) = refs[:parts], refs[parts : parts + 2]
    mine, theirs, here, gathered, normed, halo_kv, queries, sums, stats, whole, buffer, sems, copy_sems = refs[-13:]
    half, width = theirs.shape
    first = pl.ds(pl.multiple_of(branch[0] * half, half), half)
    second = pl.ds(pl.multiple_of((1 - branch[0]) * half, half), half)
    arrivals = []
    start = 0
    for index, part in enumerate(halo):
        place = gathered.at[start : start + part.shape[0]]
        arrivals.append(pltpu.make_async_copy(part, place, copy_sems.at[index]))
        arrivals[-1].start()
        start += part.shape[0]
    multiply = stream_project(normed, weights, width, buffer, sems, halo_kv)
    own_copies = [
        pltpu.make_async_copy(own_queries, queries, copy_sems.at[parts]),
        pltpu.make_async_copy(own_sums, sums, copy_sems.at[parts + 4]),
        pltpu.make_async_copy(own_stats, stats, copy_sems.at[parts + 5]),
        pltpu.make_async_copy(tokens.at[first], here, copy_sems.at[parts + 6]),
    ]
    sends = [
        pltpu.make_async_copy(here, mine.at[1], copy_sems.at[parts + 1]),
        pltpu.make_async_copy(whole.at[first], mine.at[0], copy_sems.at[parts + 2]),
        pltpu.make_async_copy(whole.at[second], theirs, copy_sems.at[parts + 3]),
    ]
    for copy in own_copies:
        copy.start()
    row, col = places[0:1], places[1:2]
    limits = [jnp.where(branch[1 + side] != 0, reach[side], 0) for side in range(4)]
    allowed = (row >= -limits[0]) & (row < rows + limits[1])
    allowed = allowed & (col >= -limits[2]) & (col < cols + limits[3])
    bias = jnp.where(allowed, 0.0, -1e30).astype(F32)
    for copy in arrivals:
        copy.wait()
    normed[...] = normalise(gathered[...], modulation[...])
    multiply()
    for copy in own_copies:
        copy.wait()
    sends[0].start()
    keys, values = split_heads(halo_kv, width)
    attend_rest(queries, keys, values, bias, sums, stats, whole)
    for copy in sends[1:]:
        copy.start()
    for copy in sends:
        copy.wait()


def window(branch, reach, tokens, own, halo, modulation, wqkv, rows, cols, after):
    count, width = tokens.shape
    places = jnp.asarray(halo_places(rows, cols))
    halo_count = places.shape[1]
    half = (count // 2, width)
    return pl.pallas_call(
        functools.partial(window_kernel, rows, cols, len(halo)),
        in_specs=[SMEM, SMEM, VMEM, HBM, HBM, HBM, HBM] + [HBM] * len(halo) + [VMEM, HBM] + [HBM] * len(after),
        out_specs=[HBM, HBM],
        out_shape=[pltpu.HBM((2,) + half, BF16), pltpu.HBM(half, BF16)],
        scratch_shapes=[
            pltpu.VMEM(half, BF16),
            pltpu.VMEM((halo_count, width), BF16),
            pltpu.VMEM((halo_count, width), BF16),
            pltpu.VMEM((halo_count, 2 * width), BF16),
            pltpu.VMEM((count, width), BF16),
            pltpu.VMEM((count, width), F32),
            pltpu.VMEM((count, LANES), F32),
            pltpu.VMEM((count, width), BF16),
        ]
        + weight_scratch(width, 2 * width)
        + [pltpu.SemaphoreType.DMA((len(halo) + 7,))],
        compiler_params=pltpu.CompilerParams(vmem_limit_bytes=VMEM_LIMIT),
        cost_estimate=pl.CostEstimate(
            flops=4 * count * halo_count * width * 3 + 4 * halo_count * width * width,
            bytes_accessed=2 * (4 * count * width + 2 * halo_count * width + 2 * width * width),
            transcendentals=count * halo_count * HEADS,
        ),
        name="window",
    )(branch, reach, places, tokens, *[in_hbm(part) for part in own], *[in_hbm(part) for part in halo], modulation, wqkv, *after)


def finish_kernel(branch, mine, window_theirs, tokens_theirs, dilated, blend, gate, weights, out, buffer, sems):
    own_factor, other_factor = guidance(branch)
    size = buffer.shape[1] // 3
    columns = [slice(start, start + size) for start in range(0, buffer.shape[1], size)]
    copies = [
        pltpu.make_async_copy(weights.at[:, place], buffer.at[:, place], sems.at[index])
        for index, place in enumerate(columns)
    ]
    for copy in copies:
        copy.start()
    weight = blend[...]
    both = own_factor * mine[0].astype(F32) + other_factor * window_theirs[...].astype(F32)
    mixed = (weight * both + (1.0 - weight) * dilated[...].astype(F32)).astype(BF16)
    for copy, place in zip(copies, columns):
        copy.wait()
        projected = jnp.dot(mixed, buffer[:, place], preferred_element_type=F32)
        kept = own_factor * mine[1, :, place].astype(F32) + other_factor * tokens_theirs[:, place].astype(F32)
        out[:, place] = (kept + gate[:, place] * projected).astype(BF16)


def finish(branch, mine, window_theirs, tokens_theirs, dilated, blend, gate, w_out):
    count, width = dilated.shape
    return pl.pallas_call(
        finish_kernel,
        in_specs=[SMEM] + [VMEM] * 6 + [HBM],
        out_specs=VMEM,
        out_shape=jax.ShapeDtypeStruct((count, width), BF16),
        scratch_shapes=[pltpu.VMEM((width, width), BF16), pltpu.SemaphoreType.DMA((3,))],
        compiler_params=pltpu.CompilerParams(vmem_limit_bytes=FINISH_LIMIT),
        cost_estimate=pl.CostEstimate(
            flops=2 * count * width * width,
            bytes_accessed=2 * (width * width + 6 * count * width),
            transcendentals=0,
        ),
        name="finish",
    )(branch, mine, window_theirs, tokens_theirs, dilated, blend, gate, w_out)


def shift(cells, axis, forward):
    count = lax.axis_size(axis)
    if forward:
        pairs = [(i, i + 1) for i in range(count - 1)]
    else:
        pairs = [(i + 1, i) for i in range(count - 1)]
    return lax.ppermute(cells, axis, pairs)


def halo_rows(tile, left, right):
    rows, cols, width = tile.shape
    square = HALO * HALO
    lower = [tile[rows - HALO :].reshape(HALO * cols, width), left[-square:], right[-square:]]
    upper = [tile[:HALO].reshape(HALO * cols, width), left[:square], right[:square]]
    above = shift(jnp.concatenate(lower, axis=0), "row", True)
    below = shift(jnp.concatenate(upper, axis=0), "row", False)
    return above, below


def on_device(tokens, modulation, wqkv, w_out, blend, reach):
    tile = tokens[0]
    rows, cols, width = tile.shape
    row_groups = lax.axis_size("row")
    col_groups = lax.axis_size("col")
    sub_rows = rows // row_groups
    sub_cols = cols // col_groups
    half = rows // 2 * cols
    branch = lax.axis_index("branch")
    wqkv, w_out = in_hbm(wqkv), in_hbm(w_out)
    devices = row_groups * col_groups
    row, col = lax.axis_index("row"), lax.axis_index("col")
    inner = [row > 0, row < row_groups - 1, col > 0, col < col_groups - 1]
    place_of = jnp.stack([branch] + [side.astype(branch.dtype) for side in inner]).astype(jnp.int32)

    def other_core(cells):
        return lax.ppermute(cells, "branch", [(0, 1), (1, 0)])

    quarters, left_strip, right_strip = arrange(in_hbm(tile))
    left = shift(right_strip, "col", True)
    right = shift(left_strip, "col", False)
    outgoing = quarters.reshape(sub_rows * sub_cols, devices, width).transpose(1, 0, 2)
    outgoing = hold(outgoing, [left, right])
    arrived = lax.all_to_all(outgoing, ("row", "col"), split_axis=0, concat_axis=0, tiled=True)

    flat = tile.reshape(rows * cols, width)
    above, below = halo_rows(tile, left, right)
    *own, tokens_send, mark = own_tile(place_of, flat, modulation, wqkv)
    tokens_theirs = other_core(tokens_send)

    arrived = arrived.transpose(1, 0, 2).reshape(rows * cols, width)
    lattice_out = lattice(arrived, modulation, wqkv, [mark])
    lattice_theirs = other_core(other_half(place_of, lattice_out, [above, below]))
    combined = combine(place_of, lattice_out, lattice_theirs)
    combined = combined.reshape(sub_cols, devices, width).transpose(1, 0, 2)
    returned = lax.all_to_all(combined, ("row", "col"), split_axis=0, concat_axis=0, tiled=True)

    mine, send = window(
        place_of, reach.reshape(4), flat, own, [above, below, left, right], modulation, wqkv, rows, cols, [combined]
    )
    window_theirs = other_core(send)
    returned = returned.reshape(row_groups, col_groups, sub_cols, width).transpose(0, 2, 1, 3)
    dilated = returned.reshape(half, width)

    weight = lax.dynamic_index_in_dim(blend.reshape(2, half, 1), branch, 0, keepdims=False)
    guided = finish(
        place_of, mine, window_theirs, tokens_theirs, dilated, weight, modulation[2:3], w_out
    )
    return guided.reshape(rows // 2, cols, width)


def solution(mesh):
    in_specs = (
        P("branch", "row", "col", None),
        P(),
        P(),
        P(),
        P("row", "col"),
        P(None, "row", "col"),
    )
    out_specs = P(("row", "branch"), "col", None)
    return jax.shard_map(
        on_device, mesh=mesh, in_specs=in_specs, out_specs=out_specs, check_vma=False
    )
```

```python
import functools
import math

import jax
import jax.numpy as jnp
import numpy as np
from jax import lax
from jax.experimental import pallas as pl
from jax.experimental.pallas import tpu as pltpu
from jax.sharding import PartitionSpec as P

HEADS = 16
HALO = 4
GUIDANCE = 4.5
LANES = 128
VMEM_LIMIT = 28 * 1024 * 1024
SMALL_LIMIT = 4 * 1024 * 1024
FINISH_LIMIT = 16 * 1024 * 1024
CHUNK = 512
IN_FLIGHT = 3

F32 = jnp.float32
BF16 = jnp.bfloat16

VMEM = pl.BlockSpec(memory_space=pltpu.VMEM)
SMEM = pl.BlockSpec(memory_space=pltpu.SMEM)
ANY = pl.BlockSpec(memory_space=pl.ANY)
HBM = pl.BlockSpec(memory_space=pltpu.HBM)
MARK = jax.ShapeDtypeStruct((8, LANES), F32)


def in_hbm(array):
    return pltpu.with_memory_space_constraint(array, pltpu.HBM)


def normalise(tokens, modulation):
    widened = tokens.astype(F32)
    centered = widened - jnp.mean(widened, axis=-1, keepdims=True)
    variance = jnp.mean(centered * centered, axis=-1, keepdims=True)
    scaled = centered * lax.rsqrt(variance + 1e-06)
    return (scaled * (1.0 + modulation[1:2]) + modulation[0:1]).astype(BF16)


def head_window(head, head_size, width):
    first = head * head_size
    low = first // LANES * LANES
    high = min(-(-(first + head_size) // LANES) * LANES, width)
    return first, low, high


def head_lanes(head, width):
    head_size = width // HEADS
    first, low, high = head_window(head, head_size, width)
    lane = lax.broadcasted_iota(jnp.int32, (1, high - low), 1) + low
    inside = (lane >= first) & (lane < first + head_size)
    return slice(low, high), inside, 0 if first > low else head_size


def head_scores(place, inside, queries, keys):
    query = queries[:, place]
    query = jnp.where(inside, query, jnp.zeros_like(query))
    return lax.dot_general(query, keys[:, place], (((1,), (1,)), ((), ())), preferred_element_type=F32)


def weigh_values(place, inside, scores, top, values):
    powers = jnp.exp2(scores - top).astype(BF16)
    value = values[:, place]
    value = jnp.where(inside, value, jnp.ones_like(value))
    return jnp.dot(powers, value, preferred_element_type=F32)


def attend(queries, keys, values, out):
    width = queries.shape[-1]
    for head in range(HEADS):
        place, inside, spare = head_lanes(head, width)
        scores = head_scores(place, inside, queries, keys)
        top = jnp.max(scores, axis=-1, keepdims=True)
        total = weigh_values(place, inside, scores, top, values)
        attended = (total * (1.0 / total[:, spare : spare + 1])).astype(out.dtype)
        out[:, place] = jnp.where(inside, attended, out[:, place])


def attend_part(queries, keys, values, bias, sums, stats):
    width = queries.shape[-1]
    column = lax.broadcasted_iota(jnp.int32, (1, LANES), 1)
    stats[:, :LANES] = jnp.zeros_like(stats[:, :LANES])
    stats[:, LANES:] = jnp.ones_like(stats[:, LANES:])
    for head in range(HEADS):
        place, inside, spare = head_lanes(head, width)
        scores = head_scores(place, inside, queries, keys)
        if bias is not None:
            scores = scores + bias
        top = jnp.max(scores, axis=-1, keepdims=True)
        total = weigh_values(place, inside, scores, top, values)
        sums[:, place] = jnp.where(inside, total, sums[:, place])
        stats[:, :LANES] = jnp.where(column == head, top, stats[:, :LANES])
        stats[:, LANES:] = jnp.where(column == head, total[:, spare : spare + 1], stats[:, LANES:])


def merge_parts(parts, out):
    width = out.shape[-1]
    row = lax.broadcasted_iota(jnp.int32, (2 * LANES, width), 0) % LANES
    column = lax.broadcasted_iota(jnp.int32, (2 * LANES, width), 1)
    head_size = width // HEADS
    spread = ((column >= row * head_size) & (column < (row + 1) * head_size)).astype(F32).astype(BF16)
    tops = [stats[:, :LANES] for _, stats in parts]
    top = functools.reduce(jnp.maximum, tops)
    factors = [jnp.exp2(part_top - top) for part_top in tops]
    weight = sum(factor * stats[:, LANES:] for factor, (_, stats) in zip(factors, parts))
    total = None
    for factor, (sums, _) in zip(factors, parts):
        factor = factor * (1.0 / weight)
        high = factor.astype(BF16)
        low = (factor - high.astype(F32)).astype(BF16)
        wide = jnp.dot(jnp.concatenate([high, low], axis=1), spread, preferred_element_type=F32)
        part = sums[...] * wide
        total = part if total is None else total + part
    out[...] = total.astype(out.dtype)


def query_scale(feature_width):
    return math.log2(math.e) / math.sqrt(feature_width // HEADS)


def column_chunks(width):
    return [(start, min(CHUNK, width - start)) for start in range(0, width, CHUNK)]


def stream_project(normed, weights, first_column, buffer, sems, out, sends=()):
    width = normed.shape[-1]
    chunks = column_chunks(out.shape[-1])
    copies = [
        pltpu.make_async_copy(
            weights.at[:, first_column + start : first_column + start + size],
            buffer.at[:, start : start + size],
            sems.at[index],
        )
        for index, (start, size) in enumerate(chunks)
    ]
    for copy in copies[:IN_FLIGHT]:
        copy.start()

    def multiply():
        for index, (start, size) in enumerate(chunks):
            copies[index].wait()
            if index + IN_FLIGHT < len(chunks):
                copies[index + IN_FLIGHT].start()
            product = jnp.dot(normed[...], buffer[:, start : start + size], preferred_element_type=F32)
            if first_column + start < width:
                column = lax.broadcasted_iota(jnp.int32, (1, size), 1) + first_column + start
                product = product * jnp.where(column < width, query_scale(width), 1.0)
            out[:, start : start + size] = product.astype(BF16)
            if sends:
                sends[index].start()

    return multiply


def weight_scratch(width, columns):
    return [pltpu.VMEM((width, columns), BF16), pltpu.SemaphoreType.DMA((len(column_chunks(columns)),))]


def split_heads(qkv, width):
    return [qkv.at[:, start : start + width] for start in range(0, qkv.shape[-1], width)]


def arrange_kernel(tile, quarters, left, right, sems):
    _, height, breadth, _ = quarters.shape
    copies = []
    for down in range(2):
        for across in range(2):
            index = 2 * down + across
            source = tile.at[
                height * down : height * (down + 1), breadth * across : breadth * (across + 1)
            ]
            copies.append(pltpu.make_async_copy(source, quarters.at[index], sems.at[index]))
            copies[-1].start()
    wide = 2 * HALO
    upper = lax.broadcasted_iota(jnp.int32, (wide, 1), 0) < HALO
    for copy in copies:
        copy.wait()
    for pair in range(height):
        down, row = divmod(2 * pair, height)
        place = slice(wide * pair, wide * (pair + 1))
        one, two = [quarters[2 * down, row + k, :wide].astype(F32) for k in range(2)]
        left[place] = jnp.where(upper, one, pltpu.roll(two, HALO, 0)).astype(BF16)
        one, two = [quarters[2 * down + 1, row + k, breadth - wide :].astype(F32) for k in range(2)]
        right[place] = jnp.where(upper, pltpu.roll(one, HALO, 0), two).astype(BF16)


def arrange(tile):
    rows, cols, width = tile.shape
    strip = jax.ShapeDtypeStruct((rows * HALO, width), BF16)
    return pl.pallas_call(
        arrange_kernel,
        in_specs=[HBM],
        out_specs=[VMEM, VMEM, VMEM],
        out_shape=[jax.ShapeDtypeStruct((4, rows // 2, cols // 2, width), BF16), strip, strip],
        scratch_shapes=[pltpu.SemaphoreType.DMA((4,))],
        compiler_params=pltpu.CompilerParams(vmem_limit_bytes=SMALL_LIMIT),
        cost_estimate=pl.CostEstimate(flops=0, bytes_accessed=4 * rows * cols * width, transcendentals=0),
        name="arrange",
    )(tile)


def own_kernel(half, branch, tokens, modulation, weights, *refs):
    queries_out, sums_out, stats_out, tokens_send, mark, here, normed, qkv, sums, stats, buffer, sems, copy_sems = refs
    arrival = pltpu.make_async_copy(tokens, here, copy_sems.at[0])
    arrival.start()
    multiply = stream_project(normed, weights, 0, buffer, sems, qkv)
    mark[...] = jnp.zeros_like(mark)
    arrival.wait()
    queries, keys, values = split_heads(qkv, here.shape[1])
    other = pl.ds(pl.multiple_of((1 - branch[0]) * half, half), half)
    sends = [
        pltpu.make_async_copy(here.at[other], tokens_send, copy_sems.at[1]),
        pltpu.make_async_copy(queries, queries_out, copy_sems.at[2]),
        pltpu.make_async_copy(sums, sums_out, copy_sems.at[3]),
        pltpu.make_async_copy(stats, stats_out, copy_sems.at[4]),
    ]
    sends[0].start()
    normed[...] = normalise(here[...], modulation[...])
    multiply()
    sends[1].start()
    attend_part(queries, keys, values, None, sums, stats)
    sends[2].start()
    sends[3].start()
    for copy in sends:
        copy.wait()


def own_tile(branch, tokens, modulation, wqkv):
    count, width = tokens.shape
    columns = wqkv.shape[1]
    half = count // 2
    return pl.pallas_call(
        functools.partial(own_kernel, half),
        in_specs=[SMEM, HBM, VMEM, HBM],
        out_specs=[HBM, HBM, HBM, HBM, VMEM],
        out_shape=[
            pltpu.HBM((count, width), BF16),
            pltpu.HBM((count, width), F32),
            pltpu.HBM((count, 2 * LANES), F32),
            pltpu.HBM((half, width), BF16),
            MARK,
        ],
        scratch_shapes=[
            pltpu.VMEM((count, width), BF16),
            pltpu.VMEM((count, width), BF16),
            pltpu.VMEM((count, columns), BF16),
            pltpu.VMEM((count, width), F32),
            pltpu.VMEM((count, 2 * LANES), F32),
        ]
        + weight_scratch(width, columns)
        + [pltpu.SemaphoreType.DMA((5,))],
        compiler_params=pltpu.CompilerParams(vmem_limit_bytes=VMEM_LIMIT),
        cost_estimate=pl.CostEstimate(
            flops=2 * count * width * columns + 4 * count * count * width * 3,
            bytes_accessed=2 * (width * columns + 5 * count * width),
            transcendentals=count * count * HEADS,
        ),
        name="own_tile",
    )(branch, tokens, modulation, wqkv)


def lattice_kernel(tokens, modulation, weights, *refs):
    whole, normed, qkv, buffer, sems = refs[-5:]
    multiply = stream_project(normed, weights, 0, buffer, sems, qkv)
    normed[...] = normalise(tokens[...], modulation[...])
    multiply()
    queries, keys, values = split_heads(qkv, tokens.shape[1])
    attend(queries, keys, values, whole)


def lattice(tokens, modulation, wqkv, after):
    count, width = tokens.shape
    columns = wqkv.shape[1]
    return pl.pallas_call(
        lattice_kernel,
        in_specs=[VMEM, VMEM, HBM] + [ANY] * len(after),
        out_specs=VMEM,
        out_shape=jax.ShapeDtypeStruct((count, width), BF16),
        scratch_shapes=[pltpu.VMEM((count, width), BF16), pltpu.VMEM((count, columns), BF16)]
        + weight_scratch(width, columns),
        compiler_params=pltpu.CompilerParams(vmem_limit_bytes=VMEM_LIMIT),
        cost_estimate=pl.CostEstimate(
            flops=2 * count * width * columns + 4 * count * count * width * 3,
            bytes_accessed=2 * (width * columns + 2 * count * width),
            transcendentals=count * count * HEADS,
        ),
        name="lattice",
    )(tokens, modulation, wqkv, *after)


def other_half_kernel(branch, whole, *refs):
    theirs = refs[-1]
    half = theirs.shape[0]
    theirs[...] = whole[pl.ds(pl.multiple_of((1 - branch[0]) * half, half), half)]


def other_half(branch, whole, after):
    half = (whole.shape[0] // 2, whole.shape[1])
    return pl.pallas_call(
        other_half_kernel,
        in_specs=[SMEM, VMEM] + [HBM] * len(after),
        out_specs=VMEM,
        out_shape=jax.ShapeDtypeStruct(half, BF16),
        compiler_params=pltpu.CompilerParams(vmem_limit_bytes=SMALL_LIMIT),
        cost_estimate=pl.CostEstimate(flops=0, bytes_accessed=2 * whole.size, transcendentals=0),
        name="other_half",
    )(branch, whole, *after)


def guidance(branch):
    conditional = branch[0] == 1
    return jnp.where(conditional, GUIDANCE, 1.0 - GUIDANCE), jnp.where(conditional, 1.0 - GUIDANCE, GUIDANCE)


def combine_kernel(branch, whole, theirs, out):
    own_factor, other_factor = guidance(branch)
    half = theirs.shape[0]
    mine = whole[pl.ds(pl.multiple_of(branch[0] * half, half), half)]
    both = own_factor * mine.astype(F32) + other_factor * theirs[...].astype(F32)
    out[...] = both.astype(BF16)


def combine(branch, whole, theirs):
    return pl.pallas_call(
        combine_kernel,
        in_specs=[SMEM, VMEM, VMEM],
        out_specs=VMEM,
        out_shape=jax.ShapeDtypeStruct(theirs.shape, BF16),
        compiler_params=pltpu.CompilerParams(vmem_limit_bytes=SMALL_LIMIT),
        cost_estimate=pl.CostEstimate(flops=3 * theirs.size, bytes_accessed=6 * theirs.size, transcendentals=0),
        name="combine",
    )(branch, whole, theirs)


def halo_places(rows, cols):
    def block(first_row, height, first_col, breadth):
        row, col = np.mgrid[first_row : first_row + height, first_col : first_col + breadth]
        return np.stack([row.reshape(-1), col.reshape(-1)])

    blocks = []
    for first_row in (-HALO, rows):
        blocks += [block(first_row, HALO, 0, cols), block(first_row, HALO, -HALO, HALO)]
        blocks += [block(first_row, HALO, cols, HALO)]
    blocks += [block(0, rows, -HALO, HALO), block(0, rows, cols, HALO)]
    return np.concatenate(blocks, axis=1).astype(np.int32)


def window_kernel(rows, cols, parts, branch, reach, places, tokens, own_queries, own_sums, own_stats, *refs):
    halo, (modulation, weights) = refs[:parts], refs[parts : parts + 2]
    mine, theirs, here, gathered, normed, halo_kv, queries, sums, stats, whole, *refs = refs[-15:]
    halo_sums, halo_stats, buffer, sems, copy_sems = refs
    half, width = theirs.shape
    first = pl.ds(pl.multiple_of(branch[0] * half, half), half)
    second = pl.ds(pl.multiple_of((1 - branch[0]) * half, half), half)
    arrivals = []
    start = 0
    for index, part in enumerate(halo):
        place = gathered.at[start : start + part.shape[0]]
        arrivals.append(pltpu.make_async_copy(part, place, copy_sems.at[index]))
        arrivals[-1].start()
        start += part.shape[0]
    multiply = stream_project(normed, weights, width, buffer, sems, halo_kv)
    own_copies = [
        pltpu.make_async_copy(own_queries, queries, copy_sems.at[parts]),
        pltpu.make_async_copy(own_sums, sums, copy_sems.at[parts + 4]),
        pltpu.make_async_copy(own_stats, stats, copy_sems.at[parts + 5]),
        pltpu.make_async_copy(tokens.at[first], here, copy_sems.at[parts + 6]),
    ]
    sends = [
        pltpu.make_async_copy(here, mine.at[1], copy_sems.at[parts + 1]),
        pltpu.make_async_copy(whole.at[first], mine.at[0], copy_sems.at[parts + 2]),
        pltpu.make_async_copy(whole.at[second], theirs, copy_sems.at[parts + 3]),
    ]
    for copy in own_copies:
        copy.start()
    row, col = places[0:1], places[1:2]
    limits = [jnp.where(branch[1 + side] != 0, reach[side], 0) for side in range(4)]
    allowed = (row >= -limits[0]) & (row < rows + limits[1])
    allowed = allowed & (col >= -limits[2]) & (col < cols + limits[3])
    bias = jnp.where(allowed, 0.0, -1e30).astype(F32)
    for copy in arrivals:
        copy.wait()
    normed[...] = normalise(gathered[...], modulation[...])
    multiply()
    for copy in own_copies:
        copy.wait()
    sends[0].start()
    keys, values = split_heads(halo_kv, width)
    attend_part(queries, keys, values, bias, halo_sums, halo_stats)
    merge_parts([(sums, stats), (halo_sums, halo_stats)], whole)
    for copy in sends[1:]:
        copy.start()
    for copy in sends:
        copy.wait()


def window(branch, reach, tokens, own, halo, modulation, wqkv, rows, cols, after):
    count, width = tokens.shape
    places = jnp.asarray(halo_places(rows, cols))
    halo_count = places.shape[1]
    half = (count // 2, width)
    return pl.pallas_call(
        functools.partial(window_kernel, rows, cols, len(halo)),
        in_specs=[SMEM, SMEM, VMEM, HBM, HBM, HBM, HBM] + [HBM] * len(halo) + [VMEM, HBM] + [HBM] * len(after),
        out_specs=[HBM, HBM],
        out_shape=[pltpu.HBM((2,) + half, BF16), pltpu.HBM(half, BF16)],
        scratch_shapes=[
            pltpu.VMEM(half, BF16),
            pltpu.VMEM((halo_count, width), BF16),
            pltpu.VMEM((halo_count, width), BF16),
            pltpu.VMEM((halo_count, 2 * width), BF16),
            pltpu.VMEM((count, width), BF16),
            pltpu.VMEM((count, width), F32),
            pltpu.VMEM((count, 2 * LANES), F32),
            pltpu.VMEM((count, width), BF16),
            pltpu.VMEM((count, width), F32),
            pltpu.VMEM((count, 2 * LANES), F32),
        ]
        + weight_scratch(width, 2 * width)
        + [pltpu.SemaphoreType.DMA((len(halo) + 7,))],
        compiler_params=pltpu.CompilerParams(vmem_limit_bytes=VMEM_LIMIT),
        cost_estimate=pl.CostEstimate(
            flops=4 * count * halo_count * width * 3 + 4 * halo_count * width * width,
            bytes_accessed=2 * (4 * count * width + 2 * halo_count * width + 2 * width * width),
            transcendentals=count * halo_count * HEADS,
        ),
        name="window",
    )(branch, reach, places, tokens, *[in_hbm(part) for part in own], *[in_hbm(part) for part in halo], modulation, wqkv, *after)


def finish_kernel(branch, mine, window_theirs, tokens_theirs, dilated, blend, gate, weights, out, buffer, sems):
    own_factor, other_factor = guidance(branch)
    size = buffer.shape[1] // 3
    columns = [slice(start, start + size) for start in range(0, buffer.shape[1], size)]
    copies = [
        pltpu.make_async_copy(weights.at[:, place], buffer.at[:, place], sems.at[index])
        for index, place in enumerate(columns)
    ]
    for copy in copies:
        copy.start()
    weight = blend[...]
    both = own_factor * mine[0].astype(F32) + other_factor * window_theirs[...].astype(F32)
    mixed = (weight * both + (1.0 - weight) * dilated[...].astype(F32)).astype(BF16)
    for copy, place in zip(copies, columns):
        copy.wait()
        projected = jnp.dot(mixed, buffer[:, place], preferred_element_type=F32)
        kept = own_factor * mine[1, :, place].astype(F32) + other_factor * tokens_theirs[:, place].astype(F32)
        out[:, place] = (kept + gate[:, place] * projected).astype(BF16)


def finish(branch, mine, window_theirs, tokens_theirs, dilated, blend, gate, w_out):
    count, width = dilated.shape
    return pl.pallas_call(
        finish_kernel,
        in_specs=[SMEM] + [VMEM] * 6 + [HBM],
        out_specs=VMEM,
        out_shape=jax.ShapeDtypeStruct((count, width), BF16),
        scratch_shapes=[pltpu.VMEM((width, width), BF16), pltpu.SemaphoreType.DMA((3,))],
        compiler_params=pltpu.CompilerParams(vmem_limit_bytes=FINISH_LIMIT),
        cost_estimate=pl.CostEstimate(
            flops=2 * count * width * width,
            bytes_accessed=2 * (width * width + 6 * count * width),
            transcendentals=0,
        ),
        name="finish",
    )(branch, mine, window_theirs, tokens_theirs, dilated, blend, gate, w_out)


def shift(cells, axis, forward):
    count = lax.axis_size(axis)
    if forward:
        pairs = [(i, i + 1) for i in range(count - 1)]
    else:
        pairs = [(i + 1, i) for i in range(count - 1)]
    return lax.ppermute(cells, axis, pairs)


def halo_rows(tile, left, right):
    rows, cols, width = tile.shape
    square = HALO * HALO
    lower = [tile[rows - HALO :].reshape(HALO * cols, width), left[-square:], right[-square:]]
    upper = [tile[:HALO].reshape(HALO * cols, width), left[:square], right[:square]]
    above = shift(jnp.concatenate(lower, axis=0), "row", True)
    below = shift(jnp.concatenate(upper, axis=0), "row", False)
    return above, below


def on_device(tokens, modulation, wqkv, w_out, blend, reach):
    tile = tokens[0]
    rows, cols, width = tile.shape
    row_groups = lax.axis_size("row")
    col_groups = lax.axis_size("col")
    sub_rows = rows // row_groups
    sub_cols = cols // col_groups
    half = rows // 2 * cols
    branch = lax.axis_index("branch")
    wqkv, w_out = in_hbm(wqkv), in_hbm(w_out)
    devices = row_groups * col_groups
    row, col = lax.axis_index("row"), lax.axis_index("col")
    inner = [row > 0, row < row_groups - 1, col > 0, col < col_groups - 1]
    place_of = jnp.stack([branch] + [side.astype(branch.dtype) for side in inner]).astype(jnp.int32)

    def other_core(cells):
        return lax.ppermute(cells, "branch", [(0, 1), (1, 0)])

    quarters, left_strip, right_strip = arrange(in_hbm(tile))
    left = shift(right_strip, "col", True)
    right = shift(left_strip, "col", False)
    outgoing = quarters.reshape(sub_rows * sub_cols, devices, width).transpose(1, 0, 2)
    arrived = lax.all_to_all(outgoing, ("row", "col"), split_axis=0, concat_axis=0, tiled=True)

    flat = tile.reshape(rows * cols, width)
    above, below = halo_rows(tile, left, right)
    *own, tokens_send, mark = own_tile(place_of, flat, modulation, wqkv)
    tokens_theirs = other_core(tokens_send)

    arrived = arrived.transpose(1, 0, 2).reshape(rows * cols, width)
    lattice_out = lattice(arrived, modulation, wqkv, [mark])
    lattice_theirs = other_core(other_half(place_of, lattice_out, [above, below]))
    combined = combine(place_of, lattice_out, lattice_theirs)
    combined = combined.reshape(sub_cols, devices, width).transpose(1, 0, 2)
    returned = lax.all_to_all(combined, ("row", "col"), split_axis=0, concat_axis=0, tiled=True)

    mine, send = window(
        place_of, reach.reshape(4), flat, own, [above, below, left, right], modulation, wqkv, rows, cols, [combined]
    )
    window_theirs = other_core(send)
    returned = returned.reshape(row_groups, col_groups, sub_cols, width).transpose(0, 2, 1, 3)
    dilated = returned.reshape(half, width)

    weight = lax.dynamic_index_in_dim(blend.reshape(2, half, 1), branch, 0, keepdims=False)
    guided = finish(
        place_of, mine, window_theirs, tokens_theirs, dilated, weight, modulation[2:3], w_out
    )
    return guided.reshape(rows // 2, cols, width)


def solution(mesh):
    in_specs = (
        P("branch", "row", "col", None),
        P(),
        P(),
        P(),
        P("row", "col"),
        P(None, "row", "col"),
    )
    out_specs = P(("row", "branch"), "col", None)
    return jax.shard_map(
        on_device, mesh=mesh, in_specs=in_specs, out_specs=out_specs, check_vma=False
    )
```

```python
import functools
import math

import jax
import jax.numpy as jnp
import numpy as np
from jax import lax
from jax.experimental import pallas as pl
from jax.experimental.pallas import tpu as pltpu
from jax.sharding import PartitionSpec as P

HEADS = 16
HALO = 4
GUIDANCE = 4.5
LANES = 128
VMEM_LIMIT = 28 * 1024 * 1024
SMALL_LIMIT = 4 * 1024 * 1024
FINISH_LIMIT = 16 * 1024 * 1024
ARRANGE_LIMIT = 8 * 1024 * 1024
FIRST_COLUMNS = 640
CHUNK = 512
IN_FLIGHT = 3

F32 = jnp.float32
BF16 = jnp.bfloat16

VMEM = pl.BlockSpec(memory_space=pltpu.VMEM)
SMEM = pl.BlockSpec(memory_space=pltpu.SMEM)
ANY = pl.BlockSpec(memory_space=pl.ANY)
HBM = pl.BlockSpec(memory_space=pltpu.HBM)
MARK = jax.ShapeDtypeStruct((8, LANES), F32)


def in_hbm(array):
    return pltpu.with_memory_space_constraint(array, pltpu.HBM)


def normalise(tokens, modulation):
    widened = tokens.astype(F32)
    centered = widened - jnp.mean(widened, axis=-1, keepdims=True)
    variance = jnp.mean(centered * centered, axis=-1, keepdims=True)
    scaled = centered * lax.rsqrt(variance + 1e-06)
    return (scaled * (1.0 + modulation[1:2]) + modulation[0:1]).astype(BF16)


def head_window(head, head_size, width):
    first = head * head_size
    low = first // LANES * LANES
    high = min(-(-(first + head_size) // LANES) * LANES, width)
    return first, low, high


def head_lanes(head, width):
    head_size = width // HEADS
    first, low, high = head_window(head, head_size, width)
    lane = lax.broadcasted_iota(jnp.int32, (1, high - low), 1) + low
    inside = (lane >= first) & (lane < first + head_size)
    return slice(low, high), inside, 0 if first > low else head_size


def head_scores(place, inside, queries, keys):
    query = queries[:, place]
    query = jnp.where(inside, query, jnp.zeros_like(query))
    return lax.dot_general(query, keys[:, place], (((1,), (1,)), ((), ())), preferred_element_type=F32)


def weigh_values(place, inside, scores, top, values):
    powers = jnp.exp2(scores - top).astype(BF16)
    value = values[:, place]
    value = jnp.where(inside, value, jnp.ones_like(value))
    return jnp.dot(powers, value, preferred_element_type=F32)


def attend(queries, keys, values, out):
    width = queries.shape[-1]
    for head in range(HEADS):
        place, inside, spare = head_lanes(head, width)
        scores = head_scores(place, inside, queries, keys)
        top = jnp.max(scores, axis=-1, keepdims=True)
        total = weigh_values(place, inside, scores, top, values)
        attended = (total * (1.0 / total[:, spare : spare + 1])).astype(out.dtype)
        out[:, place] = jnp.where(inside, attended, out[:, place])


def attend_part(queries, keys, values, bias, sums, stats):
    width = queries.shape[-1]
    column = lax.broadcasted_iota(jnp.int32, (1, LANES), 1)
    stats[:, :LANES] = jnp.zeros_like(stats[:, :LANES])
    stats[:, LANES:] = jnp.ones_like(stats[:, LANES:])
    for head in range(HEADS):
        place, inside, spare = head_lanes(head, width)
        scores = head_scores(place, inside, queries, keys)
        if bias is not None:
            scores = scores + bias
        top = jnp.max(scores, axis=-1, keepdims=True)
        total = weigh_values(place, inside, scores, top, values)
        sums[:, place] = jnp.where(inside, total, sums[:, place])
        stats[:, :LANES] = jnp.where(column == head, top, stats[:, :LANES])
        stats[:, LANES:] = jnp.where(column == head, total[:, spare : spare + 1], stats[:, LANES:])


def merge_parts(parts, out):
    width = out.shape[-1]
    row = lax.broadcasted_iota(jnp.int32, (2 * LANES, width), 0) % LANES
    column = lax.broadcasted_iota(jnp.int32, (2 * LANES, width), 1)
    head_size = width // HEADS
    spread = ((column >= row * head_size) & (column < (row + 1) * head_size)).astype(F32).astype(BF16)
    tops = [stats[:, :LANES] for _, stats in parts]
    top = functools.reduce(jnp.maximum, tops)
    factors = [jnp.exp2(part_top - top) for part_top in tops]
    weight = sum(factor * stats[:, LANES:] for factor, (_, stats) in zip(factors, parts))
    total = None
    for factor, (sums, _) in zip(factors, parts):
        factor = factor * (1.0 / weight)
        high = factor.astype(BF16)
        low = (factor - high.astype(F32)).astype(BF16)
        wide = jnp.dot(jnp.concatenate([high, low], axis=1), spread, preferred_element_type=F32)
        part = sums[...] * wide
        total = part if total is None else total + part
    out[...] = total.astype(out.dtype)


def query_scale(feature_width):
    return math.log2(math.e) / math.sqrt(feature_width // HEADS)


def column_chunks(width):
    return [(start, min(CHUNK, width - start)) for start in range(0, width, CHUNK)]


def stream_project(normed, weights, first_column, buffer, sems, out, sends=()):
    width = normed.shape[-1]
    chunks = column_chunks(out.shape[-1])
    copies = [
        pltpu.make_async_copy(
            weights.at[:, first_column + start : first_column + start + size],
            buffer.at[:, start : start + size],
            sems.at[index],
        )
        for index, (start, size) in enumerate(chunks)
    ]
    for copy in copies[:IN_FLIGHT]:
        copy.start()

    def multiply():
        for index, (start, size) in enumerate(chunks):
            copies[index].wait()
            if index + IN_FLIGHT < len(chunks):
                copies[index + IN_FLIGHT].start()
            product = jnp.dot(normed[...], buffer[:, start : start + size], preferred_element_type=F32)
            if first_column + start < width:
                column = lax.broadcasted_iota(jnp.int32, (1, size), 1) + first_column + start
                product = product * jnp.where(column < width, query_scale(width), 1.0)
            out[:, start : start + size] = product.astype(BF16)
            if sends:
                sends[index].start()

    return multiply


def weight_scratch(width, columns):
    return [pltpu.VMEM((width, columns), BF16), pltpu.SemaphoreType.DMA((len(column_chunks(columns)),))]


def split_heads(qkv, width):
    return [qkv.at[:, start : start + width] for start in range(0, qkv.shape[-1], width)]


def arrange_kernel(tile, outgoing, left, right, quarters, sems):
    _, height, breadth, width = quarters.shape
    copies = []
    for down in range(2):
        for across in range(2):
            index = 2 * down + across
            source = tile.at[
                height * down : height * (down + 1), breadth * across : breadth * (across + 1)
            ]
            copies.append(pltpu.make_async_copy(source, quarters.at[index], sems.at[index]))
            copies[-1].start()
    wide = 2 * HALO
    upper = lax.broadcasted_iota(jnp.int32, (wide, 1), 0) < HALO
    for index, copy in enumerate(copies):
        copy.wait()
        outgoing[:, index, :] = quarters[index].reshape(height * breadth, width)
    for pair in range(height):
        down, row = divmod(2 * pair, height)
        place = slice(wide * pair, wide * (pair + 1))
        one, two = [quarters[2 * down, row + k, :wide].astype(F32) for k in range(2)]
        left[place] = jnp.where(upper, one, pltpu.roll(two, HALO, 0)).astype(BF16)
        one, two = [quarters[2 * down + 1, row + k, breadth - wide :].astype(F32) for k in range(2)]
        right[place] = jnp.where(upper, pltpu.roll(one, HALO, 0), two).astype(BF16)


def arrange(tile):
    rows, cols, width = tile.shape
    strip = jax.ShapeDtypeStruct((rows * HALO, width), BF16)
    return pl.pallas_call(
        arrange_kernel,
        in_specs=[HBM],
        out_specs=[VMEM, VMEM, VMEM],
        out_shape=[jax.ShapeDtypeStruct((rows * cols // 4, 4, width), BF16), strip, strip],
        scratch_shapes=[
            pltpu.VMEM((4, rows // 2, cols // 2, width), BF16),
            pltpu.SemaphoreType.DMA((4,)),
        ],
        compiler_params=pltpu.CompilerParams(vmem_limit_bytes=ARRANGE_LIMIT),
        cost_estimate=pl.CostEstimate(flops=0, bytes_accessed=4 * rows * cols * width, transcendentals=0),
        name="arrange",
    )(tile)


def hold_kernel(cells, *refs):
    pass


def hold(cells, after):
    return pl.pallas_call(
        hold_kernel,
        in_specs=[ANY] * (1 + len(after)),
        out_specs=ANY,
        out_shape=jax.ShapeDtypeStruct(cells.shape, cells.dtype),
        input_output_aliases={0: 0},
        compiler_params=pltpu.CompilerParams(vmem_limit_bytes=SMALL_LIMIT),
        name="hold",
    )(cells, *after)


def own_kernel(half, branch, tokens, modulation, weights, *refs):
    queries_out, sums_out, stats_out, tokens_send, mark, here, normed, qkv, sums, stats, buffer, sems, copy_sems = refs
    arrival = pltpu.make_async_copy(tokens, here, copy_sems.at[0])
    arrival.start()
    multiply = stream_project(normed, weights, 0, buffer, sems, qkv)
    mark[...] = jnp.zeros_like(mark)
    arrival.wait()
    queries, keys, values = split_heads(qkv, here.shape[1])
    other = pl.ds(pl.multiple_of((1 - branch[0]) * half, half), half)
    sends = [
        pltpu.make_async_copy(here.at[other], tokens_send, copy_sems.at[1]),
        pltpu.make_async_copy(queries, queries_out, copy_sems.at[2]),
        pltpu.make_async_copy(sums, sums_out, copy_sems.at[3]),
        pltpu.make_async_copy(stats, stats_out, copy_sems.at[4]),
    ]
    sends[0].start()
    normed[...] = normalise(here[...], modulation[...])
    multiply()
    sends[1].start()
    attend_part(queries, keys, values, None, sums, stats)
    sends[2].start()
    sends[3].start()
    for copy in sends:
        copy.wait()


def own_tile(branch, tokens, modulation, wqkv):
    count, width = tokens.shape
    columns = wqkv.shape[1]
    half = count // 2
    return pl.pallas_call(
        functools.partial(own_kernel, half),
        in_specs=[SMEM, HBM, VMEM, HBM],
        out_specs=[HBM, HBM, HBM, HBM, VMEM],
        out_shape=[
            pltpu.HBM((count, width), BF16),
            pltpu.HBM((count, width), F32),
            pltpu.HBM((count, 2 * LANES), F32),
            pltpu.HBM((half, width), BF16),
            MARK,
        ],
        scratch_shapes=[
            pltpu.VMEM((count, width), BF16),
            pltpu.VMEM((count, width), BF16),
            pltpu.VMEM((count, columns), BF16),
            pltpu.VMEM((count, width), F32),
            pltpu.VMEM((count, 2 * LANES), F32),
        ]
        + weight_scratch(width, columns)
        + [pltpu.SemaphoreType.DMA((5,))],
        compiler_params=pltpu.CompilerParams(vmem_limit_bytes=VMEM_LIMIT),
        cost_estimate=pl.CostEstimate(
            flops=2 * count * width * columns + 4 * count * count * width * 3,
            bytes_accessed=2 * (width * columns + 5 * count * width),
            transcendentals=count * count * HEADS,
        ),
        name="own_tile",
    )(branch, tokens, modulation, wqkv)


def lane_tiles(width):
    return [slice(start, start + LANES) for start in range(0, width, LANES)]


def lattice_kernel(branch, tokens, modulation, weights, *refs):
    mine, theirs, normed, qkv, whole, tiles, buffer, sems = refs[-8:]
    count, width = whole.shape
    multiply = stream_project(normed, weights, 0, buffer, sems, qkv)
    normed[...] = normalise(tokens[...].reshape(count, width), modulation[...])
    multiply()
    queries, keys, values = split_heads(qkv, width)
    attend(queries, keys, values, whole)
    sources = count // 4
    for tile, lanes in enumerate(lane_tiles(width)):
        tiles[tile] = whole[:, lanes].astype(F32)
        for target, half in ((theirs, 1 - branch[0]), (mine, branch[0])):
            for across in range(2):
                rows = pl.ds(2 * half + across, sources, stride=4)
                target[sources * across : sources * (across + 1), lanes] = tiles[tile, rows, :].astype(BF16)


def lattice(branch, tokens, modulation, wqkv, after):
    sources, per_source, width = tokens.shape
    count = sources * per_source
    columns = wqkv.shape[1]
    half = jax.ShapeDtypeStruct((count // 2, width), BF16)
    return pl.pallas_call(
        lattice_kernel,
        in_specs=[SMEM, VMEM, VMEM, HBM] + [ANY] * len(after),
        out_specs=[VMEM, VMEM],
        out_shape=[half, half],
        scratch_shapes=[
            pltpu.VMEM((count, width), BF16),
            pltpu.VMEM((count, columns), BF16),
            pltpu.VMEM((count, width), BF16),
            pltpu.VMEM((width // LANES, count, LANES), F32),
        ]
        + weight_scratch(width, columns),
        compiler_params=pltpu.CompilerParams(vmem_limit_bytes=VMEM_LIMIT),
        cost_estimate=pl.CostEstimate(
            flops=2 * count * width * columns + 4 * count * count * width * 3,
            bytes_accessed=2 * (width * columns + 2 * count * width),
            transcendentals=count * count * HEADS,
        ),
        name="lattice",
    )(branch, tokens, modulation, wqkv, *after)


def guidance(branch):
    conditional = branch[0] == 1
    return jnp.where(conditional, GUIDANCE, 1.0 - GUIDANCE), jnp.where(conditional, 1.0 - GUIDANCE, GUIDANCE)


def combine_kernel(branch, mine, theirs, out):
    own_factor, other_factor = guidance(branch)
    both = own_factor * mine[...].astype(F32) + other_factor * theirs[...].astype(F32)
    sources = out.shape[0]
    for across in range(2):
        out[:, across, :] = both[sources * across : sources * (across + 1)].astype(BF16)


def combine(branch, mine, theirs):
    count, width = mine.shape
    return pl.pallas_call(
        combine_kernel,
        in_specs=[SMEM, VMEM, VMEM],
        out_specs=VMEM,
        out_shape=jax.ShapeDtypeStruct((count // 2, 2, width), BF16),
        compiler_params=pltpu.CompilerParams(vmem_limit_bytes=SMALL_LIMIT),
        cost_estimate=pl.CostEstimate(flops=3 * mine.size, bytes_accessed=6 * mine.size, transcendentals=0),
        name="combine",
    )(branch, mine, theirs)


def halo_places(rows, cols):
    def block(first_row, height, first_col, breadth):
        row, col = np.mgrid[first_row : first_row + height, first_col : first_col + breadth]
        return np.stack([row.reshape(-1), col.reshape(-1)])

    blocks = []
    for first_row in (-HALO, rows):
        blocks += [block(first_row, HALO, 0, cols), block(first_row, HALO, -HALO, HALO)]
        blocks += [block(first_row, HALO, cols, HALO)]
    blocks += [block(0, rows, -HALO, HALO), block(0, rows, cols, HALO)]
    return np.concatenate(blocks, axis=1).astype(np.int32)


def window_kernel(rows, cols, parts, branch, reach, places, own_queries, own_sums, own_stats, *refs):
    halo, (modulation, weights) = refs[:parts], refs[parts : parts + 2]
    mine, theirs, gathered, normed, halo_kv, queries, sums, stats, whole, *refs = refs[-14:]
    halo_sums, halo_stats, buffer, sems, copy_sems = refs
    half, width = theirs.shape
    first = pl.ds(pl.multiple_of(branch[0] * half, half), half)
    second = pl.ds(pl.multiple_of((1 - branch[0]) * half, half), half)
    arrivals = []
    start = 0
    for index, part in enumerate(halo):
        place = gathered.at[start : start + part.shape[0]]
        arrivals.append(pltpu.make_async_copy(part, place, copy_sems.at[index]))
        arrivals[-1].start()
        start += part.shape[0]
    multiply = stream_project(normed, weights, width, buffer, sems, halo_kv)
    own_copies = [
        pltpu.make_async_copy(own_queries, queries, copy_sems.at[parts]),
        pltpu.make_async_copy(own_sums, sums, copy_sems.at[parts + 1]),
        pltpu.make_async_copy(own_stats, stats, copy_sems.at[parts + 4]),
    ]
    sends = [
        pltpu.make_async_copy(whole.at[first], mine, copy_sems.at[parts + 2]),
        pltpu.make_async_copy(whole.at[second], theirs, copy_sems.at[parts + 3]),
    ]
    for copy in own_copies:
        copy.start()
    row, col = places[0:1], places[1:2]
    limits = [jnp.where(branch[1 + side] != 0, reach[side], 0) for side in range(4)]
    allowed = (row >= -limits[0]) & (row < rows + limits[1])
    allowed = allowed & (col >= -limits[2]) & (col < cols + limits[3])
    bias = jnp.where(allowed, 0.0, -1e30).astype(F32)
    for copy in arrivals:
        copy.wait()
    normed[...] = normalise(gathered[...], modulation[...])
    multiply()
    for copy in own_copies:
        copy.wait()
    keys, values = split_heads(halo_kv, width)
    attend_part(queries, keys, values, bias, halo_sums, halo_stats)
    merge_parts([(sums, stats), (halo_sums, halo_stats)], whole)
    for copy in sends:
        copy.start()
    for copy in sends:
        copy.wait()


def window(branch, reach, own, halo, modulation, wqkv, rows, cols, after):
    count, width = own[0].shape
    places = jnp.asarray(halo_places(rows, cols))
    halo_count = places.shape[1]
    half = (count // 2, width)
    return pl.pallas_call(
        functools.partial(window_kernel, rows, cols, len(halo)),
        in_specs=[SMEM, SMEM, VMEM, HBM, HBM, HBM] + [HBM] * len(halo) + [VMEM, HBM] + [HBM] * len(after),
        out_specs=[ANY, ANY],
        out_shape=[jax.ShapeDtypeStruct(half, BF16)] * 2,
        scratch_shapes=[
            pltpu.VMEM((halo_count, width), BF16),
            pltpu.VMEM((halo_count, width), BF16),
            pltpu.VMEM((halo_count, 2 * width), BF16),
            pltpu.VMEM((count, width), BF16),
            pltpu.VMEM((count, width), F32),
            pltpu.VMEM((count, 2 * LANES), F32),
            pltpu.VMEM((count, width), BF16),
            pltpu.VMEM((count, width), F32),
            pltpu.VMEM((count, 2 * LANES), F32),
        ]
        + weight_scratch(width, 2 * width)
        + [pltpu.SemaphoreType.DMA((len(halo) + 5,))],
        compiler_params=pltpu.CompilerParams(vmem_limit_bytes=VMEM_LIMIT),
        cost_estimate=pl.CostEstimate(
            flops=4 * count * halo_count * width * 3 + 4 * halo_count * width * width,
            bytes_accessed=2 * (4 * count * width + 2 * halo_count * width + 2 * width * width),
            transcendentals=count * halo_count * HEADS,
        ),
        name="window",
    )(branch, reach, places, *[in_hbm(part) for part in own], *[in_hbm(part) for part in halo], modulation, wqkv, *after)


def finish_kernel(
    col_groups, branch, window_mine, window_theirs, tokens, tokens_theirs, returned, blend, gate, weights, out, *refs
):
    tokens_mine, raw, dilated, result, buffer, sems, out_sems = refs
    own_factor, other_factor = guidance(branch)
    count, width = dilated.shape
    columns = [slice(0, FIRST_COLUMNS), slice(FIRST_COLUMNS, width)]
    copies = [
        pltpu.make_async_copy(weights.at[:, place], buffer.at[:, place], sems.at[index])
        for index, place in enumerate(columns)
    ]
    sends = [
        pltpu.make_async_copy(result.at[:, place], out.at[:, place], out_sems.at[index])
        for index, place in enumerate(columns)
    ]
    mine = pl.ds(pl.multiple_of(branch[0] * count, count), count)
    arrival = pltpu.make_async_copy(tokens.at[mine], tokens_mine, sems.at[len(columns)])
    for copy in [arrival] + copies:
        copy.start()
    flat = returned[...].reshape(count, width)
    for tile, lanes in enumerate(lane_tiles(width)):
        raw[tile] = flat[:, lanes].astype(F32)
        for across in range(2):
            cells = raw[tile, pl.ds(across, count // 2, stride=2), :]
            for row in range(count // 2 // col_groups):
                start = col_groups * (2 * row + across)
                dilated[start : start + col_groups, lanes] = cells[col_groups * row : col_groups * (row + 1)]
    weight = blend[...]
    both = own_factor * window_mine[...].astype(F32) + other_factor * window_theirs[...].astype(F32)
    mixed = (weight * both + (1.0 - weight) * dilated[...]).astype(BF16)
    arrival.wait()
    for copy, send, place in zip(copies, sends, columns):
        kept = own_factor * tokens_mine[:, place].astype(F32) + other_factor * tokens_theirs[:, place].astype(F32)
        copy.wait()
        projected = jnp.dot(mixed, buffer[:, place], preferred_element_type=F32)
        result[:, place] = (kept + gate[:, place] * projected).astype(BF16)
        send.start()
    for send in sends:
        send.wait()


def finish(branch, window_mine, window_theirs, tokens, tokens_theirs, returned, blend, gate, w_out, col_groups):
    count, width = window_mine.shape
    return pl.pallas_call(
        functools.partial(finish_kernel, col_groups),
        in_specs=[SMEM, VMEM, VMEM, HBM] + [VMEM] * 4 + [HBM],
        out_specs=HBM,
        out_shape=jax.ShapeDtypeStruct((count, width), BF16),
        scratch_shapes=[
            pltpu.VMEM((count, width), BF16),
            pltpu.VMEM((width // LANES, count, LANES), F32),
            pltpu.VMEM((count, width), F32),
            pltpu.VMEM((count, width), BF16),
            pltpu.VMEM((width, width), BF16),
            pltpu.SemaphoreType.DMA((3,)),
            pltpu.SemaphoreType.DMA((2,)),
        ],
        compiler_params=pltpu.CompilerParams(vmem_limit_bytes=FINISH_LIMIT),
        cost_estimate=pl.CostEstimate(
            flops=2 * count * width * width,
            bytes_accessed=2 * (width * width + 6 * count * width),
            transcendentals=0,
        ),
        name="finish",
    )(branch, window_mine, window_theirs, tokens, tokens_theirs, returned, blend, gate, w_out)


def shift(cells, axis, forward):
    count = lax.axis_size(axis)
    if forward:
        pairs = [(i, i + 1) for i in range(count - 1)]
    else:
        pairs = [(i + 1, i) for i in range(count - 1)]
    return lax.ppermute(cells, axis, pairs)


def halo_rows(tile, left, right):
    rows, cols, width = tile.shape
    square = HALO * HALO
    lower = [tile[rows - HALO :].reshape(HALO * cols, width), left[-square:], right[-square:]]
    upper = [tile[:HALO].reshape(HALO * cols, width), left[:square], right[:square]]
    above = shift(jnp.concatenate(lower, axis=0), "row", True)
    below = shift(jnp.concatenate(upper, axis=0), "row", False)
    return above, below


def on_device(tokens, modulation, wqkv, w_out, blend, reach):
    tile = tokens[0]
    rows, cols, width = tile.shape
    row_groups = lax.axis_size("row")
    col_groups = lax.axis_size("col")
    sub_rows = rows // row_groups
    sub_cols = cols // col_groups
    half = rows // 2 * cols
    branch = lax.axis_index("branch")
    wqkv, w_out = in_hbm(wqkv), in_hbm(w_out)
    devices = row_groups * col_groups
    row, col = lax.axis_index("row"), lax.axis_index("col")
    inner = [row > 0, row < row_groups - 1, col > 0, col < col_groups - 1]
    place_of = jnp.stack([branch] + [side.astype(branch.dtype) for side in inner]).astype(jnp.int32)

    def other_core(cells):
        return lax.ppermute(cells, "branch", [(0, 1), (1, 0)])

    outgoing, left_strip, right_strip = arrange(in_hbm(tile))
    left = shift(right_strip, "col", True)
    right = shift(left_strip, "col", False)
    arrived = lax.all_to_all(outgoing, ("row", "col"), split_axis=0, concat_axis=0, tiled=True)

    flat = tile.reshape(rows * cols, width)
    above, below = halo_rows(tile, left, right)
    *own, tokens_send, mark = own_tile(place_of, flat, modulation, wqkv)
    tokens_theirs = other_core(tokens_send)

    lattice_mine, lattice_send = lattice(place_of, arrived, modulation, wqkv, [mark])
    lattice_theirs = other_core(hold(lattice_send, [above, below]))
    combined = combine(place_of, lattice_mine, lattice_theirs)
    returned = lax.all_to_all(combined, ("row", "col"), split_axis=0, concat_axis=0, tiled=True)

    window_mine, send = window(
        place_of, reach.reshape(4), own, [above, below, left, right], modulation, wqkv, rows, cols, [combined]
    )
    window_theirs = other_core(send)
    weight = lax.dynamic_index_in_dim(blend.reshape(2, half, 1), branch, 0, keepdims=False)
    guided = finish(
        place_of,
        window_mine,
        window_theirs,
        in_hbm(flat),
        tokens_theirs,
        returned,
        weight,
        modulation[2:3],
        w_out,
        col_groups,
    )
    return guided.reshape(rows // 2, cols, width)


def solution(mesh):
    in_specs = (
        P("branch", "row", "col", None),
        P(),
        P(),
        P(),
        P("row", "col"),
        P(None, "row", "col"),
    )
    out_specs = P(("row", "branch"), "col", None)
    return jax.shard_map(
        on_device, mesh=mesh, in_specs=in_specs, out_specs=out_specs, check_vma=False
    )
```

```python
import functools
import math

import jax
import jax.numpy as jnp
import numpy as np
from jax import lax
from jax.experimental import pallas as pl
from jax.experimental.pallas import tpu as pltpu
from jax.sharding import PartitionSpec as P

HEADS = 16
HALO = 4
GUIDANCE = 4.5
LANES = 128
VMEM_LIMIT = 28 * 1024 * 1024
SMALL_LIMIT = 4 * 1024 * 1024
FINISH_LIMIT = 16 * 1024 * 1024
PACK_LIMIT = 8 * 1024 * 1024
FIRST_COLUMNS = 640
CHUNK = 512
IN_FLIGHT = 3

F32 = jnp.float32
BF16 = jnp.bfloat16

VMEM = pl.BlockSpec(memory_space=pltpu.VMEM)
SMEM = pl.BlockSpec(memory_space=pltpu.SMEM)
ANY = pl.BlockSpec(memory_space=pl.ANY)
HBM = pl.BlockSpec(memory_space=pltpu.HBM)
MARK = jax.ShapeDtypeStruct((8, LANES), F32)


def in_hbm(array):
    return pltpu.with_memory_space_constraint(array, pltpu.HBM)


def normalise(tokens, modulation):
    widened = tokens.astype(F32)
    centered = widened - jnp.mean(widened, axis=-1, keepdims=True)
    variance = jnp.mean(centered * centered, axis=-1, keepdims=True)
    scaled = centered * lax.rsqrt(variance + 1e-06)
    return (scaled * (1.0 + modulation[1:2]) + modulation[0:1]).astype(BF16)


def head_window(head, head_size, width):
    first = head * head_size
    low = first // LANES * LANES
    high = min(-(-(first + head_size) // LANES) * LANES, width)
    return first, low, high


def head_lanes(head, width):
    head_size = width // HEADS
    first, low, high = head_window(head, head_size, width)
    lane = lax.broadcasted_iota(jnp.int32, (1, high - low), 1) + low
    inside = (lane >= first) & (lane < first + head_size)
    return slice(low, high), inside, 0 if first > low else head_size


def head_scores(place, inside, queries, keys):
    query = queries[:, place]
    query = jnp.where(inside, query, jnp.zeros_like(query))
    return lax.dot_general(query, keys[:, place], (((1,), (1,)), ((), ())), preferred_element_type=F32)


def weigh_values(place, inside, scores, top, values):
    powers = jnp.exp2(scores - top).astype(BF16)
    value = values[:, place]
    value = jnp.where(inside, value, jnp.ones_like(value))
    return jnp.dot(powers, value, preferred_element_type=F32)


def attend(queries, keys, values, out):
    width = queries.shape[-1]
    for head in range(HEADS):
        place, inside, spare = head_lanes(head, width)
        scores = head_scores(place, inside, queries, keys)
        top = jnp.max(scores, axis=-1, keepdims=True)
        total = weigh_values(place, inside, scores, top, values)
        attended = (total * (1.0 / total[:, spare : spare + 1])).astype(out.dtype)
        out[:, place] = jnp.where(inside, attended, out[:, place])


def attend_part(queries, keys, values, bias, sums, stats):
    width = queries.shape[-1]
    column = lax.broadcasted_iota(jnp.int32, (1, LANES), 1)
    stats[:, :LANES] = jnp.zeros_like(stats[:, :LANES])
    stats[:, LANES:] = jnp.ones_like(stats[:, LANES:])
    for head in range(HEADS):
        place, inside, spare = head_lanes(head, width)
        scores = head_scores(place, inside, queries, keys)
        if bias is not None:
            scores = scores + bias
        top = jnp.max(scores, axis=-1, keepdims=True)
        total = weigh_values(place, inside, scores, top, values)
        sums[:, place] = jnp.where(inside, total, sums[:, place])
        stats[:, :LANES] = jnp.where(column == head, top, stats[:, :LANES])
        stats[:, LANES:] = jnp.where(column == head, total[:, spare : spare + 1], stats[:, LANES:])


def merge_parts(parts, out):
    width = out.shape[-1]
    row = lax.broadcasted_iota(jnp.int32, (2 * LANES, width), 0) % LANES
    column = lax.broadcasted_iota(jnp.int32, (2 * LANES, width), 1)
    head_size = width // HEADS
    spread = ((column >= row * head_size) & (column < (row + 1) * head_size)).astype(F32).astype(BF16)
    tops = [stats[:, :LANES] for _, stats in parts]
    top = functools.reduce(jnp.maximum, tops)
    factors = [jnp.exp2(part_top - top) for part_top in tops]
    weight = sum(factor * stats[:, LANES:] for factor, (_, stats) in zip(factors, parts))
    total = None
    for factor, (sums, _) in zip(factors, parts):
        factor = factor * (1.0 / weight)
        high = factor.astype(BF16)
        low = (factor - high.astype(F32)).astype(BF16)
        wide = jnp.dot(jnp.concatenate([high, low], axis=1), spread, preferred_element_type=F32)
        part = sums[...] * wide
        total = part if total is None else total + part
    out[...] = total.astype(out.dtype)


def query_scale(feature_width):
    return math.log2(math.e) / math.sqrt(feature_width // HEADS)


def column_chunks(width):
    return [(start, min(CHUNK, width - start)) for start in range(0, width, CHUNK)]


def stream_project(normed, weights, first_column, buffer, sems, out, sends=()):
    width = normed.shape[-1]
    chunks = column_chunks(out.shape[-1])
    copies = [
        pltpu.make_async_copy(
            weights.at[:, first_column + start : first_column + start + size],
            buffer.at[:, start : start + size],
            sems.at[index],
        )
        for index, (start, size) in enumerate(chunks)
    ]
    for copy in copies[:IN_FLIGHT]:
        copy.start()

    def multiply():
        for index, (start, size) in enumerate(chunks):
            copies[index].wait()
            if index + IN_FLIGHT < len(chunks):
                copies[index + IN_FLIGHT].start()
            product = jnp.dot(normed[...], buffer[:, start : start + size], preferred_element_type=F32)
            if first_column + start < width:
                column = lax.broadcasted_iota(jnp.int32, (1, size), 1) + first_column + start
                product = product * jnp.where(column < width, query_scale(width), 1.0)
            out[:, start : start + size] = product.astype(BF16)
            if sends:
                sends[index].start()

    return multiply


def weight_scratch(width, columns):
    return [pltpu.VMEM((width, columns), BF16), pltpu.SemaphoreType.DMA((len(column_chunks(columns)),))]


def split_heads(qkv, width):
    return [qkv.at[:, start : start + width] for start in range(0, qkv.shape[-1], width)]


def pack_kernel(tile, outgoing, quarters, sems):
    _, height, breadth, width = quarters.shape
    copies = []
    for down in range(2):
        for across in range(2):
            index = 2 * down + across
            source = tile.at[
                height * down : height * (down + 1), breadth * across : breadth * (across + 1)
            ]
            copies.append(pltpu.make_async_copy(source, quarters.at[index], sems.at[index]))
            copies[-1].start()
    for index, copy in enumerate(copies):
        copy.wait()
        outgoing[:, index, :] = quarters[index].reshape(height * breadth, width)


def pack(tile):
    rows, cols, width = tile.shape
    return pl.pallas_call(
        pack_kernel,
        in_specs=[HBM],
        out_specs=VMEM,
        out_shape=jax.ShapeDtypeStruct((rows * cols // 4, 4, width), BF16),
        scratch_shapes=[
            pltpu.VMEM((4, rows // 2, cols // 2, width), BF16),
            pltpu.SemaphoreType.DMA((4,)),
        ],
        compiler_params=pltpu.CompilerParams(vmem_limit_bytes=PACK_LIMIT),
        cost_estimate=pl.CostEstimate(flops=0, bytes_accessed=4 * rows * cols * width, transcendentals=0),
        name="pack",
    )(tile)


def copy_pieces(pieces):
    for target, start, source, first, count in pieces:
        if source is None:
            target[start : start + count] = jnp.zeros_like(target[start : start + count])
        else:
            target[start : start + count] = source[first : first + count]


def edges_kernel(place_of, tile, keep_out, send, keep, top, bottom, first, last, sems):
    rows, cols, width = tile.shape
    wide, strip, side, square = 2 * HALO, HALO * cols, HALO * rows, HALO * HALO
    copies = [
        pltpu.make_async_copy(tile.at[:HALO], top, sems.at[0]),
        pltpu.make_async_copy(tile.at[rows - HALO :], bottom, sems.at[1]),
        pltpu.make_async_copy(tile.at[:, :wide], first, sems.at[2]),
        pltpu.make_async_copy(tile.at[:, cols - wide :], last, sems.at[3]),
    ]
    for copy in copies:
        copy.start()
    for copy in copies:
        copy.wait()
    upper = lax.broadcasted_iota(jnp.int32, (wide, 1), 0) < HALO

    def fill(row_edges, col_edges):
        row_edges[:strip] = top[...].reshape(strip, width)
        row_edges[strip : 2 * strip] = bottom[...].reshape(strip, width)
        for pair in range(rows // 2):
            place = wide * pair
            one, two = first[2 * pair].astype(F32), first[2 * pair + 1].astype(F32)
            col_edges[place : place + wide] = jnp.where(upper, one, pltpu.roll(two, HALO, 0)).astype(BF16)
            one, two = last[2 * pair].astype(F32), last[2 * pair + 1].astype(F32)
            place += side
            col_edges[place : place + wide] = jnp.where(upper, pltpu.roll(one, HALO, 0), two).astype(BF16)
        copy_pieces(
            [
                (row_edges, 2 * strip, col_edges, 0, square),
                (row_edges, 2 * strip + square, col_edges, 2 * side - square, square),
                (col_edges, 2 * side, col_edges, side, square),
                (col_edges, 2 * side + square, col_edges, side - square, square),
                (col_edges, 2 * side + 2 * square, None, 0, 2 * (strip - side)),
            ]
        )

    @pl.when(place_of[0] == 0)
    def _():
        fill(keep, send)

    @pl.when(place_of[0] != 0)
    def _():
        fill(send, keep)

    copy = pltpu.make_async_copy(keep, keep_out, sems.at[4])
    copy.start()
    copy.wait()


def edge_count(rows, cols):
    return 2 * HALO * cols + 2 * HALO * HALO


def edges(place_of, tile):
    rows, cols, width = tile.shape
    shape = (edge_count(rows, cols), width)
    return pl.pallas_call(
        edges_kernel,
        in_specs=[SMEM, HBM],
        out_specs=[HBM, VMEM],
        out_shape=[pltpu.HBM(shape, BF16), jax.ShapeDtypeStruct(shape, BF16)],
        scratch_shapes=[pltpu.VMEM(shape, BF16)]
        + [pltpu.VMEM((HALO, cols, width), BF16)] * 2
        + [pltpu.VMEM((rows, 2 * HALO, width), BF16)] * 2
        + [pltpu.SemaphoreType.DMA((5,))],
        compiler_params=pltpu.CompilerParams(vmem_limit_bytes=PACK_LIMIT),
        cost_estimate=pl.CostEstimate(flops=0, bytes_accessed=8 * shape[0] * width, transcendentals=0),
        name="edges",
    )(place_of, tile)


def outbound_kernel(rows, cols, place_of, keep, received, forward, backward, forward_corner, backward_corner):
    strip, side, square = HALO * cols, HALO * rows, HALO * HALO

    def fill(edge, corners):
        pieces = []
        for index, source in enumerate((keep, received)):
            for target, first in ((forward, edge), (backward, 0)):
                pieces.append((target, strip * index, source, first, edge))
                if edge < strip:
                    pieces.append((target, strip * index + edge, None, 0, strip - edge))
            pieces.append((forward_corner, square * index, source, corners + square, square))
            pieces.append((backward_corner, square * index, source, corners, square))
        copy_pieces(pieces)

    @pl.when(place_of[0] == 0)
    def _():
        fill(strip, 2 * strip)

    @pl.when(place_of[0] != 0)
    def _():
        fill(side, 2 * side)


def outbound(place_of, keep, received, rows, cols):
    width = keep.shape[1]
    strip = jax.ShapeDtypeStruct((2 * HALO * cols, width), BF16)
    corner = jax.ShapeDtypeStruct((2 * HALO * HALO, width), BF16)
    return pl.pallas_call(
        functools.partial(outbound_kernel, rows, cols),
        in_specs=[SMEM, VMEM, VMEM],
        out_specs=[VMEM] * 4,
        out_shape=[strip, strip, corner, corner],
        compiler_params=pltpu.CompilerParams(vmem_limit_bytes=SMALL_LIMIT),
        cost_estimate=pl.CostEstimate(flops=0, bytes_accessed=8 * keep.size, transcendentals=0),
        name="outbound",
    )(place_of, keep, received)


def across_tiles(cells, first_step, second_step):
    row_groups, col_groups = lax.axis_size("row"), lax.axis_size("col")
    pairs = []
    for core, (down, right) in enumerate((first_step, second_step)):
        for row in range(row_groups):
            for col in range(col_groups):
                to_row, to_col = row + down, col + right
                if 0 <= to_row < row_groups and 0 <= to_col < col_groups:
                    start = core * row_groups * col_groups
                    pairs.append((start + row * col_groups + col, start + to_row * col_groups + to_col))
    return lax.ppermute(cells, ("branch", "row", "col"), pairs)


def inbound_kernel(forward, backward, forward_corner, backward_corner, after, out):
    start = 0
    for part in (forward, backward, forward_corner, backward_corner):
        count = part.shape[0] // 2
        out[start : start + count] = part[count:]
        start += count


def inbound(parts, after):
    count = sum(part.shape[0] for part in parts) // 2
    shape = jax.ShapeDtypeStruct((count, parts[0].shape[1]), BF16)
    return pl.pallas_call(
        inbound_kernel,
        in_specs=[VMEM] * 4 + [ANY],
        out_specs=VMEM,
        out_shape=shape,
        compiler_params=pltpu.CompilerParams(vmem_limit_bytes=SMALL_LIMIT),
        cost_estimate=pl.CostEstimate(flops=0, bytes_accessed=4 * shape.size, transcendentals=0),
        name="inbound",
    )(*parts, after)


def hold_kernel(cells, *refs):
    pass


def hold(cells, after):
    return pl.pallas_call(
        hold_kernel,
        in_specs=[ANY] * (1 + len(after)),
        out_specs=ANY,
        out_shape=jax.ShapeDtypeStruct(cells.shape, cells.dtype),
        input_output_aliases={0: 0},
        compiler_params=pltpu.CompilerParams(vmem_limit_bytes=SMALL_LIMIT),
        name="hold",
    )(cells, *after)


def own_kernel(half, branch, tokens, modulation, weights, *refs):
    queries_out, sums_out, stats_out, tokens_send, mark, here, normed, qkv, sums, stats, buffer, sems, copy_sems = refs
    arrival = pltpu.make_async_copy(tokens, here, copy_sems.at[0])
    arrival.start()
    multiply = stream_project(normed, weights, 0, buffer, sems, qkv)
    mark[...] = jnp.zeros_like(mark)
    arrival.wait()
    queries, keys, values = split_heads(qkv, here.shape[1])
    other = pl.ds(pl.multiple_of((1 - branch[0]) * half, half), half)
    sends = [
        pltpu.make_async_copy(here.at[other], tokens_send, copy_sems.at[1]),
        pltpu.make_async_copy(queries, queries_out, copy_sems.at[2]),
        pltpu.make_async_copy(sums, sums_out, copy_sems.at[3]),
        pltpu.make_async_copy(stats, stats_out, copy_sems.at[4]),
    ]
    sends[0].start()
    normed[...] = normalise(here[...], modulation[...])
    multiply()
    sends[1].start()
    attend_part(queries, keys, values, None, sums, stats)
    sends[2].start()
    sends[3].start()
    for copy in sends:
        copy.wait()


def own_tile(branch, tokens, modulation, wqkv):
    count, width = tokens.shape
    columns = wqkv.shape[1]
    half = count // 2
    return pl.pallas_call(
        functools.partial(own_kernel, half),
        in_specs=[SMEM, HBM, VMEM, HBM],
        out_specs=[HBM, HBM, HBM, HBM, VMEM],
        out_shape=[
            pltpu.HBM((count, width), BF16),
            pltpu.HBM((count, width), F32),
            pltpu.HBM((count, 2 * LANES), F32),
            pltpu.HBM((half, width), BF16),
            MARK,
        ],
        scratch_shapes=[
            pltpu.VMEM((count, width), BF16),
            pltpu.VMEM((count, width), BF16),
            pltpu.VMEM((count, columns), BF16),
            pltpu.VMEM((count, width), F32),
            pltpu.VMEM((count, 2 * LANES), F32),
        ]
        + weight_scratch(width, columns)
        + [pltpu.SemaphoreType.DMA((5,))],
        compiler_params=pltpu.CompilerParams(vmem_limit_bytes=VMEM_LIMIT),
        cost_estimate=pl.CostEstimate(
            flops=2 * count * width * columns + 4 * count * count * width * 3,
            bytes_accessed=2 * (width * columns + 5 * count * width),
            transcendentals=count * count * HEADS,
        ),
        name="own_tile",
    )(branch, tokens, modulation, wqkv)


def lane_tiles(width):
    return [slice(start, start + LANES) for start in range(0, width, LANES)]


def lattice_kernel(branch, tokens, modulation, weights, *refs):
    mine, theirs, normed, qkv, whole, tiles, buffer, sems = refs[-8:]
    count, width = whole.shape
    multiply = stream_project(normed, weights, 0, buffer, sems, qkv)
    normed[...] = normalise(tokens[...].reshape(count, width), modulation[...])
    multiply()
    queries, keys, values = split_heads(qkv, width)
    attend(queries, keys, values, whole)
    sources = count // 4
    for tile, lanes in enumerate(lane_tiles(width)):
        tiles[tile] = whole[:, lanes].astype(F32)
        for target, half in ((theirs, 1 - branch[0]), (mine, branch[0])):
            for across in range(2):
                rows = pl.ds(2 * half + across, sources, stride=4)
                target[sources * across : sources * (across + 1), lanes] = tiles[tile, rows, :].astype(BF16)


def lattice(branch, tokens, modulation, wqkv, after):
    sources, per_source, width = tokens.shape
    count = sources * per_source
    columns = wqkv.shape[1]
    half = jax.ShapeDtypeStruct((count // 2, width), BF16)
    return pl.pallas_call(
        lattice_kernel,
        in_specs=[SMEM, VMEM, VMEM, HBM] + [ANY] * len(after),
        out_specs=[VMEM, VMEM],
        out_shape=[half, half],
        scratch_shapes=[
            pltpu.VMEM((count, width), BF16),
            pltpu.VMEM((count, columns), BF16),
            pltpu.VMEM((count, width), BF16),
            pltpu.VMEM((width // LANES, count, LANES), F32),
        ]
        + weight_scratch(width, columns),
        compiler_params=pltpu.CompilerParams(vmem_limit_bytes=VMEM_LIMIT),
        cost_estimate=pl.CostEstimate(
            flops=2 * count * width * columns + 4 * count * count * width * 3,
            bytes_accessed=2 * (width * columns + 2 * count * width),
            transcendentals=count * count * HEADS,
        ),
        name="lattice",
    )(branch, tokens, modulation, wqkv, *after)


def guidance(branch):
    conditional = branch[0] == 1
    return jnp.where(conditional, GUIDANCE, 1.0 - GUIDANCE), jnp.where(conditional, 1.0 - GUIDANCE, GUIDANCE)


def combine_kernel(branch, mine, theirs, out):
    own_factor, other_factor = guidance(branch)
    both = own_factor * mine[...].astype(F32) + other_factor * theirs[...].astype(F32)
    sources = out.shape[0]
    for across in range(2):
        out[:, across, :] = both[sources * across : sources * (across + 1)].astype(BF16)


def combine(branch, mine, theirs):
    count, width = mine.shape
    return pl.pallas_call(
        combine_kernel,
        in_specs=[SMEM, VMEM, VMEM],
        out_specs=VMEM,
        out_shape=jax.ShapeDtypeStruct((count // 2, 2, width), BF16),
        compiler_params=pltpu.CompilerParams(vmem_limit_bytes=SMALL_LIMIT),
        cost_estimate=pl.CostEstimate(flops=3 * mine.size, bytes_accessed=6 * mine.size, transcendentals=0),
        name="combine",
    )(branch, mine, theirs)


def halo_places(rows, cols):
    def block(first_row, height, first_col, breadth):
        row, col = np.mgrid[first_row : first_row + height, first_col : first_col + breadth]
        return np.stack([row.reshape(-1), col.reshape(-1)])

    blocks = [block(-HALO, HALO, 0, cols), block(rows, HALO, 0, cols)]
    blocks += [block(0, rows, -HALO, HALO), block(0, rows, cols, HALO)]
    corners = ((-HALO, -HALO), (rows, cols), (-HALO, cols), (rows, -HALO))
    blocks += [block(first_row, HALO, first_col, HALO) for first_row, first_col in corners]
    return np.concatenate(blocks, axis=1).astype(np.int32)


def gather_halo(rows, cols, place_of, parts, gathered, sems):
    strip, side, square = HALO * cols, HALO * rows, HALO * HALO
    forward, backward, forward_corner, backward_corner, passed = parts

    def bring(pieces):
        copies = []
        for index, (start, source, first, count) in enumerate(pieces):
            copies.append(
                pltpu.make_async_copy(
                    source.at[first : first + count], gathered.at[start : start + count], sems.at[index]
                )
            )
            copies[-1].start()
        for copy in copies:
            copy.wait()

    corner = 2 * strip + 2 * side

    @pl.when(place_of[0] == 0)
    def _():
        bring(
            [
                (0, forward, 0, strip),
                (strip, backward, 0, strip),
                (2 * strip, passed, 0, side),
                (2 * strip + side, passed, strip, side),
                (corner, forward_corner, 0, square),
                (corner + square, backward_corner, 0, square),
                (corner + 2 * square, passed, 2 * strip, 2 * square),
            ]
        )

    @pl.when(place_of[0] != 0)
    def _():
        bring(
            [
                (0, passed, 0, 2 * strip),
                (2 * strip, forward, 0, side),
                (2 * strip + side, backward, 0, side),
                (corner, passed, 2 * strip, 2 * square),
                (corner + 2 * square, forward_corner, 0, square),
                (corner + 3 * square, backward_corner, 0, square),
            ]
        )


def window_kernel(rows, cols, parts, branch, reach, places, own_queries, own_sums, own_stats, *refs):
    halo, (modulation, weights) = refs[:parts], refs[parts : parts + 2]
    mine, theirs, gathered, normed, halo_kv, queries, sums, stats, whole, *refs = refs[-15:]
    halo_sums, halo_stats, buffer, sems, copy_sems, halo_sems = refs
    half, width = theirs.shape
    first = pl.ds(pl.multiple_of(branch[0] * half, half), half)
    second = pl.ds(pl.multiple_of((1 - branch[0]) * half, half), half)
    multiply = stream_project(normed, weights, width, buffer, sems, halo_kv)
    own_copies = [
        pltpu.make_async_copy(own_queries, queries, copy_sems.at[parts]),
        pltpu.make_async_copy(own_sums, sums, copy_sems.at[parts + 1]),
        pltpu.make_async_copy(own_stats, stats, copy_sems.at[parts + 4]),
    ]
    sends = [
        pltpu.make_async_copy(whole.at[first], mine, copy_sems.at[parts + 2]),
        pltpu.make_async_copy(whole.at[second], theirs, copy_sems.at[parts + 3]),
    ]
    for copy in own_copies:
        copy.start()
    row, col = places[0:1], places[1:2]
    limits = [jnp.where(branch[1 + side] != 0, reach[side], 0) for side in range(4)]
    allowed = (row >= -limits[0]) & (row < rows + limits[1])
    allowed = allowed & (col >= -limits[2]) & (col < cols + limits[3])
    bias = jnp.where(allowed, 0.0, -1e30).astype(F32)
    gather_halo(rows, cols, branch, halo, gathered, halo_sems)
    normed[...] = normalise(gathered[...], modulation[...])
    multiply()
    for copy in own_copies:
        copy.wait()
    keys, values = split_heads(halo_kv, width)
    attend_part(queries, keys, values, bias, halo_sums, halo_stats)
    merge_parts([(sums, stats), (halo_sums, halo_stats)], whole)
    for copy in sends:
        copy.start()
    for copy in sends:
        copy.wait()


def window(branch, reach, own, halo, modulation, wqkv, rows, cols, after):
    count, width = own[0].shape
    places = jnp.asarray(halo_places(rows, cols))
    halo_count = places.shape[1]
    half = (count // 2, width)
    return pl.pallas_call(
        functools.partial(window_kernel, rows, cols, len(halo)),
        in_specs=[SMEM, SMEM, VMEM, HBM, HBM, HBM] + [HBM] * len(halo) + [VMEM, HBM] + [HBM] * len(after),
        out_specs=[ANY, ANY],
        out_shape=[jax.ShapeDtypeStruct(half, BF16)] * 2,
        scratch_shapes=[
            pltpu.VMEM((halo_count, width), BF16),
            pltpu.VMEM((halo_count, width), BF16),
            pltpu.VMEM((halo_count, 2 * width), BF16),
            pltpu.VMEM((count, width), BF16),
            pltpu.VMEM((count, width), F32),
            pltpu.VMEM((count, 2 * LANES), F32),
            pltpu.VMEM((count, width), BF16),
            pltpu.VMEM((count, width), F32),
            pltpu.VMEM((count, 2 * LANES), F32),
        ]
        + weight_scratch(width, 2 * width)
        + [pltpu.SemaphoreType.DMA((len(halo) + 5,)), pltpu.SemaphoreType.DMA((7,))],
        compiler_params=pltpu.CompilerParams(vmem_limit_bytes=VMEM_LIMIT),
        cost_estimate=pl.CostEstimate(
            flops=4 * count * halo_count * width * 3 + 4 * halo_count * width * width,
            bytes_accessed=2 * (4 * count * width + 2 * halo_count * width + 2 * width * width),
            transcendentals=count * halo_count * HEADS,
        ),
        name="window",
    )(branch, reach, places, *[in_hbm(part) for part in own], *[in_hbm(part) for part in halo], modulation, wqkv, *after)


def finish_kernel(
    col_groups, branch, window_mine, window_theirs, tokens, tokens_theirs, returned, blend, gate, weights, out, *refs
):
    tokens_mine, raw, dilated, result, buffer, sems, out_sems = refs
    own_factor, other_factor = guidance(branch)
    count, width = dilated.shape
    columns = [slice(0, FIRST_COLUMNS), slice(FIRST_COLUMNS, width)]
    copies = [
        pltpu.make_async_copy(weights.at[:, place], buffer.at[:, place], sems.at[index])
        for index, place in enumerate(columns)
    ]
    sends = [
        pltpu.make_async_copy(result.at[:, place], out.at[:, place], out_sems.at[index])
        for index, place in enumerate(columns)
    ]
    mine = pl.ds(pl.multiple_of(branch[0] * count, count), count)
    arrival = pltpu.make_async_copy(tokens.at[mine], tokens_mine, sems.at[len(columns)])
    for copy in [arrival] + copies:
        copy.start()
    flat = returned[...].reshape(count, width)
    for tile, lanes in enumerate(lane_tiles(width)):
        raw[tile] = flat[:, lanes].astype(F32)
        for across in range(2):
            cells = raw[tile, pl.ds(across, count // 2, stride=2), :]
            for row in range(count // 2 // col_groups):
                start = col_groups * (2 * row + across)
                dilated[start : start + col_groups, lanes] = cells[col_groups * row : col_groups * (row + 1)]
    weight = blend[...]
    both = own_factor * window_mine[...].astype(F32) + other_factor * window_theirs[...].astype(F32)
    mixed = (weight * both + (1.0 - weight) * dilated[...]).astype(BF16)
    arrival.wait()
    for copy, send, place in zip(copies, sends, columns):
        kept = own_factor * tokens_mine[:, place].astype(F32) + other_factor * tokens_theirs[:, place].astype(F32)
        copy.wait()
        projected = jnp.dot(mixed, buffer[:, place], preferred_element_type=F32)
        result[:, place] = (kept + gate[:, place] * projected).astype(BF16)
        send.start()
    for send in sends:
        send.wait()


def finish(branch, window_mine, window_theirs, tokens, tokens_theirs, returned, blend, gate, w_out, col_groups):
    count, width = window_mine.shape
    return pl.pallas_call(
        functools.partial(finish_kernel, col_groups),
        in_specs=[SMEM, VMEM, VMEM, HBM] + [VMEM] * 4 + [HBM],
        out_specs=HBM,
        out_shape=jax.ShapeDtypeStruct((count, width), BF16),
        scratch_shapes=[
            pltpu.VMEM((count, width), BF16),
            pltpu.VMEM((width // LANES, count, LANES), F32),
            pltpu.VMEM((count, width), F32),
            pltpu.VMEM((count, width), BF16),
            pltpu.VMEM((width, width), BF16),
            pltpu.SemaphoreType.DMA((3,)),
            pltpu.SemaphoreType.DMA((2,)),
        ],
        compiler_params=pltpu.CompilerParams(vmem_limit_bytes=FINISH_LIMIT),
        cost_estimate=pl.CostEstimate(
            flops=2 * count * width * width,
            bytes_accessed=2 * (width * width + 6 * count * width),
            transcendentals=0,
        ),
        name="finish",
    )(branch, window_mine, window_theirs, tokens, tokens_theirs, returned, blend, gate, w_out)


def on_device(tokens, modulation, wqkv, w_out, blend, reach):
    tile = tokens[0]
    rows, cols, width = tile.shape
    row_groups = lax.axis_size("row")
    col_groups = lax.axis_size("col")
    sub_rows = rows // row_groups
    sub_cols = cols // col_groups
    half = rows // 2 * cols
    branch = lax.axis_index("branch")
    wqkv, w_out = in_hbm(wqkv), in_hbm(w_out)
    devices = row_groups * col_groups
    row, col = lax.axis_index("row"), lax.axis_index("col")
    inner = [row > 0, row < row_groups - 1, col > 0, col < col_groups - 1]
    place_of = jnp.stack([branch] + [side.astype(branch.dtype) for side in inner]).astype(jnp.int32)

    def other_core(cells):
        return lax.ppermute(cells, "branch", [(0, 1), (1, 0)])

    keep, send = edges(place_of, in_hbm(tile))
    received = other_core(send)
    outgoing = hold(pack(in_hbm(tile)), [received])
    arrived = lax.all_to_all(outgoing, ("row", "col"), split_axis=0, concat_axis=0, tiled=True)

    flat = tile.reshape(rows * cols, width)
    forward, backward, forward_corner, backward_corner = outbound(place_of, keep, received, rows, cols)
    halo = [
        across_tiles(forward, (1, 0), (0, 1)),
        across_tiles(backward, (-1, 0), (0, -1)),
        across_tiles(forward_corner, (1, 1), (1, -1)),
        across_tiles(backward_corner, (-1, -1), (-1, 1)),
    ]
    *own, tokens_send, mark = own_tile(place_of, flat, modulation, wqkv)
    tokens_theirs = other_core(tokens_send)

    lattice_mine, lattice_send = lattice(place_of, arrived, modulation, wqkv, [mark])
    passed = other_core(inbound(halo, lattice_mine))
    lattice_theirs = other_core(hold(lattice_send, halo))
    combined = combine(place_of, lattice_mine, lattice_theirs)
    returned = lax.all_to_all(combined, ("row", "col"), split_axis=0, concat_axis=0, tiled=True)

    window_mine, send = window(
        place_of, reach.reshape(4), own, halo + [passed], modulation, wqkv, rows, cols, [combined]
    )
    window_theirs = other_core(send)
    weight = lax.dynamic_index_in_dim(blend.reshape(2, half, 1), branch, 0, keepdims=False)
    guided = finish(
        place_of,
        window_mine,
        window_theirs,
        in_hbm(flat),
        tokens_theirs,
        returned,
        weight,
        modulation[2:3],
        w_out,
        col_groups,
    )
    return guided.reshape(rows // 2, cols, width)


def solution(mesh):
    in_specs = (
        P("branch", "row", "col", None),
        P(),
        P(),
        P(),
        P("row", "col"),
        P(None, "row", "col"),
    )
    out_specs = P(("row", "branch"), "col", None)
    return jax.shard_map(
        on_device, mesh=mesh, in_specs=in_specs, out_specs=out_specs, check_vma=False
    )
```

```python
import functools
import math

import jax
import jax.numpy as jnp
import numpy as np
from jax import lax
from jax.experimental import pallas as pl
from jax.experimental.pallas import tpu as pltpu
from jax.sharding import PartitionSpec as P

HEADS = 16
HALO = 4
GUIDANCE = 4.5
LANES = 128
VMEM_LIMIT = 28 * 1024 * 1024
SMALL_LIMIT = 4 * 1024 * 1024
FINISH_LIMIT = 16 * 1024 * 1024
PACK_LIMIT = 8 * 1024 * 1024
FIRST_COLUMNS = 640
CHUNK = 512
IN_FLIGHT = 3

F32 = jnp.float32
BF16 = jnp.bfloat16

VMEM = pl.BlockSpec(memory_space=pltpu.VMEM)
SMEM = pl.BlockSpec(memory_space=pltpu.SMEM)
ANY = pl.BlockSpec(memory_space=pl.ANY)
HBM = pl.BlockSpec(memory_space=pltpu.HBM)
MARK = jax.ShapeDtypeStruct((8, LANES), F32)


def in_hbm(array):
    return pltpu.with_memory_space_constraint(array, pltpu.HBM)


def normalise(tokens, modulation):
    widened = tokens.astype(F32)
    centered = widened - jnp.mean(widened, axis=-1, keepdims=True)
    variance = jnp.mean(centered * centered, axis=-1, keepdims=True)
    scaled = centered * lax.rsqrt(variance + 1e-06)
    return (scaled * (1.0 + modulation[1:2]) + modulation[0:1]).astype(BF16)


def head_window(head, head_size, width):
    first = head * head_size
    low = first // LANES * LANES
    high = min(-(-(first + head_size) // LANES) * LANES, width)
    return first, low, high


def head_lanes(head, width):
    head_size = width // HEADS
    first, low, high = head_window(head, head_size, width)
    lane = lax.broadcasted_iota(jnp.int32, (1, high - low), 1) + low
    inside = (lane >= first) & (lane < first + head_size)
    return slice(low, high), inside, 0 if first > low else head_size


def head_scores(place, inside, queries, keys):
    query = queries[:, place]
    query = jnp.where(inside, query, jnp.zeros_like(query))
    return lax.dot_general(query, keys[:, place], (((1,), (1,)), ((), ())), preferred_element_type=F32)


def weigh_values(place, inside, scores, top, values):
    powers = jnp.exp2(scores - top).astype(BF16)
    value = values[:, place]
    value = jnp.where(inside, value, jnp.ones_like(value))
    return jnp.dot(powers, value, preferred_element_type=F32)


def attend(queries, keys, values, out):
    width = queries.shape[-1]
    for head in range(HEADS):
        place, inside, spare = head_lanes(head, width)
        scores = head_scores(place, inside, queries, keys)
        top = jnp.max(scores, axis=-1, keepdims=True)
        total = weigh_values(place, inside, scores, top, values)
        attended = (total * (1.0 / total[:, spare : spare + 1])).astype(out.dtype)
        out[:, place] = jnp.where(inside, attended, out[:, place])


def attend_part(queries, keys, values, bias, sums, stats):
    width = queries.shape[-1]
    column = lax.broadcasted_iota(jnp.int32, (1, LANES), 1)
    stats[:, :LANES] = jnp.zeros_like(stats[:, :LANES])
    stats[:, LANES:] = jnp.ones_like(stats[:, LANES:])
    for head in range(HEADS):
        place, inside, spare = head_lanes(head, width)
        scores = head_scores(place, inside, queries, keys)
        if bias is not None:
            scores = scores + bias
        top = jnp.max(scores, axis=-1, keepdims=True)
        total = weigh_values(place, inside, scores, top, values)
        sums[:, place] = jnp.where(inside, total, sums[:, place])
        stats[:, :LANES] = jnp.where(column == head, top, stats[:, :LANES])
        stats[:, LANES:] = jnp.where(column == head, total[:, spare : spare + 1], stats[:, LANES:])


def merge_parts(parts, out):
    width = out.shape[-1]
    row = lax.broadcasted_iota(jnp.int32, (2 * LANES, width), 0) % LANES
    column = lax.broadcasted_iota(jnp.int32, (2 * LANES, width), 1)
    head_size = width // HEADS
    spread = ((column >= row * head_size) & (column < (row + 1) * head_size)).astype(F32).astype(BF16)
    tops = [stats[:, :LANES] for _, stats in parts]
    top = functools.reduce(jnp.maximum, tops)
    factors = [jnp.exp2(part_top - top) for part_top in tops]
    weight = sum(factor * stats[:, LANES:] for factor, (_, stats) in zip(factors, parts))
    total = None
    for factor, (sums, _) in zip(factors, parts):
        factor = factor * (1.0 / weight)
        high = factor.astype(BF16)
        low = (factor - high.astype(F32)).astype(BF16)
        wide = jnp.dot(jnp.concatenate([high, low], axis=1), spread, preferred_element_type=F32)
        part = sums[...] * wide
        total = part if total is None else total + part
    out[...] = total.astype(out.dtype)


def query_scale(feature_width):
    return math.log2(math.e) / math.sqrt(feature_width // HEADS)


def column_chunks(width):
    return [(start, min(CHUNK, width - start)) for start in range(0, width, CHUNK)]


def stream_project(normed, weights, first_column, buffer, sems, out, sends=()):
    width = normed.shape[-1]
    chunks = column_chunks(out.shape[-1])
    copies = [
        pltpu.make_async_copy(
            weights.at[:, first_column + start : first_column + start + size],
            buffer.at[:, start : start + size],
            sems.at[index],
        )
        for index, (start, size) in enumerate(chunks)
    ]
    for copy in copies[:IN_FLIGHT]:
        copy.start()

    def multiply():
        for index, (start, size) in enumerate(chunks):
            copies[index].wait()
            if index + IN_FLIGHT < len(chunks):
                copies[index + IN_FLIGHT].start()
            product = jnp.dot(normed[...], buffer[:, start : start + size], preferred_element_type=F32)
            if first_column + start < width:
                column = lax.broadcasted_iota(jnp.int32, (1, size), 1) + first_column + start
                product = product * jnp.where(column < width, query_scale(width), 1.0)
            out[:, start : start + size] = product.astype(BF16)
            if sends:
                sends[index].start()

    return multiply


def weight_scratch(width, columns):
    return [pltpu.VMEM((width, columns), BF16), pltpu.SemaphoreType.DMA((len(column_chunks(columns)),))]


def split_heads(qkv, width):
    return [qkv.at[:, start : start + width] for start in range(0, qkv.shape[-1], width)]


def pack_kernel(tile, outgoing, quarters, sems):
    _, height, breadth, width = quarters.shape
    copies = []
    for down in range(2):
        for across in range(2):
            index = 2 * down + across
            source = tile.at[
                height * down : height * (down + 1), breadth * across : breadth * (across + 1)
            ]
            copies.append(pltpu.make_async_copy(source, quarters.at[index], sems.at[index]))
            copies[-1].start()
    for index, copy in enumerate(copies):
        copy.wait()
        outgoing[:, index, :] = quarters[index].reshape(height * breadth, width)


def pack(tile):
    rows, cols, width = tile.shape
    return pl.pallas_call(
        pack_kernel,
        in_specs=[HBM],
        out_specs=VMEM,
        out_shape=jax.ShapeDtypeStruct((rows * cols // 4, 4, width), BF16),
        scratch_shapes=[
            pltpu.VMEM((4, rows // 2, cols // 2, width), BF16),
            pltpu.SemaphoreType.DMA((4,)),
        ],
        compiler_params=pltpu.CompilerParams(vmem_limit_bytes=PACK_LIMIT),
        cost_estimate=pl.CostEstimate(flops=0, bytes_accessed=4 * rows * cols * width, transcendentals=0),
        name="pack",
    )(tile)


def edge_scratch(tile):
    rows, cols, width = tile.shape
    return [
        pltpu.VMEM((HALO, cols, width), BF16),
        pltpu.VMEM((rows, 2 * HALO, width), BF16),
        pltpu.SemaphoreType.DMA((2,)),
    ]


def edge_sizes(rows, cols):
    return [HALO * cols, HALO * rows, HALO * HALO, HALO * HALO]


def write_edges(core, tile, targets, outer, inner, sems):
    rows, cols, width = tile.shape
    wide = 2 * HALO
    last = core == 0
    first_row = jnp.where(last, rows - HALO, 0)
    first_col = pl.multiple_of(jnp.where(last, cols - wide, 0), wide)
    copies = [
        pltpu.make_async_copy(tile.at[pl.ds(first_row, HALO)], outer, sems.at[0]),
        pltpu.make_async_copy(tile.at[:, pl.ds(first_col, wide)], inner, sems.at[1]),
    ]
    for copy in copies:
        copy.start()
    upper = lax.broadcasted_iota(jnp.int32, (wide, 1), 0) < HALO
    vertical, horizontal, near, far = targets

    def left_cells(one, two):
        return jnp.where(upper, one, pltpu.roll(two, HALO, 0))

    def right_cells(one, two):
        return jnp.where(upper, pltpu.roll(one, HALO, 0), two)

    for copy in copies:
        copy.wait()
    vertical[: HALO * cols] = outer[...].reshape(HALO * cols, width)
    for pair in range(rows // 2):
        cells = [inner[2 * pair + k].astype(F32) for k in range(2)]
        horizontal[wide * pair : wide * (pair + 1)] = jnp.where(
            last, right_cells(*cells), left_cells(*cells)
        ).astype(BF16)
    for pair in range(HALO // 2):
        place = slice(wide * pair, wide * (pair + 1))
        left = left_cells(*[outer[2 * pair + k, :wide].astype(F32) for k in range(2)])
        right = right_cells(*[outer[2 * pair + k, cols - wide :].astype(F32) for k in range(2)])
        near[place] = jnp.where(last, right, left).astype(BF16)
        far[place] = jnp.where(last, left, right).astype(BF16)


def edge_views(rows, cols, cells):
    views = []
    start = 0
    for size in edge_sizes(rows, cols):
        views.append(cells.at[start : start + size])
        start += size
    return views


def edges_kernel(place_of, tile, send, *scratch):
    rows, cols, _ = tile.shape
    write_edges(1 - place_of[0], tile, edge_views(rows, cols, send), *scratch)


def edges(place_of, tile):
    rows, cols, width = tile.shape
    shape = jax.ShapeDtypeStruct((sum(edge_sizes(rows, cols)), width), BF16)
    return pl.pallas_call(
        edges_kernel,
        in_specs=[SMEM, HBM],
        out_specs=VMEM,
        out_shape=shape,
        scratch_shapes=edge_scratch(tile),
        compiler_params=pltpu.CompilerParams(vmem_limit_bytes=PACK_LIMIT),
        cost_estimate=pl.CostEstimate(flops=0, bytes_accessed=4 * shape.size, transcendentals=0),
        name="edges",
    )(place_of, tile)


def outbound_kernel(place_of, tile, received, *refs):
    parts, scratch = refs[:4], refs[4:]
    rows, cols, _ = tile.shape
    for part, view in zip(parts, edge_views(rows, cols, received)):
        part[part.shape[0] // 2 :] = view[...]
    write_edges(place_of[0], tile, parts, *scratch)


def outbound(place_of, tile, received):
    rows, cols, width = tile.shape
    shapes = [jax.ShapeDtypeStruct((2 * size, width), BF16) for size in edge_sizes(rows, cols)]
    return pl.pallas_call(
        outbound_kernel,
        in_specs=[SMEM, HBM, VMEM],
        out_specs=[VMEM] * 4,
        out_shape=shapes,
        scratch_shapes=edge_scratch(tile),
        compiler_params=pltpu.CompilerParams(vmem_limit_bytes=PACK_LIMIT),
        cost_estimate=pl.CostEstimate(flops=0, bytes_accessed=8 * received.size, transcendentals=0),
        name="outbound",
    )(place_of, tile, received)


def across_tiles(cells, first_step, second_step):
    row_groups, col_groups = lax.axis_size("row"), lax.axis_size("col")
    pairs = []
    for core, (down, right) in enumerate((first_step, second_step)):
        for row in range(row_groups):
            for col in range(col_groups):
                to_row, to_col = row + down, col + right
                if 0 <= to_row < row_groups and 0 <= to_col < col_groups:
                    start = core * row_groups * col_groups
                    pairs.append((start + row * col_groups + col, start + to_row * col_groups + to_col))
    return lax.ppermute(cells, ("branch", "row", "col"), pairs)


def inbound_kernel(forward, backward, forward_corner, backward_corner, after, out):
    start = 0
    for part in (forward, backward, forward_corner, backward_corner):
        count = part.shape[0] // 2
        out[start : start + count] = part[count:]
        start += count


def inbound(parts, after):
    count = sum(part.shape[0] for part in parts) // 2
    shape = jax.ShapeDtypeStruct((count, parts[0].shape[1]), BF16)
    return pl.pallas_call(
        inbound_kernel,
        in_specs=[VMEM] * 4 + [ANY],
        out_specs=VMEM,
        out_shape=shape,
        compiler_params=pltpu.CompilerParams(vmem_limit_bytes=SMALL_LIMIT),
        cost_estimate=pl.CostEstimate(flops=0, bytes_accessed=4 * shape.size, transcendentals=0),
        name="inbound",
    )(*parts, after)


def hold_kernel(cells, *refs):
    pass


def hold(cells, after):
    return pl.pallas_call(
        hold_kernel,
        in_specs=[ANY] * (1 + len(after)),
        out_specs=ANY,
        out_shape=jax.ShapeDtypeStruct(cells.shape, cells.dtype),
        input_output_aliases={0: 0},
        compiler_params=pltpu.CompilerParams(vmem_limit_bytes=SMALL_LIMIT),
        name="hold",
    )(cells, *after)


def own_kernel(half, branch, tokens, modulation, weights, *refs):
    queries_out, sums_out, stats_out, tokens_send, mark, here, normed, qkv, sums, stats, buffer, sems, copy_sems = refs
    arrival = pltpu.make_async_copy(tokens, here, copy_sems.at[0])
    arrival.start()
    multiply = stream_project(normed, weights, 0, buffer, sems, qkv)
    mark[...] = jnp.zeros_like(mark)
    arrival.wait()
    queries, keys, values = split_heads(qkv, here.shape[1])
    other = pl.ds(pl.multiple_of((1 - branch[0]) * half, half), half)
    sends = [
        pltpu.make_async_copy(here.at[other], tokens_send, copy_sems.at[1]),
        pltpu.make_async_copy(queries, queries_out, copy_sems.at[2]),
        pltpu.make_async_copy(sums, sums_out, copy_sems.at[3]),
        pltpu.make_async_copy(stats, stats_out, copy_sems.at[4]),
    ]
    sends[0].start()
    normed[...] = normalise(here[...], modulation[...])
    multiply()
    sends[1].start()
    attend_part(queries, keys, values, None, sums, stats)
    sends[2].start()
    sends[3].start()
    for copy in sends:
        copy.wait()


def own_tile(branch, tokens, modulation, wqkv):
    count, width = tokens.shape
    columns = wqkv.shape[1]
    half = count // 2
    return pl.pallas_call(
        functools.partial(own_kernel, half),
        in_specs=[SMEM, HBM, VMEM, HBM],
        out_specs=[HBM, HBM, HBM, HBM, VMEM],
        out_shape=[
            pltpu.HBM((count, width), BF16),
            pltpu.HBM((count, width), F32),
            pltpu.HBM((count, 2 * LANES), F32),
            pltpu.HBM((half, width), BF16),
            MARK,
        ],
        scratch_shapes=[
            pltpu.VMEM((count, width), BF16),
            pltpu.VMEM((count, width), BF16),
            pltpu.VMEM((count, columns), BF16),
            pltpu.VMEM((count, width), F32),
            pltpu.VMEM((count, 2 * LANES), F32),
        ]
        + weight_scratch(width, columns)
        + [pltpu.SemaphoreType.DMA((5,))],
        compiler_params=pltpu.CompilerParams(vmem_limit_bytes=VMEM_LIMIT),
        cost_estimate=pl.CostEstimate(
            flops=2 * count * width * columns + 4 * count * count * width * 3,
            bytes_accessed=2 * (width * columns + 5 * count * width),
            transcendentals=count * count * HEADS,
        ),
        name="own_tile",
    )(branch, tokens, modulation, wqkv)


def lane_tiles(width):
    return [slice(start, start + LANES) for start in range(0, width, LANES)]


def lattice_kernel(branch, tokens, modulation, weights, *refs):
    mine, theirs, normed, qkv, whole, tiles, buffer, sems = refs[-8:]
    count, width = whole.shape
    multiply = stream_project(normed, weights, 0, buffer, sems, qkv)
    normed[...] = normalise(tokens[...].reshape(count, width), modulation[...])
    multiply()
    queries, keys, values = split_heads(qkv, width)
    attend(queries, keys, values, whole)
    sources = count // 4
    for tile, lanes in enumerate(lane_tiles(width)):
        tiles[tile] = whole[:, lanes].astype(F32)
        for target, half in ((theirs, 1 - branch[0]), (mine, branch[0])):
            for across in range(2):
                rows = pl.ds(2 * half + across, sources, stride=4)
                target[sources * across : sources * (across + 1), lanes] = tiles[tile, rows, :].astype(BF16)


def lattice(branch, tokens, modulation, wqkv, after):
    sources, per_source, width = tokens.shape
    count = sources * per_source
    columns = wqkv.shape[1]
    half = jax.ShapeDtypeStruct((count // 2, width), BF16)
    return pl.pallas_call(
        lattice_kernel,
        in_specs=[SMEM, VMEM, VMEM, HBM] + [ANY] * len(after),
        out_specs=[VMEM, VMEM],
        out_shape=[half, half],
        scratch_shapes=[
            pltpu.VMEM((count, width), BF16),
            pltpu.VMEM((count, columns), BF16),
            pltpu.VMEM((count, width), BF16),
            pltpu.VMEM((width // LANES, count, LANES), F32),
        ]
        + weight_scratch(width, columns),
        compiler_params=pltpu.CompilerParams(vmem_limit_bytes=VMEM_LIMIT),
        cost_estimate=pl.CostEstimate(flops=0, bytes_accessed=2 * count * width, transcendentals=0),
        name="lattice",
    )(branch, tokens, modulation, wqkv, *after)


def guidance(branch):
    conditional = branch[0] == 1
    return jnp.where(conditional, GUIDANCE, 1.0 - GUIDANCE), jnp.where(conditional, 1.0 - GUIDANCE, GUIDANCE)


def combine_kernel(branch, mine, theirs, out):
    own_factor, other_factor = guidance(branch)
    both = own_factor * mine[...].astype(F32) + other_factor * theirs[...].astype(F32)
    sources = out.shape[0]
    for across in range(2):
        out[:, across, :] = both[sources * across : sources * (across + 1)].astype(BF16)


def combine(branch, mine, theirs):
    count, width = mine.shape
    return pl.pallas_call(
        combine_kernel,
        in_specs=[SMEM, VMEM, VMEM],
        out_specs=VMEM,
        out_shape=jax.ShapeDtypeStruct((count // 2, 2, width), BF16),
        compiler_params=pltpu.CompilerParams(vmem_limit_bytes=SMALL_LIMIT),
        cost_estimate=pl.CostEstimate(flops=3 * mine.size, bytes_accessed=6 * mine.size, transcendentals=0),
        name="combine",
    )(branch, mine, theirs)


def halo_places(rows, cols):
    def block(first_row, height, first_col, breadth):
        row, col = np.mgrid[first_row : first_row + height, first_col : first_col + breadth]
        return np.stack([row.reshape(-1), col.reshape(-1)])

    blocks = [block(-HALO, HALO, 0, cols), block(0, rows, -HALO, HALO)]
    blocks += [block(-HALO, HALO, -HALO, HALO), block(-HALO, HALO, cols, HALO)]
    blocks += [block(rows, HALO, 0, cols), block(0, rows, cols, HALO)]
    blocks += [block(rows, HALO, cols, HALO), block(rows, HALO, -HALO, HALO)]
    return np.concatenate(blocks, axis=1).astype(np.int32)


def gather_halo(place_of, parts, gathered, sems):
    *parts, passed = parts
    count = passed.shape[0]
    rows = pl.ds(pl.multiple_of((1 - place_of[0]) * count, 2 * HALO), count)
    copies = [pltpu.make_async_copy(passed, gathered.at[rows], sems.at[len(parts)])]
    start = place_of[0] * count
    for index, part in enumerate(parts):
        size = part.shape[0] // 2
        rows = pl.ds(pl.multiple_of(start, 2 * HALO), size)
        copies.append(pltpu.make_async_copy(part.at[:size], gathered.at[rows], sems.at[index]))
        start += size
    return copies


def window_kernel(rows, cols, parts, branch, reach, places, own_queries, own_sums, own_stats, *refs):
    halo, (modulation, weights) = refs[:parts], refs[parts : parts + 2]
    mine, theirs, gathered, normed, halo_kv, queries, sums, stats, whole, *refs = refs[-15:]
    halo_sums, halo_stats, buffer, sems, copy_sems, halo_sems = refs
    half, width = theirs.shape
    first = pl.ds(pl.multiple_of(branch[0] * half, half), half)
    second = pl.ds(pl.multiple_of((1 - branch[0]) * half, half), half)
    arrivals = gather_halo(branch, halo, gathered, halo_sems)
    for copy in arrivals:
        copy.start()
    multiply = stream_project(normed, weights, width, buffer, sems, halo_kv)
    own_copies = [
        pltpu.make_async_copy(own_queries, queries, copy_sems.at[parts]),
        pltpu.make_async_copy(own_sums, sums, copy_sems.at[parts + 1]),
        pltpu.make_async_copy(own_stats, stats, copy_sems.at[parts + 4]),
    ]
    sends = [
        pltpu.make_async_copy(whole.at[first], mine, copy_sems.at[parts + 2]),
        pltpu.make_async_copy(whole.at[second], theirs, copy_sems.at[parts + 3]),
    ]
    for copy in own_copies:
        copy.start()
    row, col = places[0:1], places[1:2]
    limits = [jnp.where(branch[1 + side] != 0, reach[side], 0) for side in range(4)]
    allowed = (row >= -limits[0]) & (row < rows + limits[1])
    allowed = allowed & (col >= -limits[2]) & (col < cols + limits[3])
    bias = jnp.where(allowed, 0.0, -1e30).astype(F32)
    for copy in arrivals:
        copy.wait()
    normed[...] = normalise(gathered[...], modulation[...])
    multiply()
    for copy in own_copies:
        copy.wait()
    keys, values = split_heads(halo_kv, width)
    attend_part(queries, keys, values, bias, halo_sums, halo_stats)
    merge_parts([(sums, stats), (halo_sums, halo_stats)], whole)
    for copy in sends:
        copy.start()
    for copy in sends:
        copy.wait()


def window(branch, reach, own, halo, modulation, wqkv, rows, cols, after):
    count, width = own[0].shape
    places = jnp.asarray(halo_places(rows, cols))
    halo_count = places.shape[1]
    half = (count // 2, width)
    return pl.pallas_call(
        functools.partial(window_kernel, rows, cols, len(halo)),
        in_specs=[SMEM, SMEM, VMEM, HBM, HBM, HBM] + [HBM] * len(halo) + [VMEM, HBM] + [HBM] * len(after),
        out_specs=[ANY, ANY],
        out_shape=[jax.ShapeDtypeStruct(half, BF16)] * 2,
        scratch_shapes=[
            pltpu.VMEM((halo_count, width), BF16),
            pltpu.VMEM((halo_count, width), BF16),
            pltpu.VMEM((halo_count, 2 * width), BF16),
            pltpu.VMEM((count, width), BF16),
            pltpu.VMEM((count, width), F32),
            pltpu.VMEM((count, 2 * LANES), F32),
            pltpu.VMEM((count, width), BF16),
            pltpu.VMEM((count, width), F32),
            pltpu.VMEM((count, 2 * LANES), F32),
        ]
        + weight_scratch(width, 2 * width)
        + [pltpu.SemaphoreType.DMA((len(halo) + 5,)), pltpu.SemaphoreType.DMA((len(halo),))],
        compiler_params=pltpu.CompilerParams(vmem_limit_bytes=VMEM_LIMIT),
        cost_estimate=pl.CostEstimate(
            flops=4 * count * halo_count * width * 3 + 4 * halo_count * width * width,
            bytes_accessed=2 * (4 * count * width + 2 * halo_count * width + 2 * width * width),
            transcendentals=count * halo_count * HEADS,
        ),
        name="window",
    )(branch, reach, places, *[in_hbm(part) for part in own], *[in_hbm(part) for part in halo], modulation, wqkv, *after)


def finish_kernel(
    col_groups, branch, window_mine, window_theirs, tokens, tokens_theirs, returned, blend, gate, weights, out, *refs
):
    tokens_mine, raw, dilated, result, buffer, sems, out_sems = refs
    own_factor, other_factor = guidance(branch)
    count, width = dilated.shape
    columns = [slice(0, FIRST_COLUMNS), slice(FIRST_COLUMNS, width)]
    copies = [
        pltpu.make_async_copy(weights.at[:, place], buffer.at[:, place], sems.at[index])
        for index, place in enumerate(columns)
    ]
    sends = [
        pltpu.make_async_copy(result.at[:, place], out.at[:, place], out_sems.at[index])
        for index, place in enumerate(columns)
    ]
    mine = pl.ds(pl.multiple_of(branch[0] * count, count), count)
    arrival = pltpu.make_async_copy(tokens.at[mine], tokens_mine, sems.at[len(columns)])
    for copy in [arrival] + copies:
        copy.start()
    flat = returned[...].reshape(count, width)
    for tile, lanes in enumerate(lane_tiles(width)):
        raw[tile] = flat[:, lanes].astype(F32)
        for across in range(2):
            cells = raw[tile, pl.ds(across, count // 2, stride=2), :]
            for row in range(count // 2 // col_groups):
                start = col_groups * (2 * row + across)
                dilated[start : start + col_groups, lanes] = cells[col_groups * row : col_groups * (row + 1)]
    weight = blend[...]
    both = own_factor * window_mine[...].astype(F32) + other_factor * window_theirs[...].astype(F32)
    mixed = (weight * both + (1.0 - weight) * dilated[...]).astype(BF16)
    arrival.wait()
    for copy, send, place in zip(copies, sends, columns):
        kept = own_factor * tokens_mine[:, place].astype(F32) + other_factor * tokens_theirs[:, place].astype(F32)
        copy.wait()
        projected = jnp.dot(mixed, buffer[:, place], preferred_element_type=F32)
        result[:, place] = (kept + gate[:, place] * projected).astype(BF16)
        send.start()
    for send in sends:
        send.wait()


def finish(branch, window_mine, window_theirs, tokens, tokens_theirs, returned, blend, gate, w_out, col_groups):
    count, width = window_mine.shape
    return pl.pallas_call(
        functools.partial(finish_kernel, col_groups),
        in_specs=[SMEM, VMEM, VMEM, HBM] + [VMEM] * 4 + [HBM],
        out_specs=HBM,
        out_shape=jax.ShapeDtypeStruct((count, width), BF16),
        scratch_shapes=[
            pltpu.VMEM((count, width), BF16),
            pltpu.VMEM((width // LANES, count, LANES), F32),
            pltpu.VMEM((count, width), F32),
            pltpu.VMEM((count, width), BF16),
            pltpu.VMEM((width, width), BF16),
            pltpu.SemaphoreType.DMA((3,)),
            pltpu.SemaphoreType.DMA((2,)),
        ],
        compiler_params=pltpu.CompilerParams(vmem_limit_bytes=FINISH_LIMIT),
        cost_estimate=pl.CostEstimate(
            flops=2 * count * width * width,
            bytes_accessed=2 * (width * width + 6 * count * width),
            transcendentals=0,
        ),
        name="finish",
    )(branch, window_mine, window_theirs, tokens, tokens_theirs, returned, blend, gate, w_out)


def on_device(tokens, modulation, wqkv, w_out, blend, reach):
    tile = tokens[0]
    rows, cols, width = tile.shape
    row_groups = lax.axis_size("row")
    col_groups = lax.axis_size("col")
    sub_rows = rows // row_groups
    sub_cols = cols // col_groups
    half = rows // 2 * cols
    branch = lax.axis_index("branch")
    wqkv, w_out = in_hbm(wqkv), in_hbm(w_out)
    devices = row_groups * col_groups
    row, col = lax.axis_index("row"), lax.axis_index("col")
    inner = [row > 0, row < row_groups - 1, col > 0, col < col_groups - 1]
    place_of = jnp.stack([branch] + [side.astype(branch.dtype) for side in inner]).astype(jnp.int32)

    def other_core(cells):
        return lax.ppermute(cells, "branch", [(0, 1), (1, 0)])

    received = other_core(edges(place_of, in_hbm(tile)))
    outgoing = hold(pack(in_hbm(tile)), [received])
    arrived = lax.all_to_all(outgoing, ("row", "col"), split_axis=0, concat_axis=0, tiled=True)

    flat = tile.reshape(rows * cols, width)
    parts = outbound(place_of, in_hbm(tile), received)
    steps = (((1, 0), (-1, 0)), ((0, 1), (0, -1)), ((1, 1), (-1, -1)), ((1, -1), (-1, 1)))
    halo = [across_tiles(part, *step) for part, step in zip(parts, steps)]
    *own, tokens_send, mark = own_tile(place_of, flat, modulation, wqkv)
    tokens_theirs = other_core(tokens_send)

    lattice_mine, lattice_send = lattice(place_of, arrived, modulation, wqkv, [mark])
    passed = other_core(inbound(halo, lattice_mine))
    lattice_theirs = other_core(hold(lattice_send, halo))
    combined = combine(place_of, lattice_mine, lattice_theirs)
    returned = lax.all_to_all(combined, ("row", "col"), split_axis=0, concat_axis=0, tiled=True)

    window_mine, send = window(
        place_of, reach.reshape(4), own, halo + [passed], modulation, wqkv, rows, cols, [combined]
    )
    window_theirs = other_core(send)
    weight = lax.dynamic_index_in_dim(blend.reshape(2, half, 1), branch, 0, keepdims=False)
    guided = finish(
        place_of,
        window_mine,
        window_theirs,
        in_hbm(flat),
        tokens_theirs,
        returned,
        weight,
        modulation[2:3],
        w_out,
        col_groups,
    )
    return guided.reshape(rows // 2, cols, width)


def solution(mesh):
    in_specs = (
        P("branch", "row", "col", None),
        P(),
        P(),
        P(),
        P("row", "col"),
        P(None, "row", "col"),
    )
    out_specs = P(("row", "branch"), "col", None)
    return jax.shard_map(
        on_device, mesh=mesh, in_specs=in_specs, out_specs=out_specs, check_vma=False
    )
```

```python
import functools
import math

import jax
import jax.numpy as jnp
import numpy as np
from jax import lax
from jax.experimental import pallas as pl
from jax.experimental.pallas import tpu as pltpu
from jax.sharding import PartitionSpec as P

HEADS = 16
HALO = 4
GUIDANCE = 4.5
LANES = 128
VMEM_LIMIT = 28 * 1024 * 1024
SMALL_LIMIT = 4 * 1024 * 1024
FINISH_LIMIT = 16 * 1024 * 1024
PACK_LIMIT = 8 * 1024 * 1024
FIRST_COLUMNS = 640
FIRST_CHUNK = 512
SECOND_CHUNK = 1536
IN_FLIGHT = 2

F32 = jnp.float32
BF16 = jnp.bfloat16

VMEM = pl.BlockSpec(memory_space=pltpu.VMEM)
SMEM = pl.BlockSpec(memory_space=pltpu.SMEM)
ANY = pl.BlockSpec(memory_space=pl.ANY)
HBM = pl.BlockSpec(memory_space=pltpu.HBM)
MARK = jax.ShapeDtypeStruct((8, LANES), F32)


def in_hbm(array):
    return pltpu.with_memory_space_constraint(array, pltpu.HBM)


def normalise(tokens, modulation):
    widened = tokens.astype(F32)
    centered = widened - jnp.mean(widened, axis=-1, keepdims=True)
    variance = jnp.mean(centered * centered, axis=-1, keepdims=True)
    scaled = centered * lax.rsqrt(variance + 1e-06)
    return (scaled * (1.0 + modulation[1:2]) + modulation[0:1]).astype(BF16)


def head_window(head, head_size, width):
    first = head * head_size
    low = first // LANES * LANES
    high = min(-(-(first + head_size) // LANES) * LANES, width)
    return first, low, high


def head_lanes(head, width):
    head_size = width // HEADS
    first, low, high = head_window(head, head_size, width)
    lane = lax.broadcasted_iota(jnp.int32, (1, high - low), 1) + low
    inside = (lane >= first) & (lane < first + head_size)
    return slice(low, high), inside, 0 if first > low else head_size


def head_scores(place, inside, queries, keys):
    query = queries[:, place]
    query = jnp.where(inside, query, jnp.zeros_like(query))
    return lax.dot_general(query, keys[:, place], (((1,), (1,)), ((), ())), preferred_element_type=F32)


def weigh_values(place, inside, scores, top, values):
    powers = jnp.exp2(scores - top).astype(BF16)
    value = values[:, place]
    value = jnp.where(inside, value, jnp.ones_like(value))
    return jnp.dot(powers, value, preferred_element_type=F32)


def attend(queries, keys, values, out):
    width = queries.shape[-1]
    for head in range(HEADS):
        place, inside, spare = head_lanes(head, width)
        scores = head_scores(place, inside, queries, keys)
        top = jnp.max(scores, axis=-1, keepdims=True)
        total = weigh_values(place, inside, scores, top, values)
        attended = (total * (1.0 / total[:, spare : spare + 1])).astype(out.dtype)
        out[:, place] = jnp.where(inside, attended, out[:, place])


def attend_part(queries, keys, values, bias, sums, stats):
    width = queries.shape[-1]
    column = lax.broadcasted_iota(jnp.int32, (1, LANES), 1)
    stats[:, :LANES] = jnp.zeros_like(stats[:, :LANES])
    stats[:, LANES:] = jnp.ones_like(stats[:, LANES:])
    for head in range(HEADS):
        place, inside, spare = head_lanes(head, width)
        scores = head_scores(place, inside, queries, keys)
        if bias is not None:
            scores = scores + bias
        top = jnp.max(scores, axis=-1, keepdims=True)
        total = weigh_values(place, inside, scores, top, values)
        sums[:, place] = jnp.where(inside, total.astype(sums.dtype), sums[:, place])
        stats[:, :LANES] = jnp.where(column == head, top, stats[:, :LANES])
        stats[:, LANES:] = jnp.where(column == head, total[:, spare : spare + 1], stats[:, LANES:])


def merge_parts(parts, out):
    width = out.shape[-1]
    row = lax.broadcasted_iota(jnp.int32, (2 * LANES, width), 0) % LANES
    column = lax.broadcasted_iota(jnp.int32, (2 * LANES, width), 1)
    head_size = width // HEADS
    spread = ((column >= row * head_size) & (column < (row + 1) * head_size)).astype(F32).astype(BF16)
    tops = [stats[:, :LANES] for _, stats in parts]
    top = functools.reduce(jnp.maximum, tops)
    factors = [jnp.exp2(part_top - top) for part_top in tops]
    weight = sum(factor * stats[:, LANES:] for factor, (_, stats) in zip(factors, parts))
    total = None
    for factor, (sums, _) in zip(factors, parts):
        factor = factor * (1.0 / weight)
        high = factor.astype(BF16)
        low = (factor - high.astype(F32)).astype(BF16)
        wide = jnp.dot(jnp.concatenate([high, low], axis=1), spread, preferred_element_type=F32)
        part = sums[...].astype(F32) * wide
        total = part if total is None else total + part
    out[...] = total.astype(out.dtype)


def query_scale(feature_width):
    return math.log2(math.e) / math.sqrt(feature_width // HEADS)


def column_chunks(width):
    starts = [0, FIRST_CHUNK, SECOND_CHUNK, width]
    return [(start, end - start) for start, end in zip(starts, starts[1:])]


def stream_project(normed, weights, first_column, buffer, sems, out, sends=()):
    width = normed.shape[-1]
    chunks = column_chunks(out.shape[-1])
    copies = [
        pltpu.make_async_copy(
            weights.at[:, first_column + start : first_column + start + size],
            buffer.at[:, start : start + size],
            sems.at[index],
        )
        for index, (start, size) in enumerate(chunks)
    ]
    for copy in copies[:IN_FLIGHT]:
        copy.start()

    def multiply():
        for index, (start, size) in enumerate(chunks):
            copies[index].wait()
            if index + IN_FLIGHT < len(chunks):
                copies[index + IN_FLIGHT].start()
            product = jnp.dot(normed[...], buffer[:, start : start + size], preferred_element_type=F32)
            if first_column + start < width:
                column = lax.broadcasted_iota(jnp.int32, (1, size), 1) + first_column + start
                product = product * jnp.where(column < width, query_scale(width), 1.0)
            out[:, start : start + size] = product.astype(BF16)
            if sends:
                sends[index].start()

    return multiply


def weight_scratch(width, columns):
    return [pltpu.VMEM((width, columns), BF16), pltpu.SemaphoreType.DMA((len(column_chunks(columns)),))]


def split_heads(qkv, width):
    return [qkv.at[:, start : start + width] for start in range(0, qkv.shape[-1], width)]


def pack_kernel(tile, outgoing, quarters, sems):
    _, height, breadth, width = quarters.shape
    copies = []
    for down in range(2):
        for across in range(2):
            index = 2 * down + across
            source = tile.at[
                height * down : height * (down + 1), breadth * across : breadth * (across + 1)
            ]
            copies.append(pltpu.make_async_copy(source, quarters.at[index], sems.at[index]))
            copies[-1].start()
    for index, copy in enumerate(copies):
        copy.wait()
        outgoing[:, index, :] = quarters[index].reshape(height * breadth, width)


def pack(tile):
    rows, cols, width = tile.shape
    return pl.pallas_call(
        pack_kernel,
        in_specs=[HBM],
        out_specs=VMEM,
        out_shape=jax.ShapeDtypeStruct((rows * cols // 4, 4, width), BF16),
        scratch_shapes=[
            pltpu.VMEM((4, rows // 2, cols // 2, width), BF16),
            pltpu.SemaphoreType.DMA((4,)),
        ],
        compiler_params=pltpu.CompilerParams(vmem_limit_bytes=PACK_LIMIT),
        cost_estimate=pl.CostEstimate(flops=0, bytes_accessed=4 * rows * cols * width, transcendentals=0),
        name="pack",
    )(tile)


def edge_scratch(tile):
    rows, cols, width = tile.shape
    return [
        pltpu.VMEM((HALO, cols, width), BF16),
        pltpu.VMEM((rows, 2 * HALO, width), BF16),
        pltpu.SemaphoreType.DMA((2,)),
    ]


def edge_sizes(rows, cols):
    return [HALO * cols, HALO * rows, HALO * HALO, HALO * HALO]


def write_edges(core, tile, targets, outer, inner, sems):
    rows, cols, width = tile.shape
    wide = 2 * HALO
    last = core == 0
    first_row = jnp.where(last, rows - HALO, 0)
    first_col = pl.multiple_of(jnp.where(last, cols - wide, 0), wide)
    copies = [
        pltpu.make_async_copy(tile.at[pl.ds(first_row, HALO)], outer, sems.at[0]),
        pltpu.make_async_copy(tile.at[:, pl.ds(first_col, wide)], inner, sems.at[1]),
    ]
    for copy in copies:
        copy.start()
    upper = lax.broadcasted_iota(jnp.int32, (wide, 1), 0) < HALO
    vertical, horizontal, near, far = targets

    def left_cells(one, two):
        return jnp.where(upper, one, pltpu.roll(two, HALO, 0))

    def right_cells(one, two):
        return jnp.where(upper, pltpu.roll(one, HALO, 0), two)

    for copy in copies:
        copy.wait()
    vertical[: HALO * cols] = outer[...].reshape(HALO * cols, width)
    for pair in range(rows // 2):
        cells = [inner[2 * pair + k].astype(F32) for k in range(2)]
        horizontal[wide * pair : wide * (pair + 1)] = jnp.where(
            last, right_cells(*cells), left_cells(*cells)
        ).astype(BF16)
    for pair in range(HALO // 2):
        place = slice(wide * pair, wide * (pair + 1))
        left = left_cells(*[outer[2 * pair + k, :wide].astype(F32) for k in range(2)])
        right = right_cells(*[outer[2 * pair + k, cols - wide :].astype(F32) for k in range(2)])
        near[place] = jnp.where(last, right, left).astype(BF16)
        far[place] = jnp.where(last, left, right).astype(BF16)


def edge_views(rows, cols, cells):
    views = []
    start = 0
    for size in edge_sizes(rows, cols):
        views.append(cells.at[start : start + size])
        start += size
    return views


def edges_kernel(place_of, tile, send, *scratch):
    rows, cols, _ = tile.shape
    write_edges(1 - place_of[0], tile, edge_views(rows, cols, send), *scratch)


def edges(place_of, tile):
    rows, cols, width = tile.shape
    shape = jax.ShapeDtypeStruct((sum(edge_sizes(rows, cols)), width), BF16)
    return pl.pallas_call(
        edges_kernel,
        in_specs=[SMEM, HBM],
        out_specs=VMEM,
        out_shape=shape,
        scratch_shapes=edge_scratch(tile),
        compiler_params=pltpu.CompilerParams(vmem_limit_bytes=PACK_LIMIT),
        cost_estimate=pl.CostEstimate(flops=0, bytes_accessed=4 * shape.size, transcendentals=0),
        name="edges",
    )(place_of, tile)


def outbound_kernel(place_of, tile, received, *refs):
    parts, scratch = refs[:4], refs[4:]
    rows, cols, _ = tile.shape
    for part, view in zip(parts, edge_views(rows, cols, received)):
        part[part.shape[0] // 2 :] = view[...]
    write_edges(place_of[0], tile, parts, *scratch)


def outbound(place_of, tile, received):
    rows, cols, width = tile.shape
    shapes = [jax.ShapeDtypeStruct((2 * size, width), BF16) for size in edge_sizes(rows, cols)]
    return pl.pallas_call(
        outbound_kernel,
        in_specs=[SMEM, HBM, VMEM],
        out_specs=[VMEM] * 4,
        out_shape=shapes,
        scratch_shapes=edge_scratch(tile),
        compiler_params=pltpu.CompilerParams(vmem_limit_bytes=PACK_LIMIT),
        cost_estimate=pl.CostEstimate(flops=0, bytes_accessed=8 * received.size, transcendentals=0),
        name="outbound",
    )(place_of, tile, received)


def across_tiles(cells, first_step, second_step):
    row_groups, col_groups = lax.axis_size("row"), lax.axis_size("col")
    pairs = []
    for core, (down, right) in enumerate((first_step, second_step)):
        for row in range(row_groups):
            for col in range(col_groups):
                to_row, to_col = row + down, col + right
                if 0 <= to_row < row_groups and 0 <= to_col < col_groups:
                    start = core * row_groups * col_groups
                    pairs.append((start + row * col_groups + col, start + to_row * col_groups + to_col))
    return lax.ppermute(cells, ("branch", "row", "col"), pairs)


def inbound_kernel(forward, backward, forward_corner, backward_corner, after, out):
    start = 0
    for part in (forward, backward, forward_corner, backward_corner):
        count = part.shape[0] // 2
        out[start : start + count] = part[count:]
        start += count


def inbound(parts, after):
    count = sum(part.shape[0] for part in parts) // 2
    shape = jax.ShapeDtypeStruct((count, parts[0].shape[1]), BF16)
    return pl.pallas_call(
        inbound_kernel,
        in_specs=[VMEM] * 4 + [ANY],
        out_specs=VMEM,
        out_shape=shape,
        compiler_params=pltpu.CompilerParams(vmem_limit_bytes=SMALL_LIMIT),
        cost_estimate=pl.CostEstimate(flops=0, bytes_accessed=4 * shape.size, transcendentals=0),
        name="inbound",
    )(*parts, after)


def hold_kernel(cells, *refs):
    pass


def hold(cells, after):
    return pl.pallas_call(
        hold_kernel,
        in_specs=[ANY] * (1 + len(after)),
        out_specs=ANY,
        out_shape=jax.ShapeDtypeStruct(cells.shape, cells.dtype),
        input_output_aliases={0: 0},
        compiler_params=pltpu.CompilerParams(vmem_limit_bytes=SMALL_LIMIT),
        name="hold",
    )(cells, *after)


def own_kernel(half, branch, tokens, modulation, weights, *refs):
    queries_out, sums_out, stats_out, tokens_send, mark, here, normed, qkv, sums, stats, buffer, sems, copy_sems = refs
    arrival = pltpu.make_async_copy(tokens, here, copy_sems.at[0])
    arrival.start()
    multiply = stream_project(normed, weights, 0, buffer, sems, qkv)
    mark[...] = jnp.zeros_like(mark)
    arrival.wait()
    queries, keys, values = split_heads(qkv, here.shape[1])
    other = pl.ds(pl.multiple_of((1 - branch[0]) * half, half), half)
    sends = [
        pltpu.make_async_copy(here.at[other], tokens_send, copy_sems.at[1]),
        pltpu.make_async_copy(queries, queries_out, copy_sems.at[2]),
        pltpu.make_async_copy(sums, sums_out, copy_sems.at[3]),
        pltpu.make_async_copy(stats, stats_out, copy_sems.at[4]),
    ]
    sends[0].start()
    normed[...] = normalise(here[...], modulation[...])
    multiply()
    sends[1].start()
    attend_part(queries, keys, values, None, sums, stats)
    sends[2].start()
    sends[3].start()
    for copy in sends:
        copy.wait()


def own_tile(branch, tokens, modulation, wqkv):
    count, width = tokens.shape
    columns = wqkv.shape[1]
    half = count // 2
    return pl.pallas_call(
        functools.partial(own_kernel, half),
        in_specs=[SMEM, HBM, VMEM, HBM],
        out_specs=[HBM, HBM, HBM, HBM, VMEM],
        out_shape=[
            pltpu.HBM((count, width), BF16),
            pltpu.HBM((count, width), BF16),
            pltpu.HBM((count, 2 * LANES), F32),
            pltpu.HBM((half, width), BF16),
            MARK,
        ],
        scratch_shapes=[
            pltpu.VMEM((count, width), BF16),
            pltpu.VMEM((count, width), BF16),
            pltpu.VMEM((count, columns), BF16),
            pltpu.VMEM((count, width), BF16),
            pltpu.VMEM((count, 2 * LANES), F32),
        ]
        + weight_scratch(width, columns)
        + [pltpu.SemaphoreType.DMA((5,))],
        compiler_params=pltpu.CompilerParams(vmem_limit_bytes=VMEM_LIMIT),
        cost_estimate=pl.CostEstimate(
            flops=2 * count * width * columns + 4 * count * count * width * 3,
            bytes_accessed=2 * (width * columns + 5 * count * width),
            transcendentals=count * count * HEADS,
        ),
        name="own_tile",
    )(branch, tokens, modulation, wqkv)


def lane_tiles(width):
    return [slice(start, start + LANES) for start in range(0, width, LANES)]


def lattice_kernel(branch, tokens, modulation, weights, *refs):
    mine, theirs, normed, qkv, whole, tiles, buffer, sems = refs[-8:]
    count, width = whole.shape
    multiply = stream_project(normed, weights, 0, buffer, sems, qkv)
    normed[...] = normalise(tokens[...].reshape(count, width), modulation[...])
    multiply()
    queries, keys, values = split_heads(qkv, width)
    attend(queries, keys, values, whole)
    sources = count // 4
    for tile, lanes in enumerate(lane_tiles(width)):
        tiles[tile] = whole[:, lanes].astype(F32)
        for target, half in ((theirs, 1 - branch[0]), (mine, branch[0])):
            for across in range(2):
                rows = pl.ds(2 * half + across, sources, stride=4)
                target[sources * across : sources * (across + 1), lanes] = tiles[tile, rows, :].astype(BF16)


def lattice(branch, tokens, modulation, wqkv, after):
    sources, per_source, width = tokens.shape
    count = sources * per_source
    columns = wqkv.shape[1]
    half = jax.ShapeDtypeStruct((count // 2, width), BF16)
    return pl.pallas_call(
        lattice_kernel,
        in_specs=[SMEM, VMEM, VMEM, HBM] + [ANY] * len(after),
        out_specs=[VMEM, VMEM],
        out_shape=[half, half],
        scratch_shapes=[
            pltpu.VMEM((count, width), BF16),
            pltpu.VMEM((count, columns), BF16),
            pltpu.VMEM((count, width), BF16),
            pltpu.VMEM((width // LANES, count, LANES), F32),
        ]
        + weight_scratch(width, columns),
        compiler_params=pltpu.CompilerParams(vmem_limit_bytes=VMEM_LIMIT),
        cost_estimate=pl.CostEstimate(flops=0, bytes_accessed=2 * count * width, transcendentals=0),
        name="lattice",
    )(branch, tokens, modulation, wqkv, *after)


def guidance(branch):
    conditional = branch[0] == 1
    return jnp.where(conditional, GUIDANCE, 1.0 - GUIDANCE), jnp.where(conditional, 1.0 - GUIDANCE, GUIDANCE)


def combine_kernel(branch, mine, theirs, out):
    own_factor, other_factor = guidance(branch)
    both = own_factor * mine[...].astype(F32) + other_factor * theirs[...].astype(F32)
    sources = out.shape[0]
    for across in range(2):
        out[:, across, :] = both[sources * across : sources * (across + 1)].astype(BF16)


def combine(branch, mine, theirs):
    count, width = mine.shape
    return pl.pallas_call(
        combine_kernel,
        in_specs=[SMEM, VMEM, VMEM],
        out_specs=VMEM,
        out_shape=jax.ShapeDtypeStruct((count // 2, 2, width), BF16),
        compiler_params=pltpu.CompilerParams(vmem_limit_bytes=SMALL_LIMIT),
        cost_estimate=pl.CostEstimate(flops=3 * mine.size, bytes_accessed=6 * mine.size, transcendentals=0),
        name="combine",
    )(branch, mine, theirs)


def halo_places(rows, cols):
    def block(first_row, height, first_col, breadth):
        row, col = np.mgrid[first_row : first_row + height, first_col : first_col + breadth]
        return np.stack([row.reshape(-1), col.reshape(-1)])

    blocks = [block(-HALO, HALO, 0, cols), block(0, rows, -HALO, HALO)]
    blocks += [block(-HALO, HALO, -HALO, HALO), block(-HALO, HALO, cols, HALO)]
    blocks += [block(rows, HALO, 0, cols), block(0, rows, cols, HALO)]
    blocks += [block(rows, HALO, cols, HALO), block(rows, HALO, -HALO, HALO)]
    return np.concatenate(blocks, axis=1).astype(np.int32)


def gather_halo(place_of, parts, gathered, sems):
    *parts, passed = parts
    count = passed.shape[0]
    rows = pl.ds(pl.multiple_of((1 - place_of[0]) * count, 2 * HALO), count)
    copies = [pltpu.make_async_copy(passed, gathered.at[rows], sems.at[len(parts)])]
    start = place_of[0] * count
    for index, part in enumerate(parts):
        size = part.shape[0] // 2
        rows = pl.ds(pl.multiple_of(start, 2 * HALO), size)
        copies.append(pltpu.make_async_copy(part.at[:size], gathered.at[rows], sems.at[index]))
        start += size
    return copies


def window_kernel(rows, cols, parts, branch, reach, places, own_queries, own_sums, own_stats, *refs):
    halo, (modulation, weights) = refs[:parts], refs[parts : parts + 2]
    mine, theirs, gathered, normed, halo_kv, queries, sums, stats, whole, *refs = refs[-15:]
    halo_sums, halo_stats, buffer, sems, copy_sems, halo_sems = refs
    half, width = theirs.shape
    first = pl.ds(pl.multiple_of(branch[0] * half, half), half)
    second = pl.ds(pl.multiple_of((1 - branch[0]) * half, half), half)
    arrivals = gather_halo(branch, halo, gathered, halo_sems)
    for copy in arrivals:
        copy.start()
    multiply = stream_project(normed, weights, width, buffer, sems, halo_kv)
    own_copies = [
        pltpu.make_async_copy(own_queries, queries, copy_sems.at[parts]),
        pltpu.make_async_copy(own_sums, sums, copy_sems.at[parts + 1]),
        pltpu.make_async_copy(own_stats, stats, copy_sems.at[parts + 4]),
    ]
    sends = [
        pltpu.make_async_copy(whole.at[first], mine, copy_sems.at[parts + 2]),
        pltpu.make_async_copy(whole.at[second], theirs, copy_sems.at[parts + 3]),
    ]
    for copy in own_copies:
        copy.start()
    row, col = places[0:1], places[1:2]
    limits = [jnp.where(branch[1 + side] != 0, reach[side], 0) for side in range(4)]
    allowed = (row >= -limits[0]) & (row < rows + limits[1])
    allowed = allowed & (col >= -limits[2]) & (col < cols + limits[3])
    bias = jnp.where(allowed, 0.0, -1e30).astype(F32)
    for copy in arrivals:
        copy.wait()
    normed[...] = normalise(gathered[...], modulation[...])
    multiply()
    for copy in own_copies:
        copy.wait()
    keys, values = split_heads(halo_kv, width)
    attend_part(queries, keys, values, bias, halo_sums, halo_stats)
    merge_parts([(sums, stats), (halo_sums, halo_stats)], whole)
    for copy in sends:
        copy.start()
    for copy in sends:
        copy.wait()


def window(branch, reach, own, halo, modulation, wqkv, rows, cols, after):
    count, width = own[0].shape
    places = jnp.asarray(halo_places(rows, cols))
    halo_count = places.shape[1]
    half = (count // 2, width)
    return pl.pallas_call(
        functools.partial(window_kernel, rows, cols, len(halo)),
        in_specs=[SMEM, SMEM, VMEM, HBM, HBM, HBM] + [HBM] * (len(halo) - 1) + [ANY, VMEM, HBM] + [HBM] * len(after),
        out_specs=[ANY, ANY],
        out_shape=[jax.ShapeDtypeStruct(half, BF16)] * 2,
        scratch_shapes=[
            pltpu.VMEM((halo_count, width), BF16),
            pltpu.VMEM((halo_count, width), BF16),
            pltpu.VMEM((halo_count, 2 * width), BF16),
            pltpu.VMEM((count, width), BF16),
            pltpu.VMEM((count, width), BF16),
            pltpu.VMEM((count, 2 * LANES), F32),
            pltpu.VMEM((count, width), BF16),
            pltpu.VMEM((count, width), F32),
            pltpu.VMEM((count, 2 * LANES), F32),
        ]
        + weight_scratch(width, 2 * width)
        + [pltpu.SemaphoreType.DMA((len(halo) + 5,)), pltpu.SemaphoreType.DMA((len(halo),))],
        compiler_params=pltpu.CompilerParams(vmem_limit_bytes=VMEM_LIMIT),
        cost_estimate=pl.CostEstimate(
            flops=4 * count * halo_count * width * 3 + 4 * halo_count * width * width,
            bytes_accessed=2 * (4 * count * width + 2 * halo_count * width + 2 * width * width),
            transcendentals=count * halo_count * HEADS,
        ),
        name="window",
    )(branch, reach, places, *[in_hbm(part) for part in own], *[in_hbm(part) for part in halo[:-1]], halo[-1], modulation, wqkv, *after)


def finish_kernel(
    col_groups, branch, window_mine, window_theirs, tokens, tokens_theirs, returned, blend, gate, weights, out, *refs
):
    tokens_mine, raw, dilated, result, buffer, sems, out_sems = refs
    own_factor, other_factor = guidance(branch)
    count, width = dilated.shape
    columns = [slice(0, FIRST_COLUMNS), slice(FIRST_COLUMNS, width)]
    copies = [
        pltpu.make_async_copy(weights.at[:, place], buffer.at[:, place], sems.at[index])
        for index, place in enumerate(columns)
    ]
    sends = [
        pltpu.make_async_copy(result.at[:, place], out.at[:, place], out_sems.at[index])
        for index, place in enumerate(columns)
    ]
    mine = pl.ds(pl.multiple_of(branch[0] * count, count), count)
    arrival = pltpu.make_async_copy(tokens.at[mine], tokens_mine, sems.at[len(columns)])
    for copy in [arrival] + copies:
        copy.start()
    flat = returned[...].reshape(count, width)
    for tile, lanes in enumerate(lane_tiles(width)):
        raw[tile] = flat[:, lanes].astype(F32)
        for across in range(2):
            cells = raw[tile, pl.ds(across, count // 2, stride=2), :]
            for row in range(count // 2 // col_groups):
                start = col_groups * (2 * row + across)
                dilated[start : start + col_groups, lanes] = cells[col_groups * row : col_groups * (row + 1)]
    weight = blend[...]
    both = own_factor * window_mine[...].astype(F32) + other_factor * window_theirs[...].astype(F32)
    mixed = (weight * both + (1.0 - weight) * dilated[...]).astype(BF16)
    arrival.wait()
    for copy, send, place in zip(copies, sends, columns):
        kept = own_factor * tokens_mine[:, place].astype(F32) + other_factor * tokens_theirs[:, place].astype(F32)
        copy.wait()
        projected = jnp.dot(mixed, buffer[:, place], preferred_element_type=F32)
        result[:, place] = (kept + gate[:, place] * projected).astype(BF16)
        send.start()
    for send in sends:
        send.wait()


def finish(branch, window_mine, window_theirs, tokens, tokens_theirs, returned, blend, gate, w_out, col_groups):
    count, width = window_mine.shape
    return pl.pallas_call(
        functools.partial(finish_kernel, col_groups),
        in_specs=[SMEM, VMEM, VMEM, HBM] + [VMEM] * 4 + [HBM],
        out_specs=HBM,
        out_shape=jax.ShapeDtypeStruct((count, width), BF16),
        scratch_shapes=[
            pltpu.VMEM((count, width), BF16),
            pltpu.VMEM((width // LANES, count, LANES), F32),
            pltpu.VMEM((count, width), F32),
            pltpu.VMEM((count, width), BF16),
            pltpu.VMEM((width, width), BF16),
            pltpu.SemaphoreType.DMA((3,)),
            pltpu.SemaphoreType.DMA((2,)),
        ],
        compiler_params=pltpu.CompilerParams(vmem_limit_bytes=FINISH_LIMIT),
        cost_estimate=pl.CostEstimate(
            flops=2 * count * width * width,
            bytes_accessed=2 * (width * width + 6 * count * width),
            transcendentals=0,
        ),
        name="finish",
    )(branch, window_mine, window_theirs, tokens, tokens_theirs, returned, blend, gate, w_out)


def on_device(tokens, modulation, wqkv, w_out, blend, reach):
    tile = tokens[0]
    rows, cols, width = tile.shape
    row_groups = lax.axis_size("row")
    col_groups = lax.axis_size("col")
    sub_rows = rows // row_groups
    sub_cols = cols // col_groups
    half = rows // 2 * cols
    branch = lax.axis_index("branch")
    wqkv, w_out = in_hbm(wqkv), in_hbm(w_out)
    devices = row_groups * col_groups
    row, col = lax.axis_index("row"), lax.axis_index("col")
    inner = [row > 0, row < row_groups - 1, col > 0, col < col_groups - 1]
    place_of = jnp.stack([branch] + [side.astype(branch.dtype) for side in inner]).astype(jnp.int32)

    def other_core(cells):
        return lax.ppermute(cells, "branch", [(0, 1), (1, 0)])

    received = other_core(edges(place_of, in_hbm(tile)))
    outgoing = hold(pack(in_hbm(tile)), [received])
    arrived = lax.all_to_all(outgoing, ("row", "col"), split_axis=0, concat_axis=0, tiled=True)

    flat = tile.reshape(rows * cols, width)
    parts = outbound(place_of, in_hbm(tile), received)
    steps = (((1, 0), (-1, 0)), ((0, 1), (0, -1)), ((1, 1), (-1, -1)), ((1, -1), (-1, 1)))
    *own, tokens_send, mark = own_tile(place_of, flat, modulation, wqkv)
    parts = list(parts[:2]) + [hold(part, [mark]) for part in parts[2:]]
    halo = [across_tiles(part, *step) for part, step in zip(parts, steps)]
    tokens_theirs = other_core(tokens_send)

    lattice_mine, lattice_send = lattice(place_of, arrived, modulation, wqkv, [mark])
    passed = other_core(inbound(halo, lattice_mine))
    lattice_theirs = other_core(hold(lattice_send, halo))
    combined = combine(place_of, lattice_mine, lattice_theirs)
    returned = lax.all_to_all(combined, ("row", "col"), split_axis=0, concat_axis=0, tiled=True)

    window_mine, send = window(
        place_of, reach.reshape(4), own, halo + [passed], modulation, wqkv, rows, cols, [combined]
    )
    window_theirs = other_core(send)
    weight = lax.dynamic_index_in_dim(blend.reshape(2, half, 1), branch, 0, keepdims=False)
    guided = finish(
        place_of,
        window_mine,
        window_theirs,
        in_hbm(flat),
        tokens_theirs,
        returned,
        weight,
        modulation[2:3],
        w_out,
        col_groups,
    )
    return guided.reshape(rows // 2, cols, width)


def solution(mesh):
    in_specs = (
        P("branch", "row", "col", None),
        P(),
        P(),
        P(),
        P("row", "col"),
        P(None, "row", "col"),
    )
    out_specs = P(("row", "branch"), "col", None)
    return jax.shard_map(
        on_device, mesh=mesh, in_specs=in_specs, out_specs=out_specs, check_vma=False
    )
```

```python
import functools
import math

import jax
import jax.numpy as jnp
import numpy as np
from jax import lax
from jax.experimental import pallas as pl
from jax.experimental.pallas import tpu as pltpu
from jax.sharding import PartitionSpec as P

HEADS = 16
HALO = 4
GUIDANCE = 4.5
LANES = 128
VMEM_LIMIT = 28 * 1024 * 1024
SMALL_LIMIT = 4 * 1024 * 1024
FINISH_LIMIT = 16 * 1024 * 1024
PACK_LIMIT = 8 * 1024 * 1024
FIRST_COLUMNS = 640
FIRST_CHUNK = 512
SECOND_CHUNK = 1536
IN_FLIGHT = 2

F32 = jnp.float32
BF16 = jnp.bfloat16

VMEM = pl.BlockSpec(memory_space=pltpu.VMEM)
SMEM = pl.BlockSpec(memory_space=pltpu.SMEM)
ANY = pl.BlockSpec(memory_space=pl.ANY)
HBM = pl.BlockSpec(memory_space=pltpu.HBM)
MARK = jax.ShapeDtypeStruct((8, LANES), F32)


def in_hbm(array):
    return pltpu.with_memory_space_constraint(array, pltpu.HBM)


def normalise(tokens, modulation):
    widened = tokens.astype(F32)
    centered = widened - jnp.mean(widened, axis=-1, keepdims=True)
    variance = jnp.mean(centered * centered, axis=-1, keepdims=True)
    scaled = centered * lax.rsqrt(variance + 1e-06)
    if callable(modulation):
        modulation = modulation()
    return (scaled * (1.0 + modulation[1:2]) + modulation[0:1]).astype(BF16)


def head_window(head, head_size, width):
    first = head * head_size
    low = first // LANES * LANES
    high = min(-(-(first + head_size) // LANES) * LANES, width)
    return first, low, high


def head_lanes(head, width):
    head_size = width // HEADS
    first, low, high = head_window(head, head_size, width)
    lane = lax.broadcasted_iota(jnp.int32, (1, high - low), 1) + low
    inside = (lane >= first) & (lane < first + head_size)
    return slice(low, high), inside, 0 if first > low else head_size


def head_scores(place, inside, queries, keys):
    query = queries[:, place]
    query = jnp.where(inside, query, jnp.zeros_like(query))
    return lax.dot_general(query, keys[:, place], (((1,), (1,)), ((), ())), preferred_element_type=F32)


def weigh_values(place, inside, scores, top, values):
    powers = jnp.exp2(scores - top).astype(BF16)
    value = values[:, place]
    value = jnp.where(inside, value, jnp.ones_like(value))
    return jnp.dot(powers, value, preferred_element_type=F32)


def attend(queries, keys, values, out):
    width = queries.shape[-1]
    for head in range(HEADS):
        place, inside, spare = head_lanes(head, width)
        scores = head_scores(place, inside, queries, keys)
        top = jnp.max(scores, axis=-1, keepdims=True)
        total = weigh_values(place, inside, scores, top, values)
        attended = (total * (1.0 / total[:, spare : spare + 1])).astype(out.dtype)
        out[:, place] = jnp.where(inside, attended, out[:, place])


def attend_part(queries, keys, values, bias, sums, stats):
    width = queries.shape[-1]
    column = lax.broadcasted_iota(jnp.int32, (1, LANES), 1)
    stats[:, :LANES] = jnp.zeros_like(stats[:, :LANES])
    stats[:, LANES:] = jnp.ones_like(stats[:, LANES:])
    for head in range(HEADS):
        place, inside, spare = head_lanes(head, width)
        scores = head_scores(place, inside, queries, keys)
        if bias is not None:
            scores = scores + bias
        top = jnp.max(scores, axis=-1, keepdims=True)
        total = weigh_values(place, inside, scores, top, values)
        sums[:, place] = jnp.where(inside, total.astype(sums.dtype), sums[:, place])
        stats[:, :LANES] = jnp.where(column == head, top, stats[:, :LANES])
        stats[:, LANES:] = jnp.where(column == head, total[:, spare : spare + 1], stats[:, LANES:])


def merge_parts(parts, out):
    width = out.shape[-1]
    row = lax.broadcasted_iota(jnp.int32, (2 * LANES, width), 0) % LANES
    column = lax.broadcasted_iota(jnp.int32, (2 * LANES, width), 1)
    head_size = width // HEADS
    spread = ((column >= row * head_size) & (column < (row + 1) * head_size)).astype(F32).astype(BF16)
    tops = [stats[:, :LANES] for _, stats in parts]
    top = functools.reduce(jnp.maximum, tops)
    factors = [jnp.exp2(part_top - top) for part_top in tops]
    weight = sum(factor * stats[:, LANES:] for factor, (_, stats) in zip(factors, parts))
    total = None
    for factor, (sums, _) in zip(factors, parts):
        factor = factor * (1.0 / weight)
        high = factor.astype(BF16)
        low = (factor - high.astype(F32)).astype(BF16)
        wide = jnp.dot(jnp.concatenate([high, low], axis=1), spread, preferred_element_type=F32)
        part = sums[...].astype(F32) * wide
        total = part if total is None else total + part
    out[...] = total.astype(out.dtype)


def query_scale(feature_width):
    return math.log2(math.e) / math.sqrt(feature_width // HEADS)


def column_chunks(width):
    starts = [0, FIRST_CHUNK, SECOND_CHUNK, width]
    return [(start, end - start) for start, end in zip(starts, starts[1:])]


def stream_project(normed, weights, first_column, buffer, sems, out, sends=()):
    width = normed.shape[-1]
    chunks = column_chunks(out.shape[-1])
    copies = [
        pltpu.make_async_copy(
            weights.at[:, first_column + start : first_column + start + size],
            buffer.at[:, start : start + size],
            sems.at[index],
        )
        for index, (start, size) in enumerate(chunks)
    ]
    for copy in copies[:IN_FLIGHT]:
        copy.start()

    def multiply():
        for index, (start, size) in enumerate(chunks):
            copies[index].wait()
            if index + IN_FLIGHT < len(chunks):
                copies[index + IN_FLIGHT].start()
            product = jnp.dot(normed[...], buffer[:, start : start + size], preferred_element_type=F32)
            if first_column + start < width:
                column = lax.broadcasted_iota(jnp.int32, (1, size), 1) + first_column + start
                product = product * jnp.where(column < width, query_scale(width), 1.0)
            out[:, start : start + size] = product.astype(BF16)
            if sends:
                sends[index].start()

    return multiply


def weight_scratch(width, columns):
    return [pltpu.VMEM((width, columns), BF16), pltpu.SemaphoreType.DMA((len(column_chunks(columns)),))]


def split_heads(qkv, width):
    return [qkv.at[:, start : start + width] for start in range(0, qkv.shape[-1], width)]


def pack_kernel(tile, outgoing, quarters, sems):
    _, height, breadth, width = quarters.shape
    copies = []
    for down in range(2):
        for across in range(2):
            index = 2 * down + across
            source = tile.at[
                height * down : height * (down + 1), breadth * across : breadth * (across + 1)
            ]
            copies.append(pltpu.make_async_copy(source, quarters.at[index], sems.at[index]))
            copies[-1].start()
    for index, copy in enumerate(copies):
        copy.wait()
        outgoing[:, index, :] = quarters[index].reshape(height * breadth, width)


def pack(tile):
    rows, cols, width = tile.shape
    return pl.pallas_call(
        pack_kernel,
        in_specs=[HBM],
        out_specs=VMEM,
        out_shape=jax.ShapeDtypeStruct((rows * cols // 4, 4, width), BF16),
        scratch_shapes=[
            pltpu.VMEM((4, rows // 2, cols // 2, width), BF16),
            pltpu.SemaphoreType.DMA((4,)),
        ],
        compiler_params=pltpu.CompilerParams(vmem_limit_bytes=PACK_LIMIT),
        cost_estimate=pl.CostEstimate(flops=0, bytes_accessed=4 * rows * cols * width, transcendentals=0),
        name="pack",
    )(tile)


def edge_scratch(tile):
    rows, cols, width = tile.shape
    return [
        pltpu.VMEM((HALO, cols, width), BF16),
        pltpu.VMEM((rows, 2 * HALO, width), BF16),
        pltpu.SemaphoreType.DMA((2,)),
    ]


def edge_sizes(rows, cols):
    return [HALO * cols, HALO * rows, HALO * HALO, HALO * HALO]


def write_edges(core, tile, targets, outer, inner, sems):
    rows, cols, width = tile.shape
    wide = 2 * HALO
    last = core == 0
    first_row = jnp.where(last, rows - HALO, 0)
    first_col = pl.multiple_of(jnp.where(last, cols - wide, 0), wide)
    copies = [
        pltpu.make_async_copy(tile.at[pl.ds(first_row, HALO)], outer, sems.at[0]),
        pltpu.make_async_copy(tile.at[:, pl.ds(first_col, wide)], inner, sems.at[1]),
    ]
    for copy in copies:
        copy.start()
    upper = lax.broadcasted_iota(jnp.int32, (wide, 1), 0) < HALO
    vertical, horizontal, near, far = targets

    def left_cells(one, two):
        return jnp.where(upper, one, pltpu.roll(two, HALO, 0))

    def right_cells(one, two):
        return jnp.where(upper, pltpu.roll(one, HALO, 0), two)

    for copy in copies:
        copy.wait()
    vertical[: HALO * cols] = outer[...].reshape(HALO * cols, width)
    for pair in range(rows // 2):
        cells = [inner[2 * pair + k].astype(F32) for k in range(2)]
        horizontal[wide * pair : wide * (pair + 1)] = jnp.where(
            last, right_cells(*cells), left_cells(*cells)
        ).astype(BF16)
    for pair in range(HALO // 2):
        place = slice(wide * pair, wide * (pair + 1))
        left = left_cells(*[outer[2 * pair + k, :wide].astype(F32) for k in range(2)])
        right = right_cells(*[outer[2 * pair + k, cols - wide :].astype(F32) for k in range(2)])
        near[place] = jnp.where(last, right, left).astype(BF16)
        far[place] = jnp.where(last, left, right).astype(BF16)


def edge_views(rows, cols, cells):
    views = []
    start = 0
    for size in edge_sizes(rows, cols):
        views.append(cells.at[start : start + size])
        start += size
    return views


def edges_kernel(place_of, tile, send, *scratch):
    rows, cols, _ = tile.shape
    write_edges(1 - place_of[0], tile, edge_views(rows, cols, send), *scratch)


def edges(place_of, tile):
    rows, cols, width = tile.shape
    shape = jax.ShapeDtypeStruct((sum(edge_sizes(rows, cols)), width), BF16)
    return pl.pallas_call(
        edges_kernel,
        in_specs=[SMEM, HBM],
        out_specs=VMEM,
        out_shape=shape,
        scratch_shapes=edge_scratch(tile),
        compiler_params=pltpu.CompilerParams(vmem_limit_bytes=PACK_LIMIT),
        cost_estimate=pl.CostEstimate(flops=0, bytes_accessed=4 * shape.size, transcendentals=0),
        name="edges",
    )(place_of, tile)


def outbound_kernel(place_of, tile, received, *refs):
    parts, scratch = refs[:4], refs[4:]
    rows, cols, _ = tile.shape
    for part, view in zip(parts, edge_views(rows, cols, received)):
        part[part.shape[0] // 2 :] = view[...]
    write_edges(place_of[0], tile, parts, *scratch)


def outbound(place_of, tile, received):
    rows, cols, width = tile.shape
    shapes = [jax.ShapeDtypeStruct((2 * size, width), BF16) for size in edge_sizes(rows, cols)]
    return pl.pallas_call(
        outbound_kernel,
        in_specs=[SMEM, HBM, VMEM],
        out_specs=[VMEM] * 4,
        out_shape=shapes,
        scratch_shapes=edge_scratch(tile),
        compiler_params=pltpu.CompilerParams(vmem_limit_bytes=PACK_LIMIT),
        cost_estimate=pl.CostEstimate(flops=0, bytes_accessed=8 * received.size, transcendentals=0),
        name="outbound",
    )(place_of, tile, received)


def across_tiles(cells, first_step, second_step):
    row_groups, col_groups = lax.axis_size("row"), lax.axis_size("col")
    pairs = []
    for core, (down, right) in enumerate((first_step, second_step)):
        for row in range(row_groups):
            for col in range(col_groups):
                to_row, to_col = row + down, col + right
                if 0 <= to_row < row_groups and 0 <= to_col < col_groups:
                    start = core * row_groups * col_groups
                    pairs.append((start + row * col_groups + col, start + to_row * col_groups + to_col))
    return lax.ppermute(cells, ("branch", "row", "col"), pairs)


def inbound_kernel(forward, backward, forward_corner, backward_corner, after, out):
    start = 0
    for part in (forward, backward, forward_corner, backward_corner):
        count = part.shape[0] // 2
        out[start : start + count] = part[count:]
        start += count


def inbound(parts, after):
    count = sum(part.shape[0] for part in parts) // 2
    shape = jax.ShapeDtypeStruct((count, parts[0].shape[1]), BF16)
    return pl.pallas_call(
        inbound_kernel,
        in_specs=[VMEM] * 4 + [ANY],
        out_specs=VMEM,
        out_shape=shape,
        compiler_params=pltpu.CompilerParams(vmem_limit_bytes=SMALL_LIMIT),
        cost_estimate=pl.CostEstimate(flops=0, bytes_accessed=4 * shape.size, transcendentals=0),
        name="inbound",
    )(*parts, after)


def hold_kernel(cells, *refs):
    pass


def hold(cells, after):
    return pl.pallas_call(
        hold_kernel,
        in_specs=[ANY] * (1 + len(after)),
        out_specs=ANY,
        out_shape=jax.ShapeDtypeStruct(cells.shape, cells.dtype),
        input_output_aliases={0: 0},
        compiler_params=pltpu.CompilerParams(vmem_limit_bytes=SMALL_LIMIT),
        name="hold",
    )(cells, *after)


def own_kernel(half, branch, tokens, modulation, weights, *refs):
    queries_out, sums_out, stats_out, tokens_send, mark, here, normed, qkv, sums, stats, buffer, sems, copy_sems = refs
    arrival = pltpu.make_async_copy(tokens, here, copy_sems.at[0])
    arrival.start()
    multiply = stream_project(normed, weights, 0, buffer, sems, qkv)
    mark[...] = jnp.zeros_like(mark)
    arrival.wait()
    queries, keys, values = split_heads(qkv, here.shape[1])
    other = pl.ds(pl.multiple_of((1 - branch[0]) * half, half), half)
    sends = [
        pltpu.make_async_copy(here.at[other], tokens_send, copy_sems.at[1]),
        pltpu.make_async_copy(queries, queries_out, copy_sems.at[2]),
        pltpu.make_async_copy(sums, sums_out, copy_sems.at[3]),
        pltpu.make_async_copy(stats, stats_out, copy_sems.at[4]),
    ]
    sends[0].start()
    normed[...] = normalise(here[...], modulation[...])
    multiply()
    sends[1].start()
    attend_part(queries, keys, values, None, sums, stats)
    sends[2].start()
    sends[3].start()
    for copy in sends:
        copy.wait()


def own_tile(branch, tokens, modulation, wqkv):
    count, width = tokens.shape
    columns = wqkv.shape[1]
    half = count // 2
    return pl.pallas_call(
        functools.partial(own_kernel, half),
        in_specs=[SMEM, HBM, VMEM, HBM],
        out_specs=[HBM, HBM, HBM, HBM, VMEM],
        out_shape=[
            pltpu.HBM((count, width), BF16),
            pltpu.HBM((count, width), BF16),
            pltpu.HBM((count, 2 * LANES), F32),
            pltpu.HBM((half, width), BF16),
            MARK,
        ],
        scratch_shapes=[
            pltpu.VMEM((count, width), BF16),
            pltpu.VMEM((count, width), BF16),
            pltpu.VMEM((count, columns), BF16),
            pltpu.VMEM((count, width), BF16),
            pltpu.VMEM((count, 2 * LANES), F32),
        ]
        + weight_scratch(width, columns)
        + [pltpu.SemaphoreType.DMA((5,))],
        compiler_params=pltpu.CompilerParams(vmem_limit_bytes=VMEM_LIMIT),
        cost_estimate=pl.CostEstimate(
            flops=2 * count * width * columns + 4 * count * count * width * 3,
            bytes_accessed=2 * (width * columns + 5 * count * width),
            transcendentals=count * count * HEADS,
        ),
        name="own_tile",
    )(branch, tokens, modulation, wqkv)


def lane_tiles(width):
    return [slice(start, start + LANES) for start in range(0, width, LANES)]


def lattice_kernel(branch, tokens, modulation, weights, *refs):
    mine, theirs, normed, qkv, whole, tiles, buffer, sems, local, local_sem = refs[-10:]
    fetch = pltpu.make_async_copy(modulation, local, local_sem)
    fetch.start()
    count, width = whole.shape
    multiply = stream_project(normed, weights, 0, buffer, sems, qkv)
    def fetched():
        fetch.wait()
        return local[...]

    normed[...] = normalise(tokens[...].reshape(count, width), fetched)
    multiply()
    queries, keys, values = split_heads(qkv, width)
    attend(queries, keys, values, whole)
    sources = count // 4
    for tile, lanes in enumerate(lane_tiles(width)):
        tiles[tile] = whole[:, lanes].astype(F32)
        for target, half in ((theirs, 1 - branch[0]), (mine, branch[0])):
            for across in range(2):
                rows = pl.ds(2 * half + across, sources, stride=4)
                target[sources * across : sources * (across + 1), lanes] = tiles[tile, rows, :].astype(BF16)


def lattice(branch, tokens, modulation, wqkv, after):
    sources, per_source, width = tokens.shape
    count = sources * per_source
    columns = wqkv.shape[1]
    half = jax.ShapeDtypeStruct((count // 2, width), BF16)
    return pl.pallas_call(
        lattice_kernel,
        in_specs=[SMEM, VMEM, HBM, HBM] + [ANY] * len(after),
        out_specs=[VMEM, VMEM],
        out_shape=[half, half],
        scratch_shapes=[
            pltpu.VMEM((count, width), BF16),
            pltpu.VMEM((count, columns), BF16),
            pltpu.VMEM((count, width), BF16),
            pltpu.VMEM((width // LANES, count, LANES), F32),
        ]
        + weight_scratch(width, columns)
        + [pltpu.VMEM(modulation.shape, F32), pltpu.SemaphoreType.DMA],
        compiler_params=pltpu.CompilerParams(vmem_limit_bytes=VMEM_LIMIT),
        cost_estimate=pl.CostEstimate(flops=0, bytes_accessed=2 * count * width, transcendentals=0),
        name="lattice",
    )(branch, tokens, in_hbm(modulation), wqkv, *after)


def guidance(branch):
    conditional = branch[0] == 1
    return jnp.where(conditional, GUIDANCE, 1.0 - GUIDANCE), jnp.where(conditional, 1.0 - GUIDANCE, GUIDANCE)


def combine_kernel(branch, mine, theirs, out):
    own_factor, other_factor = guidance(branch)
    both = own_factor * mine[...].astype(F32) + other_factor * theirs[...].astype(F32)
    sources = out.shape[0]
    for across in range(2):
        out[:, across, :] = both[sources * across : sources * (across + 1)].astype(BF16)


def combine(branch, mine, theirs):
    count, width = mine.shape
    return pl.pallas_call(
        combine_kernel,
        in_specs=[SMEM, VMEM, VMEM],
        out_specs=VMEM,
        out_shape=jax.ShapeDtypeStruct((count // 2, 2, width), BF16),
        compiler_params=pltpu.CompilerParams(vmem_limit_bytes=SMALL_LIMIT),
        cost_estimate=pl.CostEstimate(flops=3 * mine.size, bytes_accessed=6 * mine.size, transcendentals=0),
        name="combine",
    )(branch, mine, theirs)


def halo_places(rows, cols):
    def block(first_row, height, first_col, breadth):
        row, col = np.mgrid[first_row : first_row + height, first_col : first_col + breadth]
        return np.stack([row.reshape(-1), col.reshape(-1)])

    blocks = [block(-HALO, HALO, 0, cols), block(0, rows, -HALO, HALO)]
    blocks += [block(-HALO, HALO, -HALO, HALO), block(-HALO, HALO, cols, HALO)]
    blocks += [block(rows, HALO, 0, cols), block(0, rows, cols, HALO)]
    blocks += [block(rows, HALO, cols, HALO), block(rows, HALO, -HALO, HALO)]
    return np.concatenate(blocks, axis=1).astype(np.int32)


def gather_halo(place_of, parts, gathered, sems):
    *parts, passed = parts
    count = passed.shape[0]
    rows = pl.ds(pl.multiple_of((1 - place_of[0]) * count, 2 * HALO), count)
    copies = [pltpu.make_async_copy(passed, gathered.at[rows], sems.at[len(parts)])]
    start = place_of[0] * count
    for index, part in enumerate(parts):
        size = part.shape[0] // 2
        rows = pl.ds(pl.multiple_of(start, 2 * HALO), size)
        copies.append(pltpu.make_async_copy(part.at[:size], gathered.at[rows], sems.at[index]))
        start += size
    return copies


def window_kernel(rows, cols, parts, branch, reach, places, own_queries, own_sums, own_stats, *refs):
    halo, (modulation, weights) = refs[:parts], refs[parts : parts + 2]
    mine, theirs, gathered, normed, halo_kv, queries, sums, stats, whole, *refs = refs[-15:]
    halo_sums, halo_stats, buffer, sems, copy_sems, halo_sems = refs
    half, width = theirs.shape
    first = pl.ds(pl.multiple_of(branch[0] * half, half), half)
    second = pl.ds(pl.multiple_of((1 - branch[0]) * half, half), half)
    arrivals = gather_halo(branch, halo, gathered, halo_sems)
    for copy in arrivals:
        copy.start()
    multiply = stream_project(normed, weights, width, buffer, sems, halo_kv)
    own_copies = [
        pltpu.make_async_copy(own_queries, queries, copy_sems.at[parts]),
        pltpu.make_async_copy(own_sums, sums, copy_sems.at[parts + 1]),
        pltpu.make_async_copy(own_stats, stats, copy_sems.at[parts + 4]),
    ]
    sends = [
        pltpu.make_async_copy(whole.at[first], mine, copy_sems.at[parts + 2]),
        pltpu.make_async_copy(whole.at[second], theirs, copy_sems.at[parts + 3]),
    ]
    for copy in own_copies:
        copy.start()
    row, col = places[0:1], places[1:2]
    limits = [jnp.where(branch[1 + side] != 0, reach[side], 0) for side in range(4)]
    allowed = (row >= -limits[0]) & (row < rows + limits[1])
    allowed = allowed & (col >= -limits[2]) & (col < cols + limits[3])
    bias = jnp.where(allowed, 0.0, -1e30).astype(F32)
    for copy in arrivals:
        copy.wait()
    normed[...] = normalise(gathered[...], modulation[...])
    multiply()
    for copy in own_copies:
        copy.wait()
    keys, values = split_heads(halo_kv, width)
    attend_part(queries, keys, values, bias, halo_sums, halo_stats)
    merge_parts([(sums, stats), (halo_sums, halo_stats)], whole)
    for copy in sends:
        copy.start()
    for copy in sends:
        copy.wait()


def window(branch, reach, own, halo, modulation, wqkv, rows, cols, after):
    count, width = own[0].shape
    places = jnp.asarray(halo_places(rows, cols))
    halo_count = places.shape[1]
    half = (count // 2, width)
    return pl.pallas_call(
        functools.partial(window_kernel, rows, cols, len(halo)),
        in_specs=[SMEM, SMEM, VMEM, HBM, HBM, HBM] + [HBM] * (len(halo) - 1) + [ANY, VMEM, HBM] + [HBM] * len(after),
        out_specs=[ANY, ANY],
        out_shape=[jax.ShapeDtypeStruct(half, BF16)] * 2,
        scratch_shapes=[
            pltpu.VMEM((halo_count, width), BF16),
            pltpu.VMEM((halo_count, width), BF16),
            pltpu.VMEM((halo_count, 2 * width), BF16),
            pltpu.VMEM((count, width), BF16),
            pltpu.VMEM((count, width), BF16),
            pltpu.VMEM((count, 2 * LANES), F32),
            pltpu.VMEM((count, width), BF16),
            pltpu.VMEM((count, width), F32),
            pltpu.VMEM((count, 2 * LANES), F32),
        ]
        + weight_scratch(width, 2 * width)
        + [pltpu.SemaphoreType.DMA((len(halo) + 5,)), pltpu.SemaphoreType.DMA((len(halo),))],
        compiler_params=pltpu.CompilerParams(vmem_limit_bytes=VMEM_LIMIT),
        cost_estimate=pl.CostEstimate(
            flops=4 * count * halo_count * width * 3 + 4 * halo_count * width * width,
            bytes_accessed=2 * (4 * count * width + 2 * halo_count * width + 2 * width * width),
            transcendentals=count * halo_count * HEADS,
        ),
        name="window",
    )(branch, reach, places, *[in_hbm(part) for part in own], *[in_hbm(part) for part in halo[:-1]], halo[-1], modulation, wqkv, *after)


def finish_kernel(
    col_groups, branch, window_mine, window_theirs, tokens, tokens_theirs, returned, blend, gate, weights, out, *refs
):
    tokens_mine, raw, dilated, result, buffer, sems, out_sems = refs
    own_factor, other_factor = guidance(branch)
    count, width = dilated.shape
    columns = [slice(0, FIRST_COLUMNS), slice(FIRST_COLUMNS, width)]
    copies = [
        pltpu.make_async_copy(weights.at[:, place], buffer.at[:, place], sems.at[index])
        for index, place in enumerate(columns)
    ]
    sends = [
        pltpu.make_async_copy(result.at[:, place], out.at[:, place], out_sems.at[index])
        for index, place in enumerate(columns)
    ]
    mine = pl.ds(pl.multiple_of(branch[0] * count, count), count)
    arrival = pltpu.make_async_copy(tokens.at[mine], tokens_mine, sems.at[len(columns)])
    for copy in [arrival] + copies:
        copy.start()
    flat = returned[...].reshape(count, width)
    for tile, lanes in enumerate(lane_tiles(width)):
        raw[tile] = flat[:, lanes].astype(F32)
        for across in range(2):
            cells = raw[tile, pl.ds(across, count // 2, stride=2), :]
            for row in range(count // 2 // col_groups):
                start = col_groups * (2 * row + across)
                dilated[start : start + col_groups, lanes] = cells[col_groups * row : col_groups * (row + 1)]
    weight = blend[...]
    both = own_factor * window_mine[...].astype(F32) + other_factor * window_theirs[...].astype(F32)
    mixed = (weight * both + (1.0 - weight) * dilated[...]).astype(BF16)
    arrival.wait()
    for copy, send, place in zip(copies, sends, columns):
        kept = own_factor * tokens_mine[:, place].astype(F32) + other_factor * tokens_theirs[:, place].astype(F32)
        copy.wait()
        projected = jnp.dot(mixed, buffer[:, place], preferred_element_type=F32)
        result[:, place] = (kept + gate[:, place] * projected).astype(BF16)
        send.start()
    for send in sends:
        send.wait()


def finish(branch, window_mine, window_theirs, tokens, tokens_theirs, returned, blend, gate, w_out, col_groups):
    count, width = window_mine.shape
    return pl.pallas_call(
        functools.partial(finish_kernel, col_groups),
        in_specs=[SMEM, VMEM, VMEM, HBM] + [VMEM] * 4 + [HBM],
        out_specs=HBM,
        out_shape=jax.ShapeDtypeStruct((count, width), BF16),
        scratch_shapes=[
            pltpu.VMEM((count, width), BF16),
            pltpu.VMEM((width // LANES, count, LANES), F32),
            pltpu.VMEM((count, width), F32),
            pltpu.VMEM((count, width), BF16),
            pltpu.VMEM((width, width), BF16),
            pltpu.SemaphoreType.DMA((3,)),
            pltpu.SemaphoreType.DMA((2,)),
        ],
        compiler_params=pltpu.CompilerParams(vmem_limit_bytes=FINISH_LIMIT),
        cost_estimate=pl.CostEstimate(
            flops=2 * count * width * width,
            bytes_accessed=2 * (width * width + 6 * count * width),
            transcendentals=0,
        ),
        name="finish",
    )(branch, window_mine, window_theirs, tokens, tokens_theirs, returned, blend, gate, w_out)


def on_device(tokens, modulation, wqkv, w_out, blend, reach):
    tile = tokens[0]
    rows, cols, width = tile.shape
    row_groups = lax.axis_size("row")
    col_groups = lax.axis_size("col")
    sub_rows = rows // row_groups
    sub_cols = cols // col_groups
    half = rows // 2 * cols
    branch = lax.axis_index("branch")
    wqkv, w_out = in_hbm(wqkv), in_hbm(w_out)
    devices = row_groups * col_groups
    row, col = lax.axis_index("row"), lax.axis_index("col")
    inner = [row > 0, row < row_groups - 1, col > 0, col < col_groups - 1]
    place_of = jnp.stack([branch] + [side.astype(branch.dtype) for side in inner]).astype(jnp.int32)

    def other_core(cells):
        return lax.ppermute(cells, "branch", [(0, 1), (1, 0)])

    received = other_core(edges(place_of, in_hbm(tile)))
    outgoing = hold(pack(in_hbm(tile)), [received])
    arrived = lax.all_to_all(outgoing, ("col", "row"), split_axis=0, concat_axis=0, tiled=True)

    flat = tile.reshape(rows * cols, width)
    parts = outbound(place_of, in_hbm(tile), received)
    steps = (((1, 0), (-1, 0)), ((0, 1), (0, -1)), ((1, 1), (-1, -1)), ((1, -1), (-1, 1)))
    *own, tokens_send, mark = own_tile(place_of, flat, modulation, wqkv)
    parts = list(parts[:2]) + [hold(part, [mark]) for part in parts[2:]]
    halo = [across_tiles(part, *step) for part, step in zip(parts, steps)]
    tokens_theirs = other_core(tokens_send)

    lattice_mine, lattice_send = lattice(place_of, arrived, modulation, wqkv, [mark])
    passed = other_core(inbound(halo, lattice_mine))
    lattice_theirs = other_core(hold(lattice_send, halo))
    combined = combine(place_of, lattice_mine, lattice_theirs)
    returned = lax.all_to_all(combined, ("col", "row"), split_axis=0, concat_axis=0, tiled=True)

    window_mine, send = window(
        place_of, reach.reshape(4), own, halo + [passed], modulation, wqkv, rows, cols, [combined]
    )
    window_theirs = other_core(send)
    weight = lax.dynamic_index_in_dim(blend.reshape(2, half, 1), branch, 0, keepdims=False)
    guided = finish(
        place_of,
        window_mine,
        window_theirs,
        in_hbm(flat),
        tokens_theirs,
        returned,
        weight,
        modulation[2:3],
        w_out,
        col_groups,
    )
    return guided.reshape(rows // 2, cols, width)


def solution(mesh):
    in_specs = (
        P("branch", "row", "col", None),
        P(),
        P(),
        P(),
        P("row", "col"),
        P(None, "row", "col"),
    )
    out_specs = P(("row", "branch"), "col", None)
    return jax.shard_map(
        on_device, mesh=mesh, in_specs=in_specs, out_specs=out_specs, check_vma=False
    )
```

```python
import functools
import math

import jax
import jax.numpy as jnp
import numpy as np
from jax import lax
from jax.experimental import pallas as pl
from jax.experimental.pallas import tpu as pltpu
from jax.sharding import PartitionSpec as P

HEADS = 16
HALO = 4
GUIDANCE = 4.5
LANES = 128
VMEM_LIMIT = 28 * 1024 * 1024
SMALL_LIMIT = 4 * 1024 * 1024
FINISH_LIMIT = 16 * 1024 * 1024
PACK_LIMIT = 8 * 1024 * 1024
FIRST_COLUMNS = 640
FIRST_CHUNK = 512
SECOND_CHUNK = 1536
IN_FLIGHT = 2

F32 = jnp.float32
BF16 = jnp.bfloat16

VMEM = pl.BlockSpec(memory_space=pltpu.VMEM)
SMEM = pl.BlockSpec(memory_space=pltpu.SMEM)
ANY = pl.BlockSpec(memory_space=pl.ANY)
HBM = pl.BlockSpec(memory_space=pltpu.HBM)
MARK = jax.ShapeDtypeStruct((8, LANES), F32)


def in_hbm(array):
    return pltpu.with_memory_space_constraint(array, pltpu.HBM)


def normalise(tokens, modulation):
    widened = tokens.astype(F32)
    centered = widened - jnp.mean(widened, axis=-1, keepdims=True)
    variance = jnp.mean(centered * centered, axis=-1, keepdims=True)
    scaled = centered * lax.rsqrt(variance + 1e-06)
    if callable(modulation):
        modulation = modulation()
    return (scaled * (1.0 + modulation[1:2]) + modulation[0:1]).astype(BF16)


def head_window(head, head_size, width):
    first = head * head_size
    low = first // LANES * LANES
    high = min(-(-(first + head_size) // LANES) * LANES, width)
    return first, low, high


def head_lanes(head, width):
    head_size = width // HEADS
    first, low, high = head_window(head, head_size, width)
    lane = lax.broadcasted_iota(jnp.int32, (1, high - low), 1) + low
    inside = (lane >= first) & (lane < first + head_size)
    return slice(low, high), inside, 0 if first > low else head_size


def head_scores(place, inside, queries, keys):
    query = queries[:, place]
    query = jnp.where(inside, query, jnp.zeros_like(query))
    return lax.dot_general(query, keys[:, place], (((1,), (1,)), ((), ())), preferred_element_type=F32)


def weigh_values(place, inside, scores, top, values):
    powers = jnp.exp2(scores - top).astype(BF16)
    value = values[:, place]
    value = jnp.where(inside, value, jnp.ones_like(value))
    return jnp.dot(powers, value, preferred_element_type=F32)


def attend(queries, keys, values, out):
    width = queries.shape[-1]
    for head in range(HEADS):
        place, inside, spare = head_lanes(head, width)
        scores = head_scores(place, inside, queries, keys)
        top = jnp.max(scores, axis=-1, keepdims=True)
        total = weigh_values(place, inside, scores, top, values)
        attended = (total * (1.0 / total[:, spare : spare + 1])).astype(out.dtype)
        out[:, place] = jnp.where(inside, attended, out[:, place])


def attend_part(queries, keys, values, bias, sums, stats):
    width = queries.shape[-1]
    column = lax.broadcasted_iota(jnp.int32, (1, LANES), 1)
    stats[:, :LANES] = jnp.zeros_like(stats[:, :LANES])
    stats[:, LANES:] = jnp.ones_like(stats[:, LANES:])
    for head in range(HEADS):
        place, inside, spare = head_lanes(head, width)
        scores = head_scores(place, inside, queries, keys)
        if bias is not None:
            scores = scores + bias
        top = jnp.max(scores, axis=-1, keepdims=True)
        total = weigh_values(place, inside, scores, top, values)
        sums[:, place] = jnp.where(inside, total.astype(sums.dtype), sums[:, place])
        stats[:, :LANES] = jnp.where(column == head, top, stats[:, :LANES])
        stats[:, LANES:] = jnp.where(column == head, total[:, spare : spare + 1], stats[:, LANES:])


def merge_parts(parts, out):
    width = out.shape[-1]
    row = lax.broadcasted_iota(jnp.int32, (2 * LANES, width), 0) % LANES
    column = lax.broadcasted_iota(jnp.int32, (2 * LANES, width), 1)
    head_size = width // HEADS
    spread = ((column >= row * head_size) & (column < (row + 1) * head_size)).astype(F32).astype(BF16)
    tops = [stats[:, :LANES] for _, stats in parts]
    top = functools.reduce(jnp.maximum, tops)
    factors = [jnp.exp2(part_top - top) for part_top in tops]
    weight = sum(factor * stats[:, LANES:] for factor, (_, stats) in zip(factors, parts))
    total = None
    for factor, (sums, _) in zip(factors, parts):
        factor = factor * (1.0 / weight)
        high = factor.astype(BF16)
        low = (factor - high.astype(F32)).astype(BF16)
        wide = jnp.dot(jnp.concatenate([high, low], axis=1), spread, preferred_element_type=F32)
        part = sums[...].astype(F32) * wide
        total = part if total is None else total + part
    out[...] = total.astype(out.dtype)


def query_scale(feature_width):
    return math.log2(math.e) / math.sqrt(feature_width // HEADS)


def column_chunks(width):
    starts = [0, FIRST_CHUNK, SECOND_CHUNK, width]
    return [(start, end - start) for start, end in zip(starts, starts[1:])]


def stream_project(normed, weights, first_column, buffer, sems, out, sends=()):
    width = normed.shape[-1]
    chunks = column_chunks(out.shape[-1])
    copies = [
        pltpu.make_async_copy(
            weights.at[:, first_column + start : first_column + start + size],
            buffer.at[:, start : start + size],
            sems.at[index],
        )
        for index, (start, size) in enumerate(chunks)
    ]
    for copy in copies[:IN_FLIGHT]:
        copy.start()

    def multiply():
        for index, (start, size) in enumerate(chunks):
            copies[index].wait()
            if index + IN_FLIGHT < len(chunks):
                copies[index + IN_FLIGHT].start()
            product = jnp.dot(normed[...], buffer[:, start : start + size], preferred_element_type=F32)
            if first_column + start < width:
                column = lax.broadcasted_iota(jnp.int32, (1, size), 1) + first_column + start
                product = product * jnp.where(column < width, query_scale(width), 1.0)
            out[:, start : start + size] = product.astype(BF16)
            if sends:
                sends[index].start()

    return multiply


def weight_scratch(width, columns):
    return [pltpu.VMEM((width, columns), BF16), pltpu.SemaphoreType.DMA((len(column_chunks(columns)),))]


def split_heads(qkv, width):
    return [qkv.at[:, start : start + width] for start in range(0, qkv.shape[-1], width)]


def pack_kernel(tile, outgoing, quarters, sems):
    _, height, breadth, width = quarters.shape
    copies = []
    for down in range(2):
        for across in range(2):
            index = 2 * down + across
            source = tile.at[
                height * down : height * (down + 1), breadth * across : breadth * (across + 1)
            ]
            copies.append(pltpu.make_async_copy(source, quarters.at[index], sems.at[index]))
            copies[-1].start()
    for index, copy in enumerate(copies):
        copy.wait()
        outgoing[:, index, :] = quarters[index].reshape(height * breadth, width)


def pack(tile):
    rows, cols, width = tile.shape
    return pl.pallas_call(
        pack_kernel,
        in_specs=[HBM],
        out_specs=VMEM,
        out_shape=jax.ShapeDtypeStruct((rows * cols // 4, 4, width), BF16),
        scratch_shapes=[
            pltpu.VMEM((4, rows // 2, cols // 2, width), BF16),
            pltpu.SemaphoreType.DMA((4,)),
        ],
        compiler_params=pltpu.CompilerParams(vmem_limit_bytes=PACK_LIMIT),
        cost_estimate=pl.CostEstimate(flops=0, bytes_accessed=4 * rows * cols * width, transcendentals=0),
        name="pack",
    )(tile)


def edge_scratch(tile):
    rows, cols, width = tile.shape
    return [
        pltpu.VMEM((HALO, cols, width), BF16),
        pltpu.VMEM((rows, 2 * HALO, width), BF16),
        pltpu.SemaphoreType.DMA((2,)),
    ]


def edge_sizes(rows, cols):
    return [HALO * cols, HALO * rows, HALO * HALO, HALO * HALO]


def write_edges(core, tile, targets, outer, inner, sems):
    rows, cols, width = tile.shape
    wide = 2 * HALO
    last = core == 0
    first_row = jnp.where(last, rows - HALO, 0)
    first_col = pl.multiple_of(jnp.where(last, cols - wide, 0), wide)
    copies = [
        pltpu.make_async_copy(tile.at[pl.ds(first_row, HALO)], outer, sems.at[0]),
        pltpu.make_async_copy(tile.at[:, pl.ds(first_col, wide)], inner, sems.at[1]),
    ]
    for copy in copies:
        copy.start()
    upper = lax.broadcasted_iota(jnp.int32, (wide, 1), 0) < HALO
    vertical, horizontal, near, far = targets

    def left_cells(one, two):
        return jnp.where(upper, one, pltpu.roll(two, HALO, 0))

    def right_cells(one, two):
        return jnp.where(upper, pltpu.roll(one, HALO, 0), two)

    for copy in copies:
        copy.wait()
    vertical[: HALO * cols] = outer[...].reshape(HALO * cols, width)
    for pair in range(rows // 2):
        cells = [inner[2 * pair + k].astype(F32) for k in range(2)]
        horizontal[wide * pair : wide * (pair + 1)] = jnp.where(
            last, right_cells(*cells), left_cells(*cells)
        ).astype(BF16)
    for pair in range(HALO // 2):
        place = slice(wide * pair, wide * (pair + 1))
        left = left_cells(*[outer[2 * pair + k, :wide].astype(F32) for k in range(2)])
        right = right_cells(*[outer[2 * pair + k, cols - wide :].astype(F32) for k in range(2)])
        near[place] = jnp.where(last, right, left).astype(BF16)
        far[place] = jnp.where(last, left, right).astype(BF16)


def edge_views(rows, cols, cells):
    views = []
    start = 0
    for size in edge_sizes(rows, cols):
        views.append(cells.at[start : start + size])
        start += size
    return views


def edges_kernel(place_of, tile, send, *scratch):
    rows, cols, _ = tile.shape
    write_edges(1 - place_of[0], tile, edge_views(rows, cols, send), *scratch)


def edges(place_of, tile):
    rows, cols, width = tile.shape
    shape = jax.ShapeDtypeStruct((sum(edge_sizes(rows, cols)), width), BF16)
    return pl.pallas_call(
        edges_kernel,
        in_specs=[SMEM, HBM],
        out_specs=VMEM,
        out_shape=shape,
        scratch_shapes=edge_scratch(tile),
        compiler_params=pltpu.CompilerParams(vmem_limit_bytes=PACK_LIMIT),
        cost_estimate=pl.CostEstimate(flops=0, bytes_accessed=4 * shape.size, transcendentals=0),
        name="edges",
    )(place_of, tile)


def outbound_kernel(place_of, tile, received, *refs):
    parts, scratch = refs[:4], refs[4:]
    rows, cols, _ = tile.shape
    for part, view in zip(parts, edge_views(rows, cols, received)):
        part[part.shape[0] // 2 :] = view[...]
    write_edges(place_of[0], tile, parts, *scratch)


def outbound(place_of, tile, received):
    rows, cols, width = tile.shape
    shapes = [jax.ShapeDtypeStruct((2 * size, width), BF16) for size in edge_sizes(rows, cols)]
    return pl.pallas_call(
        outbound_kernel,
        in_specs=[SMEM, HBM, VMEM],
        out_specs=[VMEM] * 4,
        out_shape=shapes,
        scratch_shapes=edge_scratch(tile),
        compiler_params=pltpu.CompilerParams(vmem_limit_bytes=PACK_LIMIT),
        cost_estimate=pl.CostEstimate(flops=0, bytes_accessed=8 * received.size, transcendentals=0),
        name="outbound",
    )(place_of, tile, received)


def across_tiles(cells, first_step, second_step):
    row_groups, col_groups = lax.axis_size("row"), lax.axis_size("col")
    pairs = []
    for core, (down, right) in enumerate((first_step, second_step)):
        for row in range(row_groups):
            for col in range(col_groups):
                to_row, to_col = row + down, col + right
                if 0 <= to_row < row_groups and 0 <= to_col < col_groups:
                    start = core * row_groups * col_groups
                    pairs.append((start + row * col_groups + col, start + to_row * col_groups + to_col))
    return lax.ppermute(cells, ("branch", "row", "col"), pairs)


def inbound_kernel(forward, backward, forward_corner, backward_corner, after, out):
    start = 0
    for part in (forward, backward, forward_corner, backward_corner):
        count = part.shape[0] // 2
        out[start : start + count] = part[count:]
        start += count


def inbound(parts, after):
    count = sum(part.shape[0] for part in parts) // 2
    shape = jax.ShapeDtypeStruct((count, parts[0].shape[1]), BF16)
    return pl.pallas_call(
        inbound_kernel,
        in_specs=[VMEM] * 4 + [ANY],
        out_specs=VMEM,
        out_shape=shape,
        compiler_params=pltpu.CompilerParams(vmem_limit_bytes=SMALL_LIMIT),
        cost_estimate=pl.CostEstimate(flops=0, bytes_accessed=4 * shape.size, transcendentals=0),
        name="inbound",
    )(*parts, after)


def hold_kernel(cells, *refs):
    pass


def hold(cells, after):
    return pl.pallas_call(
        hold_kernel,
        in_specs=[ANY] * (1 + len(after)),
        out_specs=ANY,
        out_shape=jax.ShapeDtypeStruct(cells.shape, cells.dtype),
        input_output_aliases={0: 0},
        compiler_params=pltpu.CompilerParams(vmem_limit_bytes=SMALL_LIMIT),
        name="hold",
    )(cells, *after)


def own_kernel(half, branch, tokens, modulation, weights, *refs):
    queries_out, sums_out, stats_out, tokens_send, mark, here, normed, qkv, sums, stats, buffer, sems, copy_sems = refs
    arrival = pltpu.make_async_copy(tokens, here, copy_sems.at[0])
    arrival.start()
    multiply = stream_project(normed, weights, 0, buffer, sems, qkv)
    mark[...] = jnp.zeros_like(mark)
    arrival.wait()
    queries, keys, values = split_heads(qkv, here.shape[1])
    other = pl.ds(pl.multiple_of((1 - branch[0]) * half, half), half)
    sends = [
        pltpu.make_async_copy(here.at[other], tokens_send, copy_sems.at[1]),
        pltpu.make_async_copy(queries, queries_out, copy_sems.at[2]),
        pltpu.make_async_copy(sums, sums_out, copy_sems.at[3]),
        pltpu.make_async_copy(stats, stats_out, copy_sems.at[4]),
    ]
    sends[0].start()
    normed[...] = normalise(here[...], modulation[...])
    multiply()
    sends[1].start()
    attend_part(queries, keys, values, None, sums, stats)
    sends[2].start()
    sends[3].start()
    for copy in sends:
        copy.wait()


def own_tile(branch, tokens, modulation, wqkv):
    count, width = tokens.shape
    columns = wqkv.shape[1]
    half = count // 2
    return pl.pallas_call(
        functools.partial(own_kernel, half),
        in_specs=[SMEM, HBM, VMEM, HBM],
        out_specs=[HBM, HBM, HBM, HBM, VMEM],
        out_shape=[
            pltpu.HBM((count, width), BF16),
            pltpu.HBM((count, width), BF16),
            pltpu.HBM((count, 2 * LANES), F32),
            pltpu.HBM((half, width), BF16),
            MARK,
        ],
        scratch_shapes=[
            pltpu.VMEM((count, width), BF16),
            pltpu.VMEM((count, width), BF16),
            pltpu.VMEM((count, columns), BF16),
            pltpu.VMEM((count, width), BF16),
            pltpu.VMEM((count, 2 * LANES), F32),
        ]
        + weight_scratch(width, columns)
        + [pltpu.SemaphoreType.DMA((5,))],
        compiler_params=pltpu.CompilerParams(vmem_limit_bytes=VMEM_LIMIT),
        cost_estimate=pl.CostEstimate(
            flops=2 * count * width * columns + 4 * count * count * width * 3,
            bytes_accessed=2 * (width * columns + 5 * count * width),
            transcendentals=count * count * HEADS,
        ),
        name="own_tile",
    )(branch, tokens, modulation, wqkv)


def lane_tiles(width):
    return [slice(start, start + LANES) for start in range(0, width, LANES)]


def lattice_kernel(branch, tokens, modulation, weights, *refs):
    mine, theirs, normed, qkv, whole, tiles, buffer, sems, local, local_sem = refs[-10:]
    fetch = pltpu.make_async_copy(modulation, local, local_sem)
    fetch.start()
    count, width = whole.shape
    multiply = stream_project(normed, weights, 0, buffer, sems, qkv)
    def fetched():
        fetch.wait()
        return local[...]

    normed[...] = normalise(tokens[...].reshape(count, width), fetched)
    multiply()
    queries, keys, values = split_heads(qkv, width)
    attend(queries, keys, values, whole)
    sources = count // 4
    for tile, lanes in enumerate(lane_tiles(width)):
        tiles[tile] = whole[:, lanes].astype(F32)
        for target, half in ((theirs, 1 - branch[0]), (mine, branch[0])):
            for across in range(2):
                rows = pl.ds(2 * half + across, sources, stride=4)
                target[sources * across : sources * (across + 1), lanes] = tiles[tile, rows, :].astype(BF16)


def lattice(branch, tokens, modulation, wqkv, after):
    sources, per_source, width = tokens.shape
    count = sources * per_source
    columns = wqkv.shape[1]
    half = jax.ShapeDtypeStruct((count // 2, width), BF16)
    return pl.pallas_call(
        lattice_kernel,
        in_specs=[SMEM, VMEM, HBM, HBM] + [ANY] * len(after),
        out_specs=[VMEM, VMEM],
        out_shape=[half, half],
        scratch_shapes=[
            pltpu.VMEM((count, width), BF16),
            pltpu.VMEM((count, columns), BF16),
            pltpu.VMEM((count, width), BF16),
            pltpu.VMEM((width // LANES, count, LANES), F32),
        ]
        + weight_scratch(width, columns)
        + [pltpu.VMEM(modulation.shape, F32), pltpu.SemaphoreType.DMA],
        compiler_params=pltpu.CompilerParams(vmem_limit_bytes=VMEM_LIMIT),
        cost_estimate=pl.CostEstimate(flops=0, bytes_accessed=2 * count * width, transcendentals=0),
        name="lattice",
    )(branch, tokens, in_hbm(modulation), wqkv, *after)


def guidance(branch):
    conditional = branch[0] == 1
    return jnp.where(conditional, GUIDANCE, 1.0 - GUIDANCE), jnp.where(conditional, 1.0 - GUIDANCE, GUIDANCE)


def combine_kernel(branch, mine, theirs, out):
    own_factor, other_factor = guidance(branch)
    both = own_factor * mine[...].astype(F32) + other_factor * theirs[...].astype(F32)
    sources = out.shape[0]
    for across in range(2):
        out[:, across, :] = both[sources * across : sources * (across + 1)].astype(BF16)


def combine(branch, mine, theirs):
    count, width = mine.shape
    return pl.pallas_call(
        combine_kernel,
        in_specs=[SMEM, VMEM, VMEM],
        out_specs=VMEM,
        out_shape=jax.ShapeDtypeStruct((count // 2, 2, width), BF16),
        compiler_params=pltpu.CompilerParams(vmem_limit_bytes=SMALL_LIMIT),
        cost_estimate=pl.CostEstimate(flops=3 * mine.size, bytes_accessed=6 * mine.size, transcendentals=0),
        name="combine",
    )(branch, mine, theirs)


def halo_places(rows, cols):
    def block(first_row, height, first_col, breadth):
        row, col = np.mgrid[first_row : first_row + height, first_col : first_col + breadth]
        return np.stack([row.reshape(-1), col.reshape(-1)])

    blocks = [block(-HALO, HALO, 0, cols), block(0, rows, -HALO, HALO)]
    blocks += [block(-HALO, HALO, -HALO, HALO), block(-HALO, HALO, cols, HALO)]
    blocks += [block(rows, HALO, 0, cols), block(0, rows, cols, HALO)]
    blocks += [block(rows, HALO, cols, HALO), block(rows, HALO, -HALO, HALO)]
    return np.concatenate(blocks, axis=1).astype(np.int32)


def gather_halo(place_of, parts, gathered, sems):
    *parts, passed = parts
    count = passed.shape[0]
    rows = pl.ds(pl.multiple_of((1 - place_of[0]) * count, 2 * HALO), count)
    copies = [pltpu.make_async_copy(passed, gathered.at[rows], sems.at[len(parts)])]
    start = place_of[0] * count
    for index, part in enumerate(parts):
        size = part.shape[0] // 2
        rows = pl.ds(pl.multiple_of(start, 2 * HALO), size)
        copies.append(pltpu.make_async_copy(part.at[:size], gathered.at[rows], sems.at[index]))
        start += size
    return copies


def window_kernel(rows, cols, parts, branch, reach, places, own_queries, own_sums, own_stats, *refs):
    halo, (modulation, weights) = refs[:parts], refs[parts : parts + 2]
    mine, theirs, gathered, normed, halo_kv, queries, sums, stats, whole, *refs = refs[-15:]
    halo_sums, halo_stats, buffer, sems, copy_sems, halo_sems = refs
    half, width = theirs.shape
    first = pl.ds(pl.multiple_of(branch[0] * half, half), half)
    second = pl.ds(pl.multiple_of((1 - branch[0]) * half, half), half)
    arrivals = gather_halo(branch, halo, gathered, halo_sems)
    for copy in arrivals:
        copy.start()
    multiply = stream_project(normed, weights, width, buffer, sems, halo_kv)
    own_copies = [
        pltpu.make_async_copy(own_queries, queries, copy_sems.at[parts]),
        pltpu.make_async_copy(own_sums, sums, copy_sems.at[parts + 1]),
        pltpu.make_async_copy(own_stats, stats, copy_sems.at[parts + 4]),
    ]
    sends = [
        pltpu.make_async_copy(whole.at[first], mine, copy_sems.at[parts + 2]),
        pltpu.make_async_copy(whole.at[second], theirs, copy_sems.at[parts + 3]),
    ]
    for copy in own_copies:
        copy.start()
    row, col = places[0:1], places[1:2]
    limits = [jnp.where(branch[1 + side] != 0, reach[side], 0) for side in range(4)]
    allowed = (row >= -limits[0]) & (row < rows + limits[1])
    allowed = allowed & (col >= -limits[2]) & (col < cols + limits[3])
    bias = jnp.where(allowed, 0.0, -1e30).astype(F32)
    for copy in arrivals:
        copy.wait()
    normed[...] = normalise(gathered[...], modulation[...])
    multiply()
    for copy in own_copies:
        copy.wait()
    keys, values = split_heads(halo_kv, width)
    attend_part(queries, keys, values, bias, halo_sums, halo_stats)
    merge_parts([(sums, stats), (halo_sums, halo_stats)], whole)
    for copy in sends:
        copy.start()
    for copy in sends:
        copy.wait()


def window(branch, reach, own, halo, modulation, wqkv, rows, cols, after):
    count, width = own[0].shape
    places = jnp.asarray(halo_places(rows, cols))
    halo_count = places.shape[1]
    half = (count // 2, width)
    return pl.pallas_call(
        functools.partial(window_kernel, rows, cols, len(halo)),
        in_specs=[SMEM, SMEM, VMEM, HBM, HBM, HBM] + [HBM] * (len(halo) - 1) + [ANY, VMEM, HBM] + [HBM] * len(after),
        out_specs=[ANY, ANY],
        out_shape=[jax.ShapeDtypeStruct(half, BF16)] * 2,
        scratch_shapes=[
            pltpu.VMEM((halo_count, width), BF16),
            pltpu.VMEM((halo_count, width), BF16),
            pltpu.VMEM((halo_count, 2 * width), BF16),
            pltpu.VMEM((count, width), BF16),
            pltpu.VMEM((count, width), BF16),
            pltpu.VMEM((count, 2 * LANES), F32),
            pltpu.VMEM((count, width), BF16),
            pltpu.VMEM((count, width), F32),
            pltpu.VMEM((count, 2 * LANES), F32),
        ]
        + weight_scratch(width, 2 * width)
        + [pltpu.SemaphoreType.DMA((len(halo) + 5,)), pltpu.SemaphoreType.DMA((len(halo),))],
        compiler_params=pltpu.CompilerParams(vmem_limit_bytes=VMEM_LIMIT),
        cost_estimate=pl.CostEstimate(
            flops=4 * count * halo_count * width * 3 + 4 * halo_count * width * width,
            bytes_accessed=2 * (4 * count * width + 2 * halo_count * width + 2 * width * width),
            transcendentals=count * halo_count * HEADS,
        ),
        name="window",
    )(branch, reach, places, *[in_hbm(part) for part in own], *[in_hbm(part) for part in halo[:-1]], halo[-1], modulation, wqkv, *after)


def finish_kernel(
    col_groups, branch, window_mine, window_theirs, tokens, tokens_theirs, returned, blend, gate, weights, out, *refs
):
    tokens_mine, raw, dilated, result, buffer, sems, out_sems = refs
    own_factor, other_factor = guidance(branch)
    count, width = dilated.shape
    columns = [slice(0, FIRST_COLUMNS), slice(FIRST_COLUMNS, width)]
    copies = [
        pltpu.make_async_copy(weights.at[:, place], buffer.at[:, place], sems.at[index])
        for index, place in enumerate(columns)
    ]
    sends = [
        pltpu.make_async_copy(result.at[:, place], out.at[:, place], out_sems.at[index])
        for index, place in enumerate(columns)
    ]
    mine = pl.ds(pl.multiple_of(branch[0] * count, count), count)
    arrival = pltpu.make_async_copy(tokens.at[mine], tokens_mine, sems.at[len(columns)])
    for copy in [arrival] + copies:
        copy.start()
    flat = returned[...].reshape(count, width)
    for tile, lanes in enumerate(lane_tiles(width)):
        raw[tile] = flat[:, lanes].astype(F32)
        for across in range(2):
            cells = raw[tile, pl.ds(across, count // 2, stride=2), :]
            for row in range(count // 2 // col_groups):
                start = col_groups * (2 * row + across)
                dilated[start : start + col_groups, lanes] = cells[col_groups * row : col_groups * (row + 1)]
    weight = blend[...]
    both = own_factor * window_mine[...].astype(F32) + other_factor * window_theirs[...].astype(F32)
    mixed = (weight * both + (1.0 - weight) * dilated[...]).astype(BF16)
    arrival.wait()
    for copy, send, place in zip(copies, sends, columns):
        kept = own_factor * tokens_mine[:, place].astype(F32) + other_factor * tokens_theirs[:, place].astype(F32)
        copy.wait()
        projected = jnp.dot(mixed, buffer[:, place], preferred_element_type=F32)
        result[:, place] = (kept + gate[:, place] * projected).astype(BF16)
        send.start()
    for send in sends:
        send.wait()


def finish(branch, window_mine, window_theirs, tokens, tokens_theirs, returned, blend, gate, w_out, col_groups):
    count, width = window_mine.shape
    return pl.pallas_call(
        functools.partial(finish_kernel, col_groups),
        in_specs=[SMEM, VMEM, VMEM, HBM] + [VMEM] * 4 + [HBM],
        out_specs=HBM,
        out_shape=jax.ShapeDtypeStruct((count, width), BF16),
        scratch_shapes=[
            pltpu.VMEM((count, width), BF16),
            pltpu.VMEM((width // LANES, count, LANES), F32),
            pltpu.VMEM((count, width), F32),
            pltpu.VMEM((count, width), BF16),
            pltpu.VMEM((width, width), BF16),
            pltpu.SemaphoreType.DMA((3,)),
            pltpu.SemaphoreType.DMA((2,)),
        ],
        compiler_params=pltpu.CompilerParams(vmem_limit_bytes=FINISH_LIMIT),
        cost_estimate=pl.CostEstimate(
            flops=2 * count * width * width,
            bytes_accessed=2 * (width * width + 6 * count * width),
            transcendentals=0,
        ),
        name="finish",
    )(branch, window_mine, window_theirs, tokens, tokens_theirs, returned, blend, gate, w_out)


def on_device(tokens, modulation, wqkv, w_out, blend, reach):
    tile = tokens[0]
    rows, cols, width = tile.shape
    row_groups = lax.axis_size("row")
    col_groups = lax.axis_size("col")
    sub_rows = rows // row_groups
    sub_cols = cols // col_groups
    half = rows // 2 * cols
    branch = lax.axis_index("branch")
    wqkv, w_out = in_hbm(wqkv), in_hbm(w_out)
    devices = row_groups * col_groups
    row, col = lax.axis_index("row"), lax.axis_index("col")
    inner = [row > 0, row < row_groups - 1, col > 0, col < col_groups - 1]
    place_of = jnp.stack([branch] + [side.astype(branch.dtype) for side in inner]).astype(jnp.int32)

    def other_core(cells):
        return lax.ppermute(cells, "branch", [(0, 1), (1, 0)])

    received = other_core(edges(place_of, in_hbm(tile)))
    outgoing = hold(pack(in_hbm(tile)), [received])
    arrived = lax.all_to_all(outgoing, ("col", "row"), split_axis=0, concat_axis=0, tiled=True)

    flat = tile.reshape(rows * cols, width)
    parts = outbound(place_of, in_hbm(tile), received)
    steps = (((1, 0), (-1, 0)), ((0, 1), (0, -1)), ((1, 1), (-1, -1)), ((1, -1), (-1, 1)))
    *own, tokens_send, mark = own_tile(place_of, flat, modulation, wqkv)
    halo = [across_tiles(part, *step) for part, step in zip(parts, steps)]
    tokens_theirs = other_core(tokens_send)

    lattice_mine, lattice_send = lattice(place_of, arrived, modulation, wqkv, [mark])
    passed = other_core(inbound(halo, lattice_mine))
    lattice_theirs = other_core(hold(lattice_send, halo))
    combined = combine(place_of, lattice_mine, lattice_theirs)
    returned = lax.all_to_all(combined, ("col", "row"), split_axis=0, concat_axis=0, tiled=True)

    window_mine, send = window(
        place_of, reach.reshape(4), own, halo + [passed], modulation, wqkv, rows, cols, [combined]
    )
    window_theirs = other_core(send)
    weight = lax.dynamic_index_in_dim(blend.reshape(2, half, 1), branch, 0, keepdims=False)
    guided = finish(
        place_of,
        window_mine,
        window_theirs,
        in_hbm(flat),
        tokens_theirs,
        returned,
        weight,
        modulation[2:3],
        w_out,
        col_groups,
    )
    return guided.reshape(rows // 2, cols, width)


def solution(mesh):
    in_specs = (
        P("branch", "row", "col", None),
        P(),
        P(),
        P(),
        P("row", "col"),
        P(None, "row", "col"),
    )
    out_specs = P(("row", "branch"), "col", None)
    return jax.shard_map(
        on_device, mesh=mesh, in_specs=in_specs, out_specs=out_specs, check_vma=False
    )
```

```python
import functools
import math

import jax
import jax.numpy as jnp
import numpy as np
from jax import lax
from jax.experimental import pallas as pl
from jax.experimental.pallas import tpu as pltpu
from jax.sharding import PartitionSpec as P

HEADS = 16
HALO = 4
GUIDANCE = 4.5
LANES = 128
VMEM_LIMIT = 28 * 1024 * 1024
SMALL_LIMIT = 4 * 1024 * 1024
FINISH_LIMIT = 16 * 1024 * 1024
ARRANGE_LIMIT = 8 * 1024 * 1024
FIRST_COLUMNS = 640
FIRST_CHUNK = 512
SECOND_CHUNK = 1536
IN_FLIGHT = 2

F32 = jnp.float32
BF16 = jnp.bfloat16

VMEM = pl.BlockSpec(memory_space=pltpu.VMEM)
SMEM = pl.BlockSpec(memory_space=pltpu.SMEM)
ANY = pl.BlockSpec(memory_space=pl.ANY)
HBM = pl.BlockSpec(memory_space=pltpu.HBM)
MARK = jax.ShapeDtypeStruct((8, LANES), F32)


def in_hbm(array):
    return pltpu.with_memory_space_constraint(array, pltpu.HBM)


def normalise(tokens, modulation):
    widened = tokens.astype(F32)
    centered = widened - jnp.mean(widened, axis=-1, keepdims=True)
    variance = jnp.mean(centered * centered, axis=-1, keepdims=True)
    scaled = centered * lax.rsqrt(variance + 1e-06)
    if callable(modulation):
        modulation = modulation()
    return (scaled * (1.0 + modulation[1:2]) + modulation[0:1]).astype(BF16)


def head_window(head, head_size, width):
    first = head * head_size
    low = first // LANES * LANES
    high = min(-(-(first + head_size) // LANES) * LANES, width)
    return first, low, high


def head_lanes(head, width):
    head_size = width // HEADS
    first, low, high = head_window(head, head_size, width)
    lane = lax.broadcasted_iota(jnp.int32, (1, high - low), 1) + low
    inside = (lane >= first) & (lane < first + head_size)
    return slice(low, high), inside, 0 if first > low else head_size


def head_scores(place, inside, queries, keys):
    query = queries[:, place]
    query = jnp.where(inside, query, jnp.zeros_like(query))
    return lax.dot_general(query, keys[:, place], (((1,), (1,)), ((), ())), preferred_element_type=F32)


def weigh_values(place, inside, scores, top, values):
    powers = jnp.exp2(scores - top).astype(BF16)
    value = values[:, place]
    value = jnp.where(inside, value, jnp.ones_like(value))
    return jnp.dot(powers, value, preferred_element_type=F32)


def attend(queries, keys, values, out):
    width = queries.shape[-1]
    for head in range(HEADS):
        place, inside, spare = head_lanes(head, width)
        scores = head_scores(place, inside, queries, keys)
        top = jnp.max(scores, axis=-1, keepdims=True)
        total = weigh_values(place, inside, scores, top, values)
        attended = (total * (1.0 / total[:, spare : spare + 1])).astype(out.dtype)
        out[:, place] = jnp.where(inside, attended, out[:, place])


def attend_part(queries, keys, values, bias, sums, stats):
    width = queries.shape[-1]
    column = lax.broadcasted_iota(jnp.int32, (1, LANES), 1)
    stats[:, :LANES] = jnp.zeros_like(stats[:, :LANES])
    stats[:, LANES:] = jnp.ones_like(stats[:, LANES:])
    for head in range(HEADS):
        place, inside, spare = head_lanes(head, width)
        scores = head_scores(place, inside, queries, keys)
        if bias is not None:
            scores = scores + bias
        top = jnp.max(scores, axis=-1, keepdims=True)
        total = weigh_values(place, inside, scores, top, values)
        sums[:, place] = jnp.where(inside, total.astype(sums.dtype), sums[:, place])
        stats[:, :LANES] = jnp.where(column == head, top, stats[:, :LANES])
        stats[:, LANES:] = jnp.where(column == head, total[:, spare : spare + 1], stats[:, LANES:])


def merge_parts(parts, out):
    width = out.shape[-1]
    row = lax.broadcasted_iota(jnp.int32, (2 * LANES, width), 0) % LANES
    column = lax.broadcasted_iota(jnp.int32, (2 * LANES, width), 1)
    head_size = width // HEADS
    spread = ((column >= row * head_size) & (column < (row + 1) * head_size)).astype(F32).astype(BF16)
    tops = [stats[:, :LANES] for _, stats in parts]
    top = functools.reduce(jnp.maximum, tops)
    factors = [jnp.exp2(part_top - top) for part_top in tops]
    weight = sum(factor * stats[:, LANES:] for factor, (_, stats) in zip(factors, parts))
    total = None
    for factor, (sums, _) in zip(factors, parts):
        factor = factor * (1.0 / weight)
        high = factor.astype(BF16)
        low = (factor - high.astype(F32)).astype(BF16)
        wide = jnp.dot(jnp.concatenate([high, low], axis=1), spread, preferred_element_type=F32)
        part = sums[...].astype(F32) * wide
        total = part if total is None else total + part
    out[...] = total.astype(out.dtype)


def query_scale(feature_width):
    return math.log2(math.e) / math.sqrt(feature_width // HEADS)


def column_chunks(width):
    starts = [0, FIRST_CHUNK, SECOND_CHUNK, width]
    return [(start, end - start) for start, end in zip(starts, starts[1:])]


def stream_project(normed, weights, first_column, buffer, sems, out, sends=()):
    width = normed.shape[-1]
    chunks = column_chunks(out.shape[-1])
    copies = [
        pltpu.make_async_copy(
            weights.at[:, first_column + start : first_column + start + size],
            buffer.at[:, start : start + size],
            sems.at[index],
        )
        for index, (start, size) in enumerate(chunks)
    ]
    for copy in copies[:IN_FLIGHT]:
        copy.start()

    def multiply():
        for index, (start, size) in enumerate(chunks):
            copies[index].wait()
            if index + IN_FLIGHT < len(chunks):
                copies[index + IN_FLIGHT].start()
            product = jnp.dot(normed[...], buffer[:, start : start + size], preferred_element_type=F32)
            if first_column + start < width:
                column = lax.broadcasted_iota(jnp.int32, (1, size), 1) + first_column + start
                product = product * jnp.where(column < width, query_scale(width), 1.0)
            out[:, start : start + size] = product.astype(BF16)
            if sends:
                sends[index].start()

    return multiply


def weight_scratch(width, columns):
    return [pltpu.VMEM((width, columns), BF16), pltpu.SemaphoreType.DMA((len(column_chunks(columns)),))]


def split_heads(qkv, width):
    return [qkv.at[:, start : start + width] for start in range(0, qkv.shape[-1], width)]


def arrange_kernel(tile, outgoing, left, right, quarters, sems):
    _, height, breadth, width = quarters.shape
    copies = []
    for down in range(2):
        for across in range(2):
            index = 2 * down + across
            source = tile.at[
                height * down : height * (down + 1), breadth * across : breadth * (across + 1)
            ]
            copies.append(pltpu.make_async_copy(source, quarters.at[index], sems.at[index]))
            copies[-1].start()
    wide = 2 * HALO
    upper = lax.broadcasted_iota(jnp.int32, (wide, 1), 0) < HALO
    for index, copy in enumerate(copies):
        copy.wait()
        outgoing[:, index, :] = quarters[index].reshape(height * breadth, width)
    for pair in range(height):
        down, row = divmod(2 * pair, height)
        place = slice(wide * pair, wide * (pair + 1))
        one, two = [quarters[2 * down, row + k, :wide].astype(F32) for k in range(2)]
        left[place] = jnp.where(upper, one, pltpu.roll(two, HALO, 0)).astype(BF16)
        one, two = [quarters[2 * down + 1, row + k, breadth - wide :].astype(F32) for k in range(2)]
        right[place] = jnp.where(upper, pltpu.roll(one, HALO, 0), two).astype(BF16)


def arrange(tile):
    rows, cols, width = tile.shape
    strip = jax.ShapeDtypeStruct((rows * HALO, width), BF16)
    return pl.pallas_call(
        arrange_kernel,
        in_specs=[HBM],
        out_specs=[VMEM, VMEM, VMEM],
        out_shape=[jax.ShapeDtypeStruct((rows * cols // 4, 4, width), BF16), strip, strip],
        scratch_shapes=[
            pltpu.VMEM((4, rows // 2, cols // 2, width), BF16),
            pltpu.SemaphoreType.DMA((4,)),
        ],
        compiler_params=pltpu.CompilerParams(vmem_limit_bytes=ARRANGE_LIMIT),
        cost_estimate=pl.CostEstimate(flops=0, bytes_accessed=4 * rows * cols * width, transcendentals=0),
        name="arrange",
    )(tile)


def hold_kernel(cells, *refs):
    pass


def hold(cells, after):
    return pl.pallas_call(
        hold_kernel,
        in_specs=[ANY] * (1 + len(after)),
        out_specs=ANY,
        out_shape=jax.ShapeDtypeStruct(cells.shape, cells.dtype),
        input_output_aliases={0: 0},
        compiler_params=pltpu.CompilerParams(vmem_limit_bytes=SMALL_LIMIT),
        name="hold",
    )(cells, *after)


def own_kernel(half, branch, tokens, modulation, weights, *refs):
    queries_out, sums_out, stats_out, tokens_send, mark, here, normed, qkv, sums, stats, buffer, sems, copy_sems = refs
    arrival = pltpu.make_async_copy(tokens, here, copy_sems.at[0])
    arrival.start()
    multiply = stream_project(normed, weights, 0, buffer, sems, qkv)
    mark[...] = jnp.zeros_like(mark)
    arrival.wait()
    queries, keys, values = split_heads(qkv, here.shape[1])
    other = pl.ds(pl.multiple_of((1 - branch[0]) * half, half), half)
    sends = [
        pltpu.make_async_copy(here.at[other], tokens_send, copy_sems.at[1]),
        pltpu.make_async_copy(queries, queries_out, copy_sems.at[2]),
        pltpu.make_async_copy(sums, sums_out, copy_sems.at[3]),
        pltpu.make_async_copy(stats, stats_out, copy_sems.at[4]),
    ]
    sends[0].start()
    normed[...] = normalise(here[...], modulation[...])
    multiply()
    sends[1].start()
    attend_part(queries, keys, values, None, sums, stats)
    sends[2].start()
    sends[3].start()
    for copy in sends:
        copy.wait()


def own_tile(branch, tokens, modulation, wqkv):
    count, width = tokens.shape
    columns = wqkv.shape[1]
    half = count // 2
    return pl.pallas_call(
        functools.partial(own_kernel, half),
        in_specs=[SMEM, HBM, VMEM, HBM],
        out_specs=[HBM, HBM, HBM, HBM, VMEM],
        out_shape=[
            pltpu.HBM((count, width), BF16),
            pltpu.HBM((count, width), BF16),
            pltpu.HBM((count, 2 * LANES), F32),
            pltpu.HBM((half, width), BF16),
            MARK,
        ],
        scratch_shapes=[
            pltpu.VMEM((count, width), BF16),
            pltpu.VMEM((count, width), BF16),
            pltpu.VMEM((count, columns), BF16),
            pltpu.VMEM((count, width), BF16),
            pltpu.VMEM((count, 2 * LANES), F32),
        ]
        + weight_scratch(width, columns)
        + [pltpu.SemaphoreType.DMA((5,))],
        compiler_params=pltpu.CompilerParams(vmem_limit_bytes=VMEM_LIMIT),
        cost_estimate=pl.CostEstimate(
            flops=2 * count * width * columns + 4 * count * count * width * 3,
            bytes_accessed=2 * (width * columns + 5 * count * width),
            transcendentals=count * count * HEADS,
        ),
        name="own_tile",
    )(branch, tokens, modulation, wqkv)


def lane_tiles(width):
    return [slice(start, start + LANES) for start in range(0, width, LANES)]


def lattice_kernel(branch, tokens, modulation, weights, *refs):
    mine, theirs, normed, qkv, whole, tiles, buffer, sems, local, local_sem = refs[-10:]
    fetch = pltpu.make_async_copy(modulation, local, local_sem)
    fetch.start()
    count, width = whole.shape
    multiply = stream_project(normed, weights, 0, buffer, sems, qkv)
    def fetched():
        fetch.wait()
        return local[...]

    normed[...] = normalise(tokens[...].reshape(count, width), fetched)
    multiply()
    queries, keys, values = split_heads(qkv, width)
    attend(queries, keys, values, whole)
    sources = count // 4
    for tile, lanes in enumerate(lane_tiles(width)):
        tiles[tile] = whole[:, lanes].astype(F32)
        for target, half in ((theirs, 1 - branch[0]), (mine, branch[0])):
            for across in range(2):
                rows = pl.ds(2 * half + across, sources, stride=4)
                target[sources * across : sources * (across + 1), lanes] = tiles[tile, rows, :].astype(BF16)


def lattice(branch, tokens, modulation, wqkv, after):
    sources, per_source, width = tokens.shape
    count = sources * per_source
    columns = wqkv.shape[1]
    half = jax.ShapeDtypeStruct((count // 2, width), BF16)
    return pl.pallas_call(
        lattice_kernel,
        in_specs=[SMEM, VMEM, HBM, HBM] + [ANY] * len(after),
        out_specs=[VMEM, VMEM],
        out_shape=[half, half],
        scratch_shapes=[
            pltpu.VMEM((count, width), BF16),
            pltpu.VMEM((count, columns), BF16),
            pltpu.VMEM((count, width), BF16),
            pltpu.VMEM((width // LANES, count, LANES), F32),
        ]
        + weight_scratch(width, columns)
        + [pltpu.VMEM(modulation.shape, F32), pltpu.SemaphoreType.DMA],
        compiler_params=pltpu.CompilerParams(vmem_limit_bytes=VMEM_LIMIT),
        cost_estimate=pl.CostEstimate(
            flops=2 * count * width * columns + 4 * count * count * width * 3,
            bytes_accessed=2 * (width * columns + 2 * count * width),
            transcendentals=count * count * HEADS,
        ),
        name="lattice",
    )(branch, tokens, in_hbm(modulation), wqkv, *after)


def guidance(branch):
    conditional = branch[0] == 1
    return jnp.where(conditional, GUIDANCE, 1.0 - GUIDANCE), jnp.where(conditional, 1.0 - GUIDANCE, GUIDANCE)


def combine_kernel(branch, mine, theirs, out):
    own_factor, other_factor = guidance(branch)
    both = own_factor * mine[...].astype(F32) + other_factor * theirs[...].astype(F32)
    sources = out.shape[0]
    for across in range(2):
        out[:, across, :] = both[sources * across : sources * (across + 1)].astype(BF16)


def combine(branch, mine, theirs):
    count, width = mine.shape
    return pl.pallas_call(
        combine_kernel,
        in_specs=[SMEM, VMEM, VMEM],
        out_specs=VMEM,
        out_shape=jax.ShapeDtypeStruct((count // 2, 2, width), BF16),
        compiler_params=pltpu.CompilerParams(vmem_limit_bytes=SMALL_LIMIT),
        cost_estimate=pl.CostEstimate(flops=3 * mine.size, bytes_accessed=6 * mine.size, transcendentals=0),
        name="combine",
    )(branch, mine, theirs)


def halo_places(rows, cols):
    def block(first_row, height, first_col, breadth):
        row, col = np.mgrid[first_row : first_row + height, first_col : first_col + breadth]
        return np.stack([row.reshape(-1), col.reshape(-1)])

    blocks = []
    for first_row in (-HALO, rows):
        blocks += [block(first_row, HALO, 0, cols), block(first_row, HALO, -HALO, HALO)]
        blocks += [block(first_row, HALO, cols, HALO)]
    blocks += [block(0, rows, -HALO, HALO), block(0, rows, cols, HALO)]
    return np.concatenate(blocks, axis=1).astype(np.int32)


def window_kernel(rows, cols, parts, branch, reach, places, own_queries, own_sums, own_stats, *refs):
    halo, (modulation, weights) = refs[:parts], refs[parts : parts + 2]
    mine, theirs, gathered, normed, halo_kv, queries, sums, stats, whole, *refs = refs[-14:]
    halo_sums, halo_stats, buffer, sems, copy_sems = refs
    half, width = theirs.shape
    first = pl.ds(pl.multiple_of(branch[0] * half, half), half)
    second = pl.ds(pl.multiple_of((1 - branch[0]) * half, half), half)
    arrivals = []
    start = 0
    for index, part in enumerate(halo):
        place = gathered.at[start : start + part.shape[0]]
        arrivals.append(pltpu.make_async_copy(part, place, copy_sems.at[index]))
        arrivals[-1].start()
        start += part.shape[0]
    multiply = stream_project(normed, weights, width, buffer, sems, halo_kv)
    own_copies = [
        pltpu.make_async_copy(own_queries, queries, copy_sems.at[parts]),
        pltpu.make_async_copy(own_sums, sums, copy_sems.at[parts + 1]),
        pltpu.make_async_copy(own_stats, stats, copy_sems.at[parts + 4]),
    ]
    sends = [
        pltpu.make_async_copy(whole.at[first], mine, copy_sems.at[parts + 2]),
        pltpu.make_async_copy(whole.at[second], theirs, copy_sems.at[parts + 3]),
    ]
    for copy in own_copies:
        copy.start()
    row, col = places[0:1], places[1:2]
    limits = [jnp.where(branch[1 + side] != 0, reach[side], 0) for side in range(4)]
    allowed = (row >= -limits[0]) & (row < rows + limits[1])
    allowed = allowed & (col >= -limits[2]) & (col < cols + limits[3])
    bias = jnp.where(allowed, 0.0, -1e30).astype(F32)
    for copy in arrivals:
        copy.wait()
    normed[...] = normalise(gathered[...], modulation[...])
    multiply()
    for copy in own_copies:
        copy.wait()
    keys, values = split_heads(halo_kv, width)
    attend_part(queries, keys, values, bias, halo_sums, halo_stats)
    merge_parts([(sums, stats), (halo_sums, halo_stats)], whole)
    for copy in sends:
        copy.start()
    for copy in sends:
        copy.wait()


def window(branch, reach, own, halo, modulation, wqkv, rows, cols, after):
    count, width = own[0].shape
    places = jnp.asarray(halo_places(rows, cols))
    halo_count = places.shape[1]
    half = (count // 2, width)
    return pl.pallas_call(
        functools.partial(window_kernel, rows, cols, len(halo)),
        in_specs=[SMEM, SMEM, VMEM, HBM, HBM, HBM] + [HBM] * len(halo) + [VMEM, HBM] + [HBM] * len(after),
        out_specs=[ANY, ANY],
        out_shape=[jax.ShapeDtypeStruct(half, BF16)] * 2,
        scratch_shapes=[
            pltpu.VMEM((halo_count, width), BF16),
            pltpu.VMEM((halo_count, width), BF16),
            pltpu.VMEM((halo_count, 2 * width), BF16),
            pltpu.VMEM((count, width), BF16),
            pltpu.VMEM((count, width), BF16),
            pltpu.VMEM((count, 2 * LANES), F32),
            pltpu.VMEM((count, width), BF16),
            pltpu.VMEM((count, width), F32),
            pltpu.VMEM((count, 2 * LANES), F32),
        ]
        + weight_scratch(width, 2 * width)
        + [pltpu.SemaphoreType.DMA((len(halo) + 5,))],
        compiler_params=pltpu.CompilerParams(vmem_limit_bytes=VMEM_LIMIT),
        cost_estimate=pl.CostEstimate(
            flops=4 * count * halo_count * width * 3 + 4 * halo_count * width * width,
            bytes_accessed=2 * (4 * count * width + 2 * halo_count * width + 2 * width * width),
            transcendentals=count * halo_count * HEADS,
        ),
        name="window",
    )(branch, reach, places, *[in_hbm(part) for part in own], *[in_hbm(part) for part in halo], modulation, wqkv, *after)


def finish_kernel(
    col_groups, branch, window_mine, window_theirs, tokens, tokens_theirs, returned, blend, gate, weights, out, *refs
):
    tokens_mine, raw, dilated, result, buffer, sems, out_sems = refs
    own_factor, other_factor = guidance(branch)
    count, width = dilated.shape
    columns = [slice(0, FIRST_COLUMNS), slice(FIRST_COLUMNS, width)]
    copies = [
        pltpu.make_async_copy(weights.at[:, place], buffer.at[:, place], sems.at[index])
        for index, place in enumerate(columns)
    ]
    sends = [
        pltpu.make_async_copy(result.at[:, place], out.at[:, place], out_sems.at[index])
        for index, place in enumerate(columns)
    ]
    mine = pl.ds(pl.multiple_of(branch[0] * count, count), count)
    arrival = pltpu.make_async_copy(tokens.at[mine], tokens_mine, sems.at[len(columns)])
    for copy in [arrival] + copies:
        copy.start()
    flat = returned[...].reshape(count, width)
    for tile, lanes in enumerate(lane_tiles(width)):
        raw[tile] = flat[:, lanes].astype(F32)
        for across in range(2):
            cells = raw[tile, pl.ds(across, count // 2, stride=2), :]
            for row in range(count // 2 // col_groups):
                start = col_groups * (2 * row + across)
                dilated[start : start + col_groups, lanes] = cells[col_groups * row : col_groups * (row + 1)]
    weight = blend[...]
    both = own_factor * window_mine[...].astype(F32) + other_factor * window_theirs[...].astype(F32)
    mixed = (weight * both + (1.0 - weight) * dilated[...]).astype(BF16)
    arrival.wait()
    for copy, send, place in zip(copies, sends, columns):
        kept = own_factor * tokens_mine[:, place].astype(F32) + other_factor * tokens_theirs[:, place].astype(F32)
        copy.wait()
        projected = jnp.dot(mixed, buffer[:, place], preferred_element_type=F32)
        result[:, place] = (kept + gate[:, place] * projected).astype(BF16)
        send.start()
    for send in sends:
        send.wait()


def finish(branch, window_mine, window_theirs, tokens, tokens_theirs, returned, blend, gate, w_out, col_groups):
    count, width = window_mine.shape
    return pl.pallas_call(
        functools.partial(finish_kernel, col_groups),
        in_specs=[SMEM, VMEM, VMEM, HBM] + [VMEM] * 4 + [HBM],
        out_specs=HBM,
        out_shape=jax.ShapeDtypeStruct((count, width), BF16),
        scratch_shapes=[
            pltpu.VMEM((count, width), BF16),
            pltpu.VMEM((width // LANES, count, LANES), F32),
            pltpu.VMEM((count, width), F32),
            pltpu.VMEM((count, width), BF16),
            pltpu.VMEM((width, width), BF16),
            pltpu.SemaphoreType.DMA((3,)),
            pltpu.SemaphoreType.DMA((2,)),
        ],
        compiler_params=pltpu.CompilerParams(vmem_limit_bytes=FINISH_LIMIT),
        cost_estimate=pl.CostEstimate(
            flops=2 * count * width * width,
            bytes_accessed=2 * (width * width + 6 * count * width),
            transcendentals=0,
        ),
        name="finish",
    )(branch, window_mine, window_theirs, tokens, tokens_theirs, returned, blend, gate, w_out)


def shift(cells, axis, forward):
    count = lax.axis_size(axis)
    if forward:
        pairs = [(i, i + 1) for i in range(count - 1)]
    else:
        pairs = [(i + 1, i) for i in range(count - 1)]
    return lax.ppermute(cells, axis, pairs)


def halo_rows(tile, left, right):
    rows, cols, width = tile.shape
    square = HALO * HALO
    lower = [tile[rows - HALO :].reshape(HALO * cols, width), left[-square:], right[-square:]]
    upper = [tile[:HALO].reshape(HALO * cols, width), left[:square], right[:square]]
    above = shift(jnp.concatenate(lower, axis=0), "row", True)
    below = shift(jnp.concatenate(upper, axis=0), "row", False)
    return above, below


def on_device(tokens, modulation, wqkv, w_out, blend, reach):
    tile = tokens[0]
    rows, cols, width = tile.shape
    row_groups = lax.axis_size("row")
    col_groups = lax.axis_size("col")
    sub_rows = rows // row_groups
    sub_cols = cols // col_groups
    half = rows // 2 * cols
    branch = lax.axis_index("branch")
    wqkv, w_out = in_hbm(wqkv), in_hbm(w_out)
    devices = row_groups * col_groups
    row, col = lax.axis_index("row"), lax.axis_index("col")
    inner = [row > 0, row < row_groups - 1, col > 0, col < col_groups - 1]
    place_of = jnp.stack([branch] + [side.astype(branch.dtype) for side in inner]).astype(jnp.int32)

    def other_core(cells):
        return lax.ppermute(cells, "branch", [(0, 1), (1, 0)])

    outgoing, left_strip, right_strip = arrange(in_hbm(tile))
    left = shift(right_strip, "col", True)
    right = shift(left_strip, "col", False)
    arrived = lax.all_to_all(outgoing, ("row", "col"), split_axis=0, concat_axis=0, tiled=True)

    flat = tile.reshape(rows * cols, width)
    above, below = halo_rows(tile, left, right)
    *own, tokens_send, mark = own_tile(place_of, flat, modulation, wqkv)
    tokens_theirs = other_core(tokens_send)

    lattice_mine, lattice_send = lattice(place_of, arrived, modulation, wqkv, [mark])
    lattice_theirs = other_core(hold(lattice_send, [above, below]))
    combined = combine(place_of, lattice_mine, lattice_theirs)
    returned = lax.all_to_all(combined, ("row", "col"), split_axis=0, concat_axis=0, tiled=True)

    window_mine, send = window(
        place_of, reach.reshape(4), own, [above, below, left, right], modulation, wqkv, rows, cols, [combined]
    )
    window_theirs = other_core(send)
    weight = lax.dynamic_index_in_dim(blend.reshape(2, half, 1), branch, 0, keepdims=False)
    guided = finish(
        place_of,
        window_mine,
        window_theirs,
        in_hbm(flat),
        tokens_theirs,
        returned,
        weight,
        modulation[2:3],
        w_out,
        col_groups,
    )
    return guided.reshape(rows // 2, cols, width)


def solution(mesh):
    in_specs = (
        P("branch", "row", "col", None),
        P(),
        P(),
        P(),
        P("row", "col"),
        P(None, "row", "col"),
    )
    out_specs = P(("row", "branch"), "col", None)
    return jax.shard_map(
        on_device, mesh=mesh, in_specs=in_specs, out_specs=out_specs, check_vma=False
    )
```
